32 devices in a mesh: dp: 4 (over y, x), seq: 8 (over z, core).
Axes of the slice: x: 2, y: 2, z: 4, core: 2. Of those that a mesh axis runs over, the one named last changes fastest.
Arguments:
- tokens: bfloat16 [16, 1024, 768], P('dp', 'seq'), may hold values from -6 to 6
- cotangent: bfloat16 [16, 1024, 768], P('dp', 'seq'), may hold values from -6 to 6
- document_starts: int32 [16, 8], P('dp'), may hold values from 0 to 1023, as said below
- vectors: float32 [2, 11, 768], P(None, None, ('dp', 'seq')), may hold values from -17 to 2
- matrices: float32 [2, 4, 768, 768], P(None, None, ('dp', 'seq')), may hold values from -0.21875 to 0.21875
- time_output: float32 [2, 768, 768], P(None, ('dp', 'seq')), may hold values from -0.875 to 0.875
- feed_key: float32 [2, 768, 3072], P(None, ('dp', 'seq')), may hold values from -0.21875 to 0.21875
- feed_value: float32 [2, 3072, 768], P(None, ('dp', 'seq')), may hold values from -0.109375 to 0.109375
- mean_vectors: float32 [2, 11, 768], P(None, None, ('dp', 'seq')), may hold values from -128 to 128
- mean_matrices: float32 [2, 4, 768, 768], P(None, None, ('dp', 'seq')), may hold values from -128 to 128
- mean_output: float32 [2, 768, 768], P(None, ('dp', 'seq')), may hold values from -128 to 128
- mean_key: float32 [2, 768, 3072], P(None, ('dp', 'seq')), may hold values from -128 to 128
- mean_value: float32 [2, 3072, 768], P(None, ('dp', 'seq')), may hold values from -128 to 128
- power_vectors: float32 [2, 11, 768], P(None, None, ('dp', 'seq')), may hold values from 0 to 1638
- power_matrices: float32 [2, 4, 768, 768], P(None, None, ('dp', 'seq')), may hold values from 0 to 327
- power_output: float32 [2, 768, 768], P(None, ('dp', 'seq')), may hold values from 0 to 327
- power_key: float32 [2, 768, 3072], P(None, ('dp', 'seq')), may hold values from 0 to 327
- power_value: float32 [2, 3072, 768], P(None, ('dp', 'seq')), may hold values from 0 to 327
Outputs:
- block_out: bfloat16 [16, 1024, 768], P('dp', 'seq')
- grad_tokens: float32 [16, 1024, 768], P('dp', 'seq')
- grad_vectors: float32 [2, 11, 768], P(None, None, ('dp', 'seq'))
- grad_matrices: float32 [2, 4, 768, 768], P(None, None, ('dp', 'seq'))
- grad_output: float32 [2, 768, 768], P(None, ('dp', 'seq'))
- grad_key: float32 [2, 768, 3072], P(None, ('dp', 'seq'))
- grad_value: float32 [2, 3072, 768], P(None, ('dp', 'seq'))
- step_vectors: float32 [2, 11, 768], P(None, None, ('dp', 'seq'))
- step_matrices: float32 [2, 4, 768, 768], P(None, None, ('dp', 'seq'))
- step_output: float32 [2, 768, 768], P(None, ('dp', 'seq'))
- step_key: float32 [2, 768, 3072], P(None, ('dp', 'seq'))
- step_value: float32 [2, 3072, 768], P(None, ('dp', 'seq'))
- new_mean_vectors: float32 [2, 11, 768], P(None, None, ('dp', 'seq'))
- new_mean_matrices: float32 [2, 4, 768, 768], P(None, None, ('dp', 'seq'))
- new_mean_output: float32 [2, 768, 768], P(None, ('dp', 'seq'))
- new_mean_key: float32 [2, 768, 3072], P(None, ('dp', 'seq'))
- new_mean_value: float32 [2, 3072, 768], P(None, ('dp', 'seq'))
- new_power_vectors: float32 [2, 11, 768], P(None, None, ('dp', 'seq'))
- new_power_matrices: float32 [2, 4, 768, 768], P(None, None, ('dp', 'seq'))
- new_power_output: float32 [2, 768, 768], P(None, ('dp', 'seq'))
- new_power_key: float32 [2, 768, 3072], P(None, ('dp', 'seq'))
- new_power_value: float32 [2, 3072, 768], P(None, ('dp', 'seq'))
The draws below stay inside these ranges and needn't reach their ends.
Inputs may be any that keep to these rules, and one draw needn't show every extreme that they name: `document_starts`: each row's starts are strictly increasing and the first is 0. In each group of 4 rows on one index of dp, one row drawn from the seed has a document that begins within the first 128 positions and ends within the last 128, and that row's last document is its final position alone.
All inputs are finite; a program needn't handle non-finite values.
Results may differ from the reference program's by a relative error of at most 0.033.
Values may be sent and summed in bfloat16 or wider, within the bound.
No kernel may reach another device: no remote copies, remote signals or barrier semaphores. Data moves between devices by JAX's collectives and lax.ppermute only.
A program may use at most 256 MiB of HBM per device.

```python
import jax
import jax.numpy as jnp
from jax import lax

D = 768
FF = 3072
T_DEV = 128
MICRO = 4
LAYERS = 2
DOCS = 8
WBLK = 8
ROWS = 16
LENGTH = 1024


def draw_document_starts(key, part):
    key = jax.random.fold_in(key, 11)
    group_total = ROWS // MICRO
    picks = jax.random.randint(jax.random.fold_in(key, 1), (group_total,), 0, MICRO)
    spanning = jnp.arange(ROWS) % MICRO == jnp.repeat(picks, MICRO)
    early = (DOCS - 1) // 2
    late_count = DOCS - 1 - early

    def one_row(present_sequence_slot):
        row_key = jax.random.fold_in(key, present_sequence_slot + 100)
        spread = jnp.sort(jax.random.permutation(jax.random.fold_in(row_key, 0), LENGTH - 1)[:DOCS - 1] + 1)
        head_starts = jnp.sort(jax.random.permutation(jax.random.fold_in(row_key, 1), T_DEV - 1)[:early] + 1)
        tail_inner = jnp.sort(jax.random.permutation(jax.random.fold_in(row_key, 2), T_DEV - 2)[:late_count - 1] + LENGTH - T_DEV + 1)
        tail_last = jnp.full((1,), LENGTH - 1, dtype=tail_inner.dtype)
        return (spread, jnp.concatenate([head_starts, tail_inner, tail_last]))
    spread, bounded = jax.vmap(one_row)(jnp.arange(ROWS))
    rest = jnp.where(spanning[:, None], bounded, spread)
    return jnp.concatenate([jnp.zeros((ROWS, 1), jnp.int32), rest.astype(jnp.int32)], axis=1)


def draw_vectors(key, part):
    key = jax.random.fold_in(key, 7)
    shape = (LAYERS, 11, D)
    norm_magnitude = jax.random.uniform(jax.random.fold_in(key, 1), shape, jnp.float32)
    present_sequence_slot = jnp.arange(11)[None, :, None]
    scale_parameters = 0.85 + 0.3 * norm_magnitude
    offset_parameters = 0.6 * norm_magnitude - 0.3
    channel_quantities = 0.05 + 0.9 * norm_magnitude
    forgetting_multiplier = jnp.log(1e-06) + norm_magnitude * (jnp.log(0.1) - jnp.log(1e-06))
    present_extra_weight = 2.0 * norm_magnitude - 1.0
    scale_enabled = (present_sequence_slot == 0) | (present_sequence_slot == 7)
    shift_enabled = (present_sequence_slot == 1) | (present_sequence_slot == 8)
    layer_response = jnp.where(scale_enabled, scale_parameters, jnp.where(shift_enabled, offset_parameters, jnp.where(present_sequence_slot == 5, forgetting_multiplier, jnp.where(present_sequence_slot == 6, present_extra_weight, channel_quantities))))
    return layer_response.astype(jnp.float32)


def moment_pair(key, salt_number, array_shape, magnitude):
    pair_key = jax.random.fold_in(key, salt_number)
    position_draw = jax.random.uniform(jax.random.fold_in(pair_key, 1), array_shape, jnp.float32)
    spread_factor = jnp.exp(jnp.log(0.01) + position_draw * (jnp.log(3.0) - jnp.log(0.01)))
    squared = 0.01 * ROWS * LENGTH * magnitude * spread_factor
    signed_draw = jax.random.truncated_normal(jax.random.fold_in(pair_key, 2), -4.0, 4.0, array_shape, jnp.float32)
    leading = 0.7 * jnp.sqrt(squared) * signed_draw
    return (leading.astype(jnp.float32), squared.astype(jnp.float32))


def draw_mean_vectors(key, part):
    return moment_pair(key, 21, (LAYERS, 11, D), 2.0)[0]


def draw_power_vectors(key, part):
    return moment_pair(key, 21, (LAYERS, 11, D), 2.0)[1]


def draw_mean_matrices(key, part):
    return moment_pair(key, 22, (LAYERS, 4, D, D), 0.4)[0]


def draw_power_matrices(key, part):
    return moment_pair(key, 22, (LAYERS, 4, D, D), 0.4)[1]


def draw_mean_output(key, part):
    return moment_pair(key, 23, (LAYERS, D, D), 0.4)[0]


def draw_power_output(key, part):
    return moment_pair(key, 23, (LAYERS, D, D), 0.4)[1]


def draw_mean_key(key, part):
    return moment_pair(key, 24, (LAYERS, D, FF), 0.4)[0]


def draw_power_key(key, part):
    return moment_pair(key, 24, (LAYERS, D, FF), 0.4)[1]


def draw_mean_value(key, part):
    return moment_pair(key, 25, (LAYERS, FF, D), 0.4)[0]


def draw_power_value(key, part):
    return moment_pair(key, 25, (LAYERS, FF, D), 0.4)[1]


def block_levels(key, shape, shards, low, top_value):
    level = 1.0
    for dim, shards_of in shards:
        heights = jax.random.uniform(jax.random.fold_in(jax.random.fold_in(key, 6), dim), (shards_of,), jnp.float32, low / len(shards), top_value / len(shards))
        level = level * jnp.repeat(jnp.exp(heights), shape[dim] // shards_of).reshape((-1,) + (1,) * (len(shape) - 1 - dim))
    return level


def noise(stream_key, shape, scale, limit, pieces=(), kind=jnp.bfloat16):
    result = jax.random.normal(stream_key, shape, jnp.float32) * scale
    if len(pieces) > 0:
        result = block_levels(stream_key, shape, pieces, -0.22, 0.18) * result
    return jnp.clip(result, min=-limit, max=limit).astype(kind)


def setup_inputs(seed: int = 0) -> dict:
    splits = jax.random.split(jax.random.key(seed), 19)
    tokens = noise(splits[0], (ROWS, LENGTH, D), 1.0, 6.0, ((0, 4), (1, 8)))
    cotangent = noise(splits[1], (ROWS, LENGTH, D), 1.0, 6.0, ((0, 4), (1, 8)))
    document_starts = draw_document_starts(jax.random.fold_in(splits[18], 71), 0)
    vectors = draw_vectors(jax.random.fold_in(splits[18], 71), 0)
    matrices = noise(splits[4], (LAYERS, 4, D, D), D ** -0.5, 0.21875, ((2, 32),), jnp.float32)
    time_output = noise(splits[5], (LAYERS, D, D), (D // 16) ** -0.5, 0.875, ((1, 32),), jnp.float32)
    feed_key = noise(splits[6], (LAYERS, D, FF), D ** -0.5, 0.21875, ((1, 32),), jnp.float32)
    feed_value = noise(splits[7], (LAYERS, FF, D), FF ** -0.5, 0.109375, ((1, 32),), jnp.float32)
    mean_vectors = draw_mean_vectors(jax.random.fold_in(splits[18], 71), 0)
    mean_matrices = draw_mean_matrices(jax.random.fold_in(splits[18], 71), 0)
    mean_output = draw_mean_output(jax.random.fold_in(splits[18], 71), 0)
    mean_key = draw_mean_key(jax.random.fold_in(splits[18], 71), 0)
    mean_value = draw_mean_value(jax.random.fold_in(splits[18], 71), 0)
    power_vectors = draw_power_vectors(jax.random.fold_in(splits[18], 71), 0)
    power_matrices = draw_power_matrices(jax.random.fold_in(splits[18], 71), 0)
    power_output = draw_power_output(jax.random.fold_in(splits[18], 71), 0)
    power_key = draw_power_key(jax.random.fold_in(splits[18], 71), 0)
    power_value = draw_power_value(jax.random.fold_in(splits[18], 71), 0)
    return {"tokens": tokens, "cotangent": cotangent, "document_starts": document_starts, "vectors": vectors, "matrices": matrices, "time_output": time_output, "feed_key": feed_key, "feed_value": feed_value, "mean_vectors": mean_vectors, "mean_matrices": mean_matrices, "mean_output": mean_output, "mean_key": mean_key, "mean_value": mean_value, "power_vectors": power_vectors, "power_matrices": power_matrices, "power_output": power_output, "power_key": power_key, "power_value": power_value}


norm_epsilon = 1e-05
beta_one = 0.9
beta_two = 0.99
adam_epsilon = 1e-08
step_count = 10
rate_main = 0.0006
rate_time = 0.0012
weight_decay = 0.1

@jax.custom_vjp
def low(v):
    return lax.optimization_barrier(v.astype(jnp.bfloat16)).astype(jnp.float32)

@jax.custom_vjp
def low_back(v):
    return v

def low_keep(v):
    return (low(v), None)

def low_pass(kept, grad):
    return (grad,)

def back_keep(v):
    return (v, None)

def back_low(kept, grad):
    return (low(grad),)
low.defvjp(low_keep, low_pass)
low_back.defvjp(back_keep, back_low)

def layer_norm(values_in, gain, bias):
    centre = lax.optimization_barrier(jnp.mean(values_in, axis=-1, keepdims=True))
    centred = values_in - centre
    spread = lax.optimization_barrier(jnp.mean(centred * centred, axis=-1, keepdims=True))
    return centred * lax.rsqrt(spread + norm_epsilon) * gain + bias

def decay_block(carry_state, block_item, decay_rate):
    running_state_numerator, running_state_denominator, state_document = carry_state
    lookup_projection_lines, value_matrix_rows, document_index = block_item
    block_length = lookup_projection_lines.shape[1]
    offsets = jnp.arange(block_length)
    lag_steps = offsets[:, None] - offsets[None, :] - 1
    earlier = lag_steps >= 0
    lag_decay = jnp.exp(-jnp.maximum(lag_steps, 0).astype(jnp.float32)[:, :, None] * decay_rate)
    same_document = (document_index[:, :, None] == document_index[:, None, :]) & earlier[None]
    coefficient = jnp.where(same_document[..., None], lag_decay[None], 0.0)
    exp_keys = jnp.exp(lookup_projection_lines)
    weighted = exp_keys * value_matrix_rows
    numerator = lax.optimization_barrier(jnp.sum(coefficient * weighted[:, None], axis=2))
    denominator = lax.optimization_barrier(jnp.sum(coefficient * exp_keys[:, None], axis=2))
    recurrent_memory = (document_index == state_document[:, None]).astype(jnp.float32)[:, :, None] * jnp.exp(-offsets.astype(jnp.float32)[:, None] * decay_rate)[None]
    numerator = numerator + recurrent_memory * running_state_numerator[:, None]
    denominator = denominator + recurrent_memory * running_state_denominator[:, None]
    last_document = document_index[:, -1].astype(jnp.int32)
    tail_weight = (document_index == last_document[:, None]).astype(jnp.float32)[:, :, None] * jnp.exp(-(block_length - 1 - offsets).astype(jnp.float32)[:, None] * decay_rate)[None]
    keep_factor = (state_document == last_document).astype(jnp.float32)[:, None] * jnp.exp(-block_length * decay_rate)[None]
    new_numerator = keep_factor * running_state_numerator + lax.optimization_barrier(jnp.sum(tail_weight * weighted, axis=1))
    new_denominator = keep_factor * running_state_denominator + lax.optimization_barrier(jnp.sum(tail_weight * exp_keys, axis=1))
    return ((new_numerator, new_denominator, last_document), (numerator, denominator))

def decay_sums(lookup_projection_lines, value_matrix_rows, document_index, decay_rate, document_start_flag, running_state_numerator, running_state_denominator):
    row_count, token_count, model_width = lookup_projection_lines.shape
    block_count = token_count // WBLK

    def to_blocks(array):
        return jnp.swapaxes(array.reshape((row_count, block_count, WBLK) + array.shape[2:]), 0, 1)

    def from_blocks(array):
        return jnp.swapaxes(array, 0, 1).reshape(row_count, token_count, model_width)
    block_step = jax.checkpoint(decay_block)
    final_state, (numerator, denominator) = lax.scan(lambda carry_state, block_item: block_step(carry_state, block_item, decay_rate), (running_state_numerator, running_state_denominator, document_start_flag.astype(jnp.int32)), (to_blocks(lookup_projection_lines), to_blocks(value_matrix_rows), to_blocks(document_index.astype(jnp.int32))))
    return (final_state, from_blocks(numerator), from_blocks(denominator))

def product(left, weight):
    return jnp.einsum('rtd,de->rte', left, weight, precision=lax.Precision.HIGHEST)

def shift_tokens(normalized, document_index, document_start_flag, edge_token):
    previous = jnp.concatenate([edge_token[:, None], normalized[:, :-1]], axis=1)
    before = jnp.concatenate([document_start_flag[:, None], document_index[:, :-1]], axis=1)
    return previous * (document_index == before).astype(jnp.float32)[:, :, None]

def mix_in(normalized, previous, amount):
    return normalized * amount + previous * (1.0 - amount)

def block_forward(layer_input, document_index, weights):
    vectors, matrices, time_output, feed_key, feed_value = weights
    row_count = layer_input.shape[0]
    document_start_flag = jnp.zeros((row_count,), jnp.int32)
    edge_token = jnp.zeros((row_count, layer_input.shape[2]), jnp.float32)
    normalized = layer_norm(layer_input, vectors[0], vectors[1])
    previous = shift_tokens(normalized, document_index, document_start_flag, edge_token)
    lookup_projection_lines = low_back(product(low(mix_in(normalized, previous, vectors[2])), matrices[0]))
    value_matrix_rows = low_back(product(low(mix_in(normalized, previous, vectors[3])), matrices[1]))
    receptance = low_back(product(low(mix_in(normalized, previous, vectors[4])), matrices[2]))
    decay_rate = jnp.exp(vectors[5])
    final_state, numerator, denominator = decay_sums(lookup_projection_lines, value_matrix_rows, document_index, decay_rate, document_start_flag, edge_token, edge_token)
    initial_extra_weight = jnp.exp(vectors[6] + lookup_projection_lines)
    weighted_mean = (numerator + initial_extra_weight * value_matrix_rows) / (denominator + initial_extra_weight)
    gated_mean = low(jax.nn.sigmoid(receptance) * weighted_mean)
    middle = layer_input + low_back(product(gated_mean, time_output))
    normalized_two = layer_norm(middle, vectors[7], vectors[8])
    previous_two = shift_tokens(normalized_two, document_index, document_start_flag, edge_token)
    hidden_input = low_back(product(low(mix_in(normalized_two, previous_two, vectors[9])), feed_key))
    hidden = low(jnp.square(jax.nn.softplus(hidden_input)))
    value_branch = low_back(product(hidden, feed_value))
    gate_logit = low_back(product(low(mix_in(normalized_two, previous_two, vectors[10])), matrices[3]))
    return middle + jax.nn.sigmoid(gate_logit) * value_branch

def vector_rates(row_total):
    present_sequence_slot = jnp.arange(row_total)
    special = (present_sequence_slot == 5) | (present_sequence_slot == 6)
    return jnp.where(special, rate_time, rate_main)[:, None]

def adam_step(parameter, gradient, first_moment, second_moment, learning_rates, decay_weight):
    new_first = beta_one * first_moment + (1.0 - beta_one) * gradient
    new_second = beta_two * second_moment + (1.0 - beta_two) * gradient * gradient
    step_ratio = new_first / (1.0 - beta_one ** step_count) / (jnp.sqrt(new_second / (1.0 - beta_two ** step_count)) + adam_epsilon)
    return (learning_rates * (step_ratio + decay_weight * parameter), new_first, new_second)

def reference(tokens, cotangent, document_starts, vectors, matrices, time_output, feed_key, feed_value, mean_vectors, mean_matrices, mean_output, mean_key, mean_value, power_vectors, power_matrices, power_output, power_key, power_value):
    params = (vectors, matrices, time_output, feed_key, feed_value)
    positions = jnp.arange(LENGTH).astype(jnp.int32)

    def forward(layer_input, document_index, weights):
        lowered = tuple((low(weight) for weight in weights))
        for layer_index in range(LAYERS):
            layer_input = block_forward(layer_input, document_index, tuple((weight[layer_index] for weight in lowered)))
        return layer_input

    def row_step(totals, row_item):
        row_tokens, row_cotangent, row_starts = row_item
        document_index = lax.optimization_barrier(jnp.sum((row_starts[:, None] <= positions[None, :]).astype(jnp.int32), axis=0)).astype(jnp.int32)[None]
        layer_response, pullback = jax.vjp(lambda row_input, weights: forward(row_input, document_index, weights), row_tokens[None].astype(jnp.float32), params)
        grad_input, grad_weights = pullback(row_cotangent[None].astype(jnp.float32))
        totals = tuple((total_now + grad_now for total_now, grad_now in zip(totals, grad_weights)))
        return (totals, (layer_response[0].astype(jnp.bfloat16), grad_input[0]))
    zero_grads = tuple((jnp.zeros_like(weight) for weight in params))
    grads, (block_out, grad_tokens) = lax.scan(row_step, zero_grads, (tokens, cotangent, document_starts))
    vector_new = adam_step(vectors, grads[0], mean_vectors, power_vectors, vector_rates(vectors.shape[1]), 0.0)
    matrix_new = adam_step(matrices, grads[1], mean_matrices, power_matrices, rate_main, weight_decay)
    output_new = adam_step(time_output, grads[2], mean_output, power_output, rate_main, weight_decay)
    key_new = adam_step(feed_key, grads[3], mean_key, power_key, rate_main, weight_decay)
    value_new = adam_step(feed_value, grads[4], mean_value, power_value, rate_main, weight_decay)
    return (block_out, grad_tokens, grads[0], grads[1], grads[2], grads[3], grads[4], vector_new[0], matrix_new[0], output_new[0], key_new[0], value_new[0], vector_new[1], matrix_new[1], output_new[1], key_new[1], value_new[1], vector_new[2], matrix_new[2], output_new[2], key_new[2], value_new[2])
```

```python
import jax
import jax.numpy as jnp
from jax import lax
from jax.experimental import pallas as pl
from jax.experimental.pallas import tpu as pltpu
from jax.sharding import PartitionSpec as P

norm_epsilon = 1e-05
beta_one = 0.9
beta_two = 0.99
adam_epsilon = 1e-08
step_count = 10
rate_main = 0.0006
rate_time = 0.0012
weight_decay = 0.1

RB = 2
VMEM = 48 * 1024 * 1024
F32, BF16 = jnp.float32, jnp.bfloat16


def wide(mask, width):
    return jnp.concatenate([mask] * (width // 128), axis=1)


def dot_nn(a, b):
    return lax.dot_general(a, b, (((1,), (0,)), ((), ())), preferred_element_type=F32)


def dot_nt(a, b):
    return lax.dot_general(a, b, (((1,), (1,)), ((), ())), preferred_element_type=F32)


def colsum(a):
    return jnp.sum(a, axis=0, keepdims=True)


def places(starts_ref, base_ref, first_row, rows, T):
    at = lax.broadcasted_iota(jnp.int32, (T, 128), 0)
    base = base_ref[0]
    local, dist, tail = [], [], []
    for q in range(rows):
        begin = jnp.zeros((T, 128), jnp.int32)
        last_begin = jnp.int32(0)
        for j in range(starts_ref.shape[1]):
            s = starts_ref[first_row + q, j]
            begin = jnp.where(at + base >= s, jnp.maximum(begin, s), begin)
            last_begin = jnp.where(base + T - 1 >= s, jnp.maximum(last_begin, s), last_begin)
        local.append(at)
        dist.append(at + base - begin)
        tail.append((at + base >= last_begin).astype(F32))
    return tuple(jnp.concatenate(z, axis=0) for z in (local, dist, tail))


def norm_parts(x):
    centred = x - jnp.mean(x, axis=-1, keepdims=True)
    rstd = lax.rsqrt(jnp.mean(centred * centred, axis=-1, keepdims=True) + norm_epsilon)
    return centred * rstd, rstd


def shifted(normalized, edge, local, joined, T):
    M, D = normalized.shape
    rolled = pltpu.roll(normalized, 1, 0)
    edges = jnp.concatenate(
        [jnp.broadcast_to(edge[q : q + 1], (T, D)) for q in range(M // T)], axis=0
    )
    return jnp.where(wide(local, D) == 0, edges, rolled) * wide(joined, D)


def shift_up(masked, local, T):
    M, D = masked.shape
    rolled = pltpu.roll(masked, M - 1, 0)
    return jnp.where(wide(local, D) == T - 1, 0.0, rolled)


def row_firsts(a, T):
    return jnp.concatenate([a[q * T : q * T + 1] for q in range(a.shape[0] // T)], axis=0)


def row_lasts(a, T):
    return jnp.concatenate(
        [a[q * T + T - 1 : q * T + T] for q in range(a.shape[0] // T)], axis=0
    )


def levels(T):
    k = 1
    while k < T:
        yield k
        k *= 2


def scan_down(pair, rate, local, dist, T):
    M, D = pair[0].shape
    for k in levels(T):
        keep = ((dist >= k) & (local >= k)).astype(F32)
        weight = wide(keep, D) * jnp.exp(-float(k) * rate)
        pair = tuple(a + weight * pltpu.roll(a, k, 0) for a in pair)
    return pair


def scan_up(pair, rate, local, dist, T):
    M, D = pair[0].shape
    for k in levels(T):
        keep = ((dist >= k) & (local >= k)).astype(F32)
        weight = wide(keep, D) * jnp.exp(-float(k) * rate)
        pair = tuple(a + pltpu.roll(weight * a, M - k, 0) for a in pair)
    return pair


def per_row(values, T, D):
    return jnp.concatenate(
        [jnp.broadcast_to(values[q : q + 1], (T, D)) for q in range(values.shape[0])], axis=0
    )


def k_time_in(T, starts, base, x, edge, vec, wk, wv, wr,
              mk, mv, mr, ko, vo, ro, no, do, last):
    D = x.shape[1]
    i = pl.program_id(0)
    local, dist, _ = places(starts, base, i * RB, RB, T)
    joined = (dist >= 1).astype(F32)
    gain, bias = vec[0:1], vec[1:2]
    normalized = norm_parts(x[...].astype(F32))[0] * gain + bias
    edge_norm = norm_parts(edge[0])[0] * gain + bias
    previous = shifted(normalized, edge_norm, local, joined, T)
    for j, out in ((2, mk), (3, mv), (4, mr)):
        mu = vec[j : j + 1]
        out[...] = (normalized * mu + previous * (1.0 - mu)).astype(BF16)
    key = dot_nn(mk[...], wk[...])
    value = dot_nn(mv[...], wv[...])
    ko[...] = key
    vo[...] = value
    ro[...] = dot_nn(mr[...], wr[...]).astype(ro.dtype)
    rate = jnp.exp(vec[5:6])
    weight = jnp.exp(key)
    num, den = scan_down((weight * value, weight), rate, local, dist, T)
    keep = wide(((dist >= 1) & (local >= 1)).astype(F32), D)
    no[...] = keep * pltpu.roll(num, 1, 0)
    do[...] = keep * pltpu.roll(den, 1, 0)
    ends = (row_lasts(num, T), row_lasts(den, T))
    for q in range(RB):
        last[q] = jnp.concatenate([ends[0][q : q + 1], ends[1][q : q + 1]], axis=0)


def decay_state(vec, key, value, num, den, state, local, dist, T):
    D = key.shape[1]
    rate = jnp.exp(vec[5:6])
    fade = wide((dist >= local + 1).astype(F32), D) * jnp.exp(
        -wide(local.astype(F32), D) * rate
    )
    full_n = num + fade * per_row(state[:, 0], T, D)
    full_d = den + fade * per_row(state[:, 1], T, D)
    extra = jnp.exp(vec[6:7] + key)
    inverse = 1.0 / (full_d + extra)
    mean = (full_n + extra * value) * inverse
    return full_n, full_d, extra, inverse, mean


def k_time_out(T, starts, base, x, key, value, recept, num, den, state, vec, wo,
               gated, middle):
    i = pl.program_id(0)
    local, dist, _ = places(starts, base, i * RB, RB, T)
    mean = decay_state(
        vec, key[...], value[...], num[...], den[...], state[...], local, dist, T
    )[4]
    gated[...] = (jax.nn.sigmoid(recept[...].astype(F32)) * mean).astype(BF16)
    middle[...] = x[...].astype(F32) + dot_nn(gated[...], wo[...])


def k_feed(T, starts, base, middle, edge, vec, wg, wk, wv,
           fm, gm, sp, hid, vb, gl, xo, acc):
    M, D = middle.shape
    j = pl.program_id(0)

    @pl.when(j == 0)
    def _():
        local, dist, _ = places(starts, base, 0, M // T, T)
        gain, bias = vec[7:8], vec[8:9]
        normalized = norm_parts(middle[...])[0] * gain + bias
        edge_norm = norm_parts(edge[...])[0] * gain + bias
        previous = shifted(normalized, edge_norm, local, (dist >= 1).astype(F32), T)
        for row, out in ((9, fm), (10, gm)):
            mu = vec[row : row + 1]
            out[...] = (normalized * mu + previous * (1.0 - mu)).astype(BF16)
        acc[...] = jnp.zeros_like(acc)

    pre = dot_nn(fm[...], wk[...])
    soft = jnp.maximum(pre, 0.0) + jnp.log1p(jnp.exp(-jnp.abs(pre)))
    sp[...] = soft.astype(BF16)
    hidden = (soft * soft).astype(BF16)
    hid[...] = hidden
    acc[...] += dot_nn(hidden, wv[...])

    @pl.when(j == pl.num_programs(0) - 1)
    def _():
        gate = dot_nn(gm[...], wg[...])
        gl[...] = gate.astype(BF16)
        vb[...] = acc[...].astype(BF16)
        xo[...] = middle[...] + jax.nn.sigmoid(gate) * acc[...]


def k_feed_back(T, starts, base, grad, gl, vb, sp, middle, edge, vec, wg, wk, wv,
                gb, gg, gin, gn, first, sums, acc):
    M, D = middle.shape
    j = pl.program_id(0)

    @pl.when(j == 0)
    def _():
        g = grad[...].astype(F32)
        s = jax.nn.sigmoid(gl[...].astype(F32))
        gb[...] = (g * s).astype(BF16)
        gg[...] = (g * vb[...].astype(F32) * s * (1.0 - s)).astype(BF16)
        acc[...] = jnp.zeros_like(acc)

    soft = sp[...].astype(F32)
    gh = dot_nt(gb[...], wv[...])
    pre = (gh * (2.0 * soft * (1.0 - jnp.exp(-soft)))).astype(BF16)
    gin[...] = pre
    acc[...] += dot_nt(pre, wk[...])

    @pl.when(j == pl.num_programs(0) - 1)
    def _():
        local, dist, _ = places(starts, base, 0, M // T, T)
        joined = (dist >= 1).astype(F32)
        gain, bias = vec[7:8], vec[8:9]
        normalized = norm_parts(middle[...])[0] * gain + bias
        edge_norm = norm_parts(edge[...])[0] * gain + bias
        difference = normalized - shifted(normalized, edge_norm, local, joined, T)
        ga = acc[...]
        gc = dot_nt(gg[...], wg[...])
        sums[0:1] = colsum(ga * difference)
        sums[1:2] = colsum(gc * difference)
        sums[2:8] = jnp.zeros((6, D), F32)
        mu_a, mu_c = vec[9:10], vec[10:11]
        masked = (ga * (1.0 - mu_a) + gc * (1.0 - mu_c)) * wide(joined, D)
        gn[...] = ga * mu_a + gc * mu_c + shift_up(masked, local, T)
        first[...] = row_firsts(masked, T)


def norm_back(x, gain, gn):
    hat, rstd = norm_parts(x)
    scaled = gn * gain
    gx = rstd * (
        scaled
        - jnp.mean(scaled, axis=-1, keepdims=True)
        - hat * jnp.mean(scaled * hat, axis=-1, keepdims=True)
    )
    return gx, colsum(gn * hat), colsum(gn)


def with_edge(gn, edge, local, T):
    D = gn.shape[1]
    return gn + jnp.where(wide(local, D) == T - 1, per_row(edge, T, D), 0.0)


def k_mid_back(T, starts, base, gn, edge, middle, grad, vec, wo,
               key, value, recept, num, den, state,
               gm, gblk, gr, gkp, gvp, gno, gdo, direct, sums):
    D = middle.shape[1]
    i = pl.program_id(0)
    local, dist, _ = places(starts, base, i * RB, RB, T)
    total = with_edge(gn[...], edge[0], local, T)
    gx, ggain, gbias = norm_back(middle[...], vec[7:8], total)
    gmid = grad[...].astype(F32) + gx
    gm[...] = gmid
    gblk[...] = gmid.astype(BF16)
    ggated = dot_nt(gblk[...], wo[...])
    v = value[...]
    _, _, extra, inverse, mean = decay_state(
        vec, key[...], v, num[...], den[...], state[...], local, dist, T
    )
    s = jax.nn.sigmoid(recept[...].astype(F32))
    gr[...] = (ggated * mean * s * (1.0 - s)).astype(BF16)
    q = ggated * s * inverse
    ge = extra * q * (v - mean)
    gkp[...] = ge
    gvp[...] = q * extra
    rate = jnp.exp(vec[5:6])
    an, ad = scan_up((q, -q * mean), rate, local, dist, T)
    keep = wide(((dist >= 1) & (local >= 1)).astype(F32), D)
    gno[...] = pltpu.roll(keep * an, an.shape[0] - 1, 0)
    gdo[...] = pltpu.roll(keep * ad, ad.shape[0] - 1, 0)
    joined = wide((dist >= 1).astype(F32), D)
    ends = (row_firsts(joined * an, T), row_firsts(joined * ad, T))
    for r in range(RB):
        direct[r] = jnp.concatenate([ends[0][r : r + 1], ends[1][r : r + 1]], axis=0)

    @pl.when(i == 0)
    def _():
        sums[...] = jnp.zeros_like(sums)

    sums[0:1] += ggain
    sums[1:2] += gbias
    sums[2:3] += colsum(ge)


def k_time_back(T, starts, base, x, edge, vec, wk, wv, wr, key, value, num, den, state,
                gkp, gvp, gno, gdo, after, gr,
                gk, gv, gn, first, sums):
    D = x.shape[1]
    i = pl.program_id(0)
    local, dist, tail = places(starts, base, i * RB, RB, T)
    rate = jnp.exp(vec[5:6])
    fade = wide((dist >= local + 1).astype(F32), D) * jnp.exp(
        -wide(local.astype(F32), D) * rate
    )
    st = state[...]
    full_n = num[...] + fade * per_row(st[:, 0], T, D)
    full_d = den[...] + fade * per_row(st[:, 1], T, D)
    left = wide(tail, D) * jnp.exp(-wide((T - 1 - local).astype(F32), D) * rate)
    af = after[...]
    grad_n = gno[...] + left * per_row(af[:, 0], T, D)
    grad_d = gdo[...] + left * per_row(af[:, 1], T, D)
    weight = jnp.exp(key[...])
    gk[...] = (gkp[...] + weight * (grad_n * value[...] + grad_d)).astype(BF16)
    gv[...] = (gvp[...] + weight * grad_n).astype(BF16)
    joined = (dist >= 1).astype(F32)
    gain, bias = vec[0:1], vec[1:2]
    normalized = norm_parts(x[...].astype(F32))[0] * gain + bias
    edge_norm = norm_parts(edge[0])[0] * gain + bias
    difference = normalized - shifted(normalized, edge_norm, local, joined, T)

    @pl.when(i == 0)
    def _():
        sums[...] = jnp.zeros_like(sums)

    sums[3:4] += -rate * jnp.exp(-rate) * colsum(grad_n * full_n + grad_d * full_d)
    grad_norm = jnp.zeros(x.shape, F32)
    grad_prev = jnp.zeros(x.shape, F32)
    for row, (g, w) in enumerate(((gk, wk), (gv, wv), (gr, wr))):
        mu = vec[2 + row : 3 + row]
        g_mix = dot_nt(g[...], w[...])
        sums[row : row + 1] += colsum(g_mix * difference)
        grad_norm = grad_norm + g_mix * mu
        grad_prev = grad_prev + g_mix * (1.0 - mu)
    masked = grad_prev * wide(joined, D)
    gn[...] = grad_norm + shift_up(masked, local, T)
    first[0] = row_firsts(masked, T)


def k_norm_back(T, x, gn, edge, gmid, vec, go, sums):
    i = pl.program_id(0)
    M = x.shape[0]
    at = lax.broadcasted_iota(jnp.int32, (T, 128), 0)
    local = jnp.concatenate([at] * (M // T), axis=0)
    total = with_edge(gn[...], edge[0], local, T)
    gx, ggain, gbias = norm_back(x[...].astype(F32), vec[0:1], total)
    go[...] = gmid[...] + gx

    @pl.when(i == 0)
    def _():
        sums[...] = jnp.zeros_like(sums)

    sums[0:1] += ggain
    sums[1:2] += gbias


def smem():
    return pl.BlockSpec(memory_space=pltpu.SMEM)


def rows_spec(T, D):
    return pl.BlockSpec((RB * T, D), lambda i: (i, 0))


def col_spec(rows, width, at):
    return pl.BlockSpec((rows, width), lambda i: (0, at))


def whole_spec(shape):
    zeros = (0,) * len(shape)
    return pl.BlockSpec(shape, lambda i: zeros)


def edge_spec(D):
    return pl.BlockSpec((1, RB, D), lambda i: (i, 0, 0))


def state_spec(D):
    return pl.BlockSpec((RB, 2, D), lambda i: (i, 0, 0))


def shape(dims, kind):
    return jax.ShapeDtypeStruct(dims, kind)


def run(kernel, T, grid, in_specs, out_specs, outs, args, flops, moved, scratch=()):
    def body(*refs):
        kernel(T, *refs)

    return pl.pallas_call(
        body,
        grid=(grid,),
        in_specs=in_specs,
        out_specs=out_specs,
        out_shape=outs,
        scratch_shapes=scratch,
        compiler_params=pltpu.CompilerParams(
            dimension_semantics=("arbitrary",), vmem_limit_bytes=VMEM
        ),
        cost_estimate=pl.CostEstimate(flops=flops, bytes_accessed=moved, transcendentals=0),
        name=kernel.__name__,
    )(*args)


def time_in(T, place, x, edge, vec, mats):
    N, D = x.shape
    R = N // T
    rs = rows_spec(T, D)
    return run(
        k_time_in, T, R // RB,
        [smem(), smem(), rs, edge_spec(D), whole_spec(vec.shape)]
        + [col_spec(D, D, c) for c in range(3)],
        [rs] * 8 + [state_spec(D)],
        [shape((N, D), BF16)] * 3 + [shape((N, D), F32)] * 2 + [shape((N, D), BF16)]
        + [shape((N, D), F32)] * 2 + [shape((R, 2, D), F32)],
        (*place, x, edge.reshape(R // RB, RB, D), vec, mats, mats, mats),
        6 * N * D * D, 40 * N * D,
    )


def time_out(T, place, x, kept, state, vec, mats):
    N, D = x.shape
    R = N // T
    rs = rows_spec(T, D)
    return run(
        k_time_out, T, R // RB,
        [smem(), smem()] + [rs] * 6 + [state_spec(D), whole_spec(vec.shape), col_spec(D, D, 4)],
        [rs] * 2,
        [shape((N, D), BF16), shape((N, D), F32)],
        (*place, x, *kept, state, vec, mats),
        2 * N * D * D, 30 * N * D,
    )


def feed(T, place, middle, edge, vec, mats, fk, fv):
    N, D = middle.shape
    F = fk.shape[1]
    B = D
    whole = whole_spec((N, D))
    wide_spec = pl.BlockSpec((N, B), lambda j: (0, j))
    return run(
        k_feed, T, F // B,
        [smem(), smem(), whole, whole_spec(edge.shape), whole_spec(vec.shape), col_spec(D, D, 3),
         pl.BlockSpec((D, B), lambda j: (0, j)), pl.BlockSpec((B, D), lambda j: (j, 0))],
        [whole, whole, wide_spec, wide_spec, whole, whole, whole],
        [shape((N, D), BF16)] * 2 + [shape((N, F), BF16)] * 2 + [shape((N, D), BF16)] * 2
        + [shape((N, D), F32)],
        (*place, middle, edge, vec, mats, fk, fv),
        4 * N * D * F + 2 * N * D * D, 20 * N * D + 4 * N * F + 4 * D * F,
        [pltpu.VMEM((N, D), F32)],
    )


def feed_back(T, place, grad, gl, vb, sp, middle, edge, vec, mats, fk, fv):
    N, D = middle.shape
    F = fk.shape[1]
    B = D
    R = N // T
    whole = whole_spec((N, D))
    wide_spec = pl.BlockSpec((N, B), lambda j: (0, j))
    return run(
        k_feed_back, T, F // B,
        [smem(), smem(), whole, whole, whole, wide_spec, whole, whole_spec(edge.shape),
         whole_spec(vec.shape), col_spec(D, D, 3),
         pl.BlockSpec((D, B), lambda j: (0, j)), pl.BlockSpec((B, D), lambda j: (j, 0))],
        [whole, whole, wide_spec, whole, whole_spec((R, D)), whole_spec((8, D))],
        [shape((N, D), BF16)] * 2 + [shape((N, F), BF16), shape((N, D), F32)]
        + [shape((R, D), F32), shape((8, D), F32)],
        (*place, grad, gl, vb, sp, middle, edge, vec, mats, fk, fv),
        4 * N * D * F + 2 * N * D * D, 20 * N * D + 4 * N * F + 4 * D * F,
        [pltpu.VMEM((N, D), F32)],
    )


def mid_back(T, place, gn, edge, middle, grad, vec, mats, kept, state):
    N, D = middle.shape
    R = N // T
    rs = rows_spec(T, D)
    return run(
        k_mid_back, T, R // RB,
        [smem(), smem(), rs, edge_spec(D), rs, rs, whole_spec(vec.shape), col_spec(D, D, 4)]
        + [rs] * 5 + [state_spec(D)],
        [rs] * 7 + [state_spec(D), whole_spec((8, D))],
        [shape((N, D), F32)] + [shape((N, D), BF16)] * 2 + [shape((N, D), F32)] * 4
        + [shape((R, 2, D), F32), shape((8, D), F32)],
        (*place, gn, edge.reshape(R // RB, RB, D), middle, grad, vec, mats, *kept, state),
        2 * N * D * D, 50 * N * D,
    )


def time_back(T, place, x, edge, vec, mats, kept, state, part, after, gr):
    N, D = x.shape
    R = N // T
    rs = rows_spec(T, D)
    key, value, num, den = kept
    return run(
        k_time_back, T, R // RB,
        [smem(), smem(), rs, edge_spec(D), whole_spec(vec.shape)]
        + [col_spec(D, D, c) for c in range(3)] + [rs] * 4 + [state_spec(D)] + [rs] * 4
        + [state_spec(D), rs],
        [rs] * 3 + [edge_spec(D), whole_spec((8, D))],
        [shape((N, D), BF16)] * 2 + [shape((N, D), F32)]
        + [shape((R // RB, RB, D), F32), shape((8, D), F32)],
        (*place, x, edge.reshape(R // RB, RB, D), vec, mats, mats, mats, key, value, num, den,
         state, *part, after, gr),
        6 * N * D * D, 50 * N * D,
    )


def norm_in_back(T, x, gn, edge, gmid, vec):
    N, D = x.shape
    R = N // T
    rs = rows_spec(T, D)
    return run(
        k_norm_back, T, R // RB,
        [rs, rs, edge_spec(D), rs, whole_spec(vec.shape)],
        [rs, whole_spec((8, D))],
        [shape((N, D), F32), shape((8, D), F32)],
        (x, gn, edge.reshape(R // RB, RB, D), gmid, vec),
        0, 16 * N * D,
    )


def from_behind(block, distance):
    devices = range(lax.axis_size("seq"))
    route = [(i - distance, i) for i in devices if i - distance in devices]
    return lax.ppermute(block, "seq", route)


def chain(mine, starts, rate, T, forward):
    S, i = lax.axis_size("seq"), lax.axis_index("seq")
    all_states = lax.all_gather(mine.astype(BF16), "seq").astype(F32)
    j = jnp.arange(S, dtype=jnp.int32)

    def document(at):
        return jnp.sum((starts[None] <= at[:, None, None]).astype(jnp.int32), axis=2)

    if forward:
        lag = i - 1 - j
        same = document((j + 1) * T - 1) == document((i * T - 1)[None])
    else:
        lag = j - 1 - i
        same = document(j * T - 1) == document(((i + 1) * T - 1)[None])
    keep = (same & (lag >= 0)[:, None]).astype(F32)
    fade = jnp.exp(-(T * jnp.maximum(lag, 0)).astype(F32)[:, None] * rate[None])
    weight = keep[:, :, None, None] * fade[:, None, None, :]
    return jnp.sum(weight * all_states, axis=0)


def layer_forward(T, place, starts, x, edge, vec, weights):
    mats, fk, fv = weights
    N, D = x.shape
    R = N // T
    rate = jnp.exp(vec[5])
    mk, mv, mr, key, value, recept, num, den, last = time_in(T, place, x, edge, vec, mats)
    state = chain(last, starts, rate, T, True)
    gated, middle = time_out(T, place, x, (key, value, recept, num, den), state, vec, mats)
    edge_two = from_behind(middle.reshape(R, T, D)[:, -1], 1)
    fm, gm, sp, hid, vb, gl, out = feed(T, place, middle, edge_two, vec, mats, fk, fv)
    saved = (x, edge, mk, mv, mr, key, value, recept, num, den, state, gated, middle, edge_two,
             fm, gm, sp, hid, vb, gl)
    return out, saved


def weight_grad(left, gradient):
    return lax.dot_general(
        left, gradient, (((0,), (0,)), ((), ())), preferred_element_type=F32
    ).astype(BF16)


def layer_backward(T, place, starts, grad, saved, vec, weights):
    mats, fk, fv = weights
    (x, edge, mk, mv, mr, key, value, recept, num, den, state, gated, middle, edge_two,
     fm, gm, sp, hid, vb, gl) = saved
    rate = jnp.exp(vec[5])
    gb, gg, gin, gn, first, sums_feed = feed_back(
        T, place, grad, gl, vb, sp, middle, edge_two, vec, mats, fk, fv
    )
    d_fv = weight_grad(hid, gb)
    d_fk = weight_grad(fm, gin)
    d_gate = weight_grad(gm, gg)
    behind = from_behind(first, -1)
    gmid, gblk, gr, gkp, gvp, gno, gdo, direct, sums_mid = mid_back(
        T, place, gn, behind, middle, grad, vec, mats, (key, value, recept, num, den), state
    )
    d_out = weight_grad(gated, gblk)
    d_recept = weight_grad(mr, gr)
    after = chain(direct, starts, rate, T, False)
    gk, gv, gn_one, first_one, sums_time = time_back(
        T, place, x, edge, vec, mats, (key, value, num, den), state, (gkp, gvp, gno, gdo), after, gr
    )
    d_key = weight_grad(mk, gk)
    d_value = weight_grad(mv, gv)
    behind_one = from_behind(first_one.reshape(edge.shape), -1)
    grad_in, sums_norm = norm_in_back(T, x, gn_one, behind_one, gmid, vec)
    d_vec = jnp.concatenate(
        [sums_norm[0:2], sums_time[0:4], sums_mid[2:3], sums_mid[0:2], sums_feed[0:2]], axis=0
    )
    return grad_in, (d_key, d_value, d_recept, d_gate, d_out), d_fk, d_fv, d_vec


def vector_rates(row_total):
    slot = jnp.arange(row_total)
    return jnp.where((slot == 5) | (slot == 6), rate_time, rate_main)[:, None]


def adam_step(parameter, gradient, first_moment, second_moment, learning_rates, decay_weight):
    new_first = beta_one * first_moment + (1.0 - beta_one) * gradient
    new_second = beta_two * second_moment + (1.0 - beta_two) * gradient * gradient
    step_ratio = (
        new_first
        / (1.0 - beta_one**step_count)
        / (jnp.sqrt(new_second / (1.0 - beta_two**step_count)) + adam_epsilon)
    )
    return (learning_rates * (step_ratio + decay_weight * parameter), new_first, new_second)


AXES = ("dp", "seq")


def body(tokens, cotangent, document_starts, *rest):
    weights, means, powers = rest[:5], rest[5:10], rest[10:15]
    vectors, matrices, time_output, feed_key, feed_value = weights
    R, T, D = tokens.shape
    layers, n = vectors.shape[0], matrices.shape[2]
    base = (lax.axis_index("seq") * T).astype(jnp.int32).reshape(1)
    place = (document_starts, base)

    def gather(part):
        return lax.all_gather(part.astype(BF16), AXES, axis=0, tiled=True)

    order = (0, 1, 2, 3)
    all_vectors = gather(vectors.transpose(2, 0, 1).reshape(n, layers * vectors.shape[1]))
    all_vectors = all_vectors.astype(F32).T.reshape(layers, vectors.shape[1], D)
    vecs = [jnp.pad(all_vectors[l], ((0, 5), (0, 0))) for l in range(layers)]
    gathered = []
    for l in range(layers):
        mats = jnp.concatenate([matrices[l, j] for j in order] + [time_output[l]], axis=1)
        gathered.append((gather(mats), gather(feed_key[l]), gather(feed_value[l])))

    x = tokens.reshape(R * T, D)
    saved = []
    for l in range(layers):
        edge = from_behind(x.reshape(R, T, D)[:, -1], 1).astype(F32)
        x, kept = layer_forward(T, place, document_starts, x, edge, vecs[l], gathered[l])
        saved.append(kept)
    block_out = x.astype(BF16).reshape(R, T, D)

    grad = cotangent.reshape(R * T, D)
    grads = [None] * layers
    for l in reversed(range(layers)):
        grad, d_mats, d_fk, d_fv, d_vec = layer_backward(
            T, place, document_starts, grad, saved[l], vecs[l], gathered[l]
        )
        vec_cols = jnp.pad(d_vec.T.astype(BF16), ((0, 0), (0, 128 - d_vec.shape[0])))

        def scatter(part):
            return lax.psum_scatter(part, AXES, scatter_dimension=0, tiled=True).astype(F32)

        g_fv = scatter(d_fv)
        g_fk = scatter(d_fk)
        g_mats = scatter(jnp.concatenate(list(d_mats) + [vec_cols], axis=1))
        grads[l] = (
            g_mats[:, 5 * D : 5 * D + vectors.shape[1]].T,
            jnp.stack([g_mats[:, j * D : (j + 1) * D] for j in range(4)]),
            g_mats[:, 4 * D : 5 * D],
            g_fk,
            g_fv,
        )
    shards = tuple(jnp.stack([g[m] for g in grads]) for m in range(5))
    rates = (vector_rates(vectors.shape[1]),) + (rate_main,) * 4
    decays = (0.0,) + (weight_decay,) * 4
    new = [adam_step(*z) for z in zip(weights, shards, means, powers, rates, decays)]
    return (
        block_out,
        grad.reshape(R, T, D),
        *shards,
        *[z[0] for z in new],
        *[z[1] for z in new],
        *[z[2] for z in new],
    )


def solution(mesh):
    tokens = P("dp", "seq", None)
    group = (
        P(None, None, AXES),
        P(None, None, AXES, None),
        P(None, AXES, None),
        P(None, AXES, None),
        P(None, AXES, None),
    )
    in_specs = (tokens, tokens, P("dp", None)) + group * 3
    out_specs = (tokens, tokens) + group * 4
    return jax.shard_map(body, mesh=mesh, in_specs=in_specs, out_specs=out_specs, check_vma=False)
```

```python
import jax
import jax.numpy as jnp
from jax import lax
from jax.experimental import pallas as pl
from jax.experimental.pallas import tpu as pltpu
from jax.sharding import Mesh, PartitionSpec as P

norm_epsilon = 1e-05
beta_one = 0.9
beta_two = 0.99
adam_epsilon = 1e-08
step_count = 10
rate_main = 0.0006
rate_time = 0.0012
weight_decay = 0.1

RB = 2
COST = 20
VMEM = 48 * 1024 * 1024
F32, BF16 = jnp.float32, jnp.bfloat16


def wide(mask, width):
    return jnp.concatenate([mask] * (width // 128), axis=1)


def dot_nn(a, b):
    return lax.dot_general(a, b, (((1,), (0,)), ((), ())), preferred_element_type=F32)


def dot_nt(a, b):
    return lax.dot_general(a, b, (((1,), (1,)), ((), ())), preferred_element_type=F32)


def colsum(a):
    return jnp.sum(a, axis=0, keepdims=True)


def places(starts_ref, base_ref, first_row, rows, T):
    at = lax.broadcasted_iota(jnp.int32, (T, 128), 0)
    base = base_ref[0]
    local, dist, tail = [], [], []
    for q in range(rows):
        begin = jnp.zeros((T, 128), jnp.int32)
        last_begin = jnp.int32(0)
        for j in range(starts_ref.shape[1]):
            s = starts_ref[first_row + q, j]
            begin = jnp.where(at + base >= s, jnp.maximum(begin, s), begin)
            last_begin = jnp.where(base + T - 1 >= s, jnp.maximum(last_begin, s), last_begin)
        local.append(at)
        dist.append(at + base - begin)
        tail.append((at + base >= last_begin).astype(F32))
    return tuple(jnp.concatenate(z, axis=0) for z in (local, dist, tail))


def norm_parts(x):
    centred = x - jnp.mean(x, axis=-1, keepdims=True)
    rstd = lax.rsqrt(jnp.mean(centred * centred, axis=-1, keepdims=True) + norm_epsilon)
    return centred * rstd, rstd


def shifted(normalized, edge, local, joined, T):
    M, D = normalized.shape
    rolled = pltpu.roll(normalized, 1, 0)
    edges = jnp.concatenate(
        [jnp.broadcast_to(edge[q : q + 1], (T, D)) for q in range(M // T)], axis=0
    )
    return jnp.where(wide(local, D) == 0, edges, rolled) * wide(joined, D)


def shift_up(masked, local, T):
    M, D = masked.shape
    rolled = pltpu.roll(masked, M - 1, 0)
    return jnp.where(wide(local, D) == T - 1, 0.0, rolled)


def row_firsts(a, T):
    return jnp.concatenate([a[q * T : q * T + 1] for q in range(a.shape[0] // T)], axis=0)


def row_lasts(a, T):
    return jnp.concatenate(
        [a[q * T + T - 1 : q * T + T] for q in range(a.shape[0] // T)], axis=0
    )


def levels(T):
    k = 1
    while k < T:
        yield k
        k *= 2


def scan_down(pair, rate, local, dist, T):
    M, D = pair[0].shape
    for k in levels(T):
        keep = ((dist >= k) & (local >= k)).astype(F32)
        weight = wide(keep, D) * jnp.exp(-float(k) * rate)
        pair = tuple(a + weight * pltpu.roll(a, k, 0) for a in pair)
    return pair


def scan_up(pair, rate, local, dist, T):
    M, D = pair[0].shape
    for k in levels(T):
        keep = ((dist >= k) & (local >= k)).astype(F32)
        weight = wide(keep, D) * jnp.exp(-float(k) * rate)
        pair = tuple(a + pltpu.roll(weight * a, M - k, 0) for a in pair)
    return pair


def per_row(values, T, D):
    return jnp.concatenate(
        [jnp.broadcast_to(values[q : q + 1], (T, D)) for q in range(values.shape[0])], axis=0
    )


def piece_copies(base, pieces, item, target, sems, at):
    count, first_in_block, first, width, rows, bits = item
    columns = pl.ds(first, width)
    if count == 1:
        return [(0, pltpu.make_async_copy(pieces[0].at[:, pl.ds(first_in_block, width)], target, sems.at[at]))]
    block, one, two, other_one, other_two = pieces
    d, c = base[1], base[2]
    copies = []
    for half, first_ref, second_ref in ((c, one, two), (1 - c, other_one, other_two)):
        start = pl.multiple_of(half * rows, rows)
        for source, m in (
            (block.at[pl.ds(start, rows), pl.ds(first_in_block, width)], 0),
            (first_ref.at[:, columns], bits[0]),
            (second_ref.at[0, :, columns], bits[1]),
            (second_ref.at[1, :, columns], bits[0] | bits[1]),
        ):
            row = pl.multiple_of(((d ^ m) * 2 + half) * rows, rows)
            copies.append(
                (m, pltpu.make_async_copy(
                    source, target.at[pl.ds(row, rows)], sems.at[at + len(copies)]
                ))
            )
    return copies


def split_refs(items, refs):
    groups, at = [], 0
    for count in items:
        groups.append(refs[at : at + count])
        at += count
    return groups, refs[at:]


def k_time_in(items, T, starts, base, x, edge, vec, *refs):
    (pieces,), (mk, mv, mr, ko, vo, ro, no, do, last, w, sems) = split_refs([items[0][0]], refs)
    D = x.shape[1]
    i = pl.program_id(0)
    copies = [
        copy
        for s, item in enumerate(items)
        for copy in piece_copies(base, pieces, item, w.at[s], sems, 8 * s)
    ]

    @pl.when(i == 0)
    def _():
        for _, copy in copies:
            copy.start()

    local, dist, _ = places(starts, base, i * RB, RB, T)
    joined = (dist >= 1).astype(F32)
    gain, bias = vec[0:1], vec[1:2]
    normalized = norm_parts(x[...].astype(F32))[0] * gain + bias
    edge_norm = norm_parts(edge[0])[0] * gain + bias
    previous = shifted(normalized, edge_norm, local, joined, T)
    for j, out in ((2, mk), (3, mv), (4, mr)):
        mu = vec[j : j + 1]
        out[...] = (normalized * mu + previous * (1.0 - mu)).astype(BF16)

    @pl.when(i == 0)
    def _():
        for _, copy in copies:
            copy.wait()

    key = dot_nn(mk[...], w[0])
    value = dot_nn(mv[...], w[1])
    ko[...] = key
    vo[...] = value
    ro[...] = dot_nn(mr[...], w[2]).astype(ro.dtype)
    rate = jnp.exp(vec[5:6])
    weight = jnp.exp(key)
    num, den = scan_down((weight * value, weight), rate, local, dist, T)
    keep = wide(((dist >= 1) & (local >= 1)).astype(F32), D)
    no[...] = keep * pltpu.roll(num, 1, 0)
    do[...] = keep * pltpu.roll(den, 1, 0)
    ends = (row_lasts(num, T), row_lasts(den, T))
    for q in range(RB):
        last[q] = jnp.concatenate([ends[0][q : q + 1], ends[1][q : q + 1]], axis=0)


def decay_state(vec, key, value, num, den, state, local, dist, T):
    D = key.shape[1]
    rate = jnp.exp(vec[5:6])
    fade = wide((dist >= local + 1).astype(F32), D) * jnp.exp(
        -wide(local.astype(F32), D) * rate
    )
    full_n = num + fade * per_row(state[:, 0], T, D)
    full_d = den + fade * per_row(state[:, 1], T, D)
    extra = jnp.exp(vec[6:7] + key)
    inverse = 1.0 / (full_d + extra)
    mean = (full_n + extra * value) * inverse
    return full_n, full_d, extra, inverse, mean


def k_time_out(items, T, starts, base, x, key, value, recept, num, den, state, vec, *refs):
    (pieces,), (gated, middle, w, sems) = split_refs([items[0][0]], refs)
    i = pl.program_id(0)
    copies = piece_copies(base, pieces, items[0], w, sems, 0)

    @pl.when(i == 0)
    def _():
        for _, copy in copies:
            copy.start()

    local, dist, _ = places(starts, base, i * RB, RB, T)
    mean = decay_state(
        vec, key[...], value[...], num[...], den[...], state[...], local, dist, T
    )[4]
    gated[...] = (jax.nn.sigmoid(recept[...].astype(F32)) * mean).astype(BF16)

    @pl.when(i == 0)
    def _():
        for _, copy in copies:
            copy.wait()

    middle[...] = x[...].astype(F32) + dot_nn(gated[...], w[...])


def feed_copies(items, base, gate_pieces, key_pieces, value_pieces, wg, wk, wv, sems):
    gate = piece_copies(base, gate_pieces, items[0], wg, sems, 0)
    keys = [
        piece_copies(base, key_pieces, item, wk.at[b], sems, 8 + 8 * b)
        for b, item in enumerate(items[1:-1])
    ]
    values = piece_copies(base, value_pieces, items[-1], wv, sems, 8 * len(items) - 8)
    return gate, keys, values


def feed_start(copies):
    gate, keys, values = copies
    for _, copy in keys[0] + values + [z for block in keys[1:] for z in block] + gate:
        copy.start()


def feed_wait(copies, base, j):
    gate, keys, values = copies
    for b, block in enumerate(keys):

        @pl.when(j == b)
        def _():
            for _, copy in block:
                copy.wait()

    whole = len(values) == 1
    for m, copy in values:

        @pl.when((j == 0) if whole else ((base[1] ^ m) == j))
        def _():
            copy.wait()


def k_feed(items, T, starts, base, middle, edge, vec, *refs):
    counts = [items[0][0], items[1][0], items[-1][0]]
    pieces, (fm, gm, sp, hid, vb, gl, xo, acc, wg, wk, wv, sems) = split_refs(counts, refs)
    M, D = middle.shape
    j = pl.program_id(0)
    copies = feed_copies(items, base, *pieces, wg, wk, wv, sems)

    @pl.when(j == 0)
    def _():
        feed_start(copies)
        local, dist, _ = places(starts, base, 0, M // T, T)
        gain, bias = vec[7:8], vec[8:9]
        normalized = norm_parts(middle[...])[0] * gain + bias
        edge_norm = norm_parts(edge[...])[0] * gain + bias
        previous = shifted(normalized, edge_norm, local, (dist >= 1).astype(F32), T)
        for row, out in ((9, fm), (10, gm)):
            mu = vec[row : row + 1]
            out[...] = (normalized * mu + previous * (1.0 - mu)).astype(BF16)
        acc[...] = jnp.zeros_like(acc)

    feed_wait(copies, base, j)
    block = pl.ds(pl.multiple_of(j * D, D), D)
    pre = dot_nn(fm[...], wk[j])
    soft = jnp.maximum(pre, 0.0) + jnp.log1p(jnp.exp(-jnp.abs(pre)))
    sp[...] = soft.astype(BF16)
    hidden = (soft * soft).astype(BF16)
    hid[...] = hidden
    acc[...] += dot_nn(hidden, wv[block])

    @pl.when(j == pl.num_programs(0) - 1)
    def _():
        for _, copy in copies[0]:
            copy.wait()
        gate = dot_nn(gm[...], wg[...])
        gl[...] = gate.astype(BF16)
        vb[...] = acc[...].astype(BF16)
        xo[...] = middle[...] + jax.nn.sigmoid(gate) * acc[...]


def k_feed_back(items, T, starts, base, grad, gl, vb, sp, middle, edge, vec, *refs):
    counts = [items[0][0], items[1][0], items[-1][0]]
    pieces, (gb, gg, gin, gn, first, sums, acc, wg, wk, wv, sems) = split_refs(counts, refs)
    M, D = middle.shape
    j = pl.program_id(0)
    copies = feed_copies(items, base, *pieces, wg, wk, wv, sems)

    @pl.when(j == 0)
    def _():
        feed_start(copies)
        g = grad[...].astype(F32)
        s = jax.nn.sigmoid(gl[...].astype(F32))
        gb[...] = (g * s).astype(BF16)
        gg[...] = (g * vb[...].astype(F32) * s * (1.0 - s)).astype(BF16)
        acc[...] = jnp.zeros_like(acc)

    feed_wait(copies, base, j)
    soft = sp[...].astype(F32)
    gh = dot_nt(gb[...], wv[pl.ds(pl.multiple_of(j * D, D), D)])
    pre = (gh * (2.0 * soft * (1.0 - jnp.exp(-soft)))).astype(BF16)
    gin[...] = pre
    acc[...] += dot_nt(pre, wk[j])

    @pl.when(j == pl.num_programs(0) - 1)
    def _():
        local, dist, _ = places(starts, base, 0, M // T, T)
        joined = (dist >= 1).astype(F32)
        gain, bias = vec[7:8], vec[8:9]
        normalized = norm_parts(middle[...])[0] * gain + bias
        edge_norm = norm_parts(edge[...])[0] * gain + bias
        difference = normalized - shifted(normalized, edge_norm, local, joined, T)
        ga = acc[...]
        for _, copy in copies[0]:
            copy.wait()
        gc = dot_nt(gg[...], wg[...])
        sums[0:1] = colsum(ga * difference)
        sums[1:2] = colsum(gc * difference)
        sums[2:8] = jnp.zeros((6, D), F32)
        mu_a, mu_c = vec[9:10], vec[10:11]
        masked = (ga * (1.0 - mu_a) + gc * (1.0 - mu_c)) * wide(joined, D)
        gn[...] = ga * mu_a + gc * mu_c + shift_up(masked, local, T)
        first[...] = row_firsts(masked, T)


def norm_back(x, gain, gn):
    hat, rstd = norm_parts(x)
    scaled = gn * gain
    gx = rstd * (
        scaled
        - jnp.mean(scaled, axis=-1, keepdims=True)
        - hat * jnp.mean(scaled * hat, axis=-1, keepdims=True)
    )
    return gx, colsum(gn * hat), colsum(gn)


def with_edge(gn, edge, local, T):
    D = gn.shape[1]
    return gn + jnp.where(wide(local, D) == T - 1, per_row(edge, T, D), 0.0)


def k_mid_back(items, T, starts, base, gn, edge, middle, grad, vec,
               key, value, recept, num, den, state, *refs):
    (pieces,), (gm, gblk, gr, gkp, gvp, gno, gdo, direct, sums, w, sems) = split_refs(
        [items[0][0]], refs
    )
    D = middle.shape[1]
    i = pl.program_id(0)
    copies = piece_copies(base, pieces, items[0], w, sems, 0)

    @pl.when(i == 0)
    def _():
        for _, copy in copies:
            copy.start()

    local, dist, _ = places(starts, base, i * RB, RB, T)
    total = with_edge(gn[...], edge[0], local, T)
    gx, ggain, gbias = norm_back(middle[...], vec[7:8], total)
    gmid = grad[...].astype(F32) + gx
    gm[...] = gmid
    gblk[...] = gmid.astype(BF16)

    @pl.when(i == 0)
    def _():
        for _, copy in copies:
            copy.wait()

    ggated = dot_nt(gblk[...], w[...])
    v = value[...]
    _, _, extra, inverse, mean = decay_state(
        vec, key[...], v, num[...], den[...], state[...], local, dist, T
    )
    s = jax.nn.sigmoid(recept[...].astype(F32))
    gr[...] = (ggated * mean * s * (1.0 - s)).astype(BF16)
    q = ggated * s * inverse
    ge = extra * q * (v - mean)
    gkp[...] = ge
    gvp[...] = q * extra
    rate = jnp.exp(vec[5:6])
    an, ad = scan_up((q, -q * mean), rate, local, dist, T)
    keep = wide(((dist >= 1) & (local >= 1)).astype(F32), D)
    gno[...] = pltpu.roll(keep * an, an.shape[0] - 1, 0)
    gdo[...] = pltpu.roll(keep * ad, ad.shape[0] - 1, 0)
    joined = wide((dist >= 1).astype(F32), D)
    ends = (row_firsts(joined * an, T), row_firsts(joined * ad, T))
    for r in range(RB):
        direct[r] = jnp.concatenate([ends[0][r : r + 1], ends[1][r : r + 1]], axis=0)

    @pl.when(i == 0)
    def _():
        sums[...] = jnp.zeros_like(sums)

    sums[0:1] += ggain
    sums[1:2] += gbias
    sums[2:3] += colsum(ge)


def k_time_back(items, T, starts, base, x, edge, vec, key, value, num, den, state,
                gkp, gvp, gno, gdo, after, gr, *refs):
    (pieces,), (gk, gv, gn, first, sums, w, sems) = split_refs([items[0][0]], refs)
    D = x.shape[1]
    i = pl.program_id(0)
    copies = [
        copy
        for s, item in enumerate(items)
        for copy in piece_copies(base, pieces, item, w.at[s], sems, 8 * s)
    ]

    @pl.when(i == 0)
    def _():
        for _, copy in copies:
            copy.start()

    local, dist, tail = places(starts, base, i * RB, RB, T)
    rate = jnp.exp(vec[5:6])
    fade = wide((dist >= local + 1).astype(F32), D) * jnp.exp(
        -wide(local.astype(F32), D) * rate
    )
    st = state[...]
    full_n = num[...] + fade * per_row(st[:, 0], T, D)
    full_d = den[...] + fade * per_row(st[:, 1], T, D)
    left = wide(tail, D) * jnp.exp(-wide((T - 1 - local).astype(F32), D) * rate)
    af = after[...]
    grad_n = gno[...] + left * per_row(af[:, 0], T, D)
    grad_d = gdo[...] + left * per_row(af[:, 1], T, D)
    weight = jnp.exp(key[...])
    gk[...] = (gkp[...] + weight * (grad_n * value[...] + grad_d)).astype(BF16)
    gv[...] = (gvp[...] + weight * grad_n).astype(BF16)
    joined = (dist >= 1).astype(F32)
    gain, bias = vec[0:1], vec[1:2]
    normalized = norm_parts(x[...].astype(F32))[0] * gain + bias
    edge_norm = norm_parts(edge[0])[0] * gain + bias
    difference = normalized - shifted(normalized, edge_norm, local, joined, T)

    @pl.when(i == 0)
    def _():
        sums[...] = jnp.zeros_like(sums)

    sums[3:4] += -rate * jnp.exp(-rate) * colsum(grad_n * full_n + grad_d * full_d)
    grad_norm = jnp.zeros(x.shape, F32)
    grad_prev = jnp.zeros(x.shape, F32)

    @pl.when(i == 0)
    def _():
        for _, copy in copies:
            copy.wait()

    for row, g in enumerate((gk, gv, gr)):
        mu = vec[2 + row : 3 + row]
        g_mix = dot_nt(g[...], w[row])
        sums[row : row + 1] += colsum(g_mix * difference)
        grad_norm = grad_norm + g_mix * mu
        grad_prev = grad_prev + g_mix * (1.0 - mu)
    masked = grad_prev * wide(joined, D)
    gn[...] = grad_norm + shift_up(masked, local, T)
    first[0] = row_firsts(masked, T)


def k_norm_back(T, x, gn, edge, gmid, vec, go, sums):
    i = pl.program_id(0)
    M = x.shape[0]
    at = lax.broadcasted_iota(jnp.int32, (T, 128), 0)
    local = jnp.concatenate([at] * (M // T), axis=0)
    total = with_edge(gn[...], edge[0], local, T)
    gx, ggain, gbias = norm_back(x[...].astype(F32), vec[0:1], total)
    go[...] = gmid[...] + gx

    @pl.when(i == 0)
    def _():
        sums[...] = jnp.zeros_like(sums)

    sums[0:1] += ggain
    sums[1:2] += gbias


def k_weight_grad(count, T, *refs):
    lefts, grads, (out, left, grad, sems) = refs[:count], refs[count : 2 * count], refs[2 * count :]
    i = pl.program_id(0)
    pairs = [
        [
            pltpu.make_async_copy(source, target.at[n], sems.at[2 * n + side])
            for side, (source, target) in enumerate(((lefts[n], left), (grads[n], grad)))
        ]
        for n in range(count)
    ]

    @pl.when(i == 0)
    def _():
        for pair in pairs:
            for copy in pair:
                copy.start()

    for n, pair in enumerate(pairs):

        @pl.when(i == n)
        def _():
            for copy in pair:
                copy.wait()

    out[0] = lax.dot_general(
        left[i], grad[i], (((0,), (0,)), ((), ())), preferred_element_type=F32
    ).astype(BF16)


def smem():
    return pl.BlockSpec(memory_space=pltpu.SMEM)


def rows_spec(T, D):
    return pl.BlockSpec((RB * T, D), lambda i: (i, 0))


def col_spec(rows, width, at):
    return pl.BlockSpec((rows, width), lambda i: (0, at))


def whole_spec(shape):
    zeros = (0,) * len(shape)
    return pl.BlockSpec(shape, lambda i: zeros)


def edge_spec(D):
    return pl.BlockSpec((1, RB, D), lambda i: (i, 0, 0))


def state_spec(D):
    return pl.BlockSpec((RB, 2, D), lambda i: (i, 0, 0))


def shape(dims, kind):
    return jax.ShapeDtypeStruct(dims, kind)


def run(kernel, T, grid, in_specs, out_specs, outs, args, flops, moved, scratch=(), items=(),
        after=()):
    count = len(args)
    in_specs = in_specs + anywhere(len(after))
    args = args + tuple(after)

    def body(*refs):
        kernel(*((items,) if items else ()), T, *refs[:count], *refs[count + len(after) :])

    return pl.pallas_call(
        body,
        grid=(grid,),
        in_specs=in_specs,
        out_specs=out_specs,
        out_shape=outs,
        scratch_shapes=scratch,
        compiler_params=pltpu.CompilerParams(
            dimension_semantics=("arbitrary",), vmem_limit_bytes=VMEM
        ),
        cost_estimate=pl.CostEstimate(
            flops=flops // COST, bytes_accessed=moved // COST, transcendentals=0
        ),
        name=kernel.__name__,
    )(*args)


def anywhere(count):
    return [pl.BlockSpec(memory_space=pl.ANY)] * count


def weight_room(shapes, copies):
    return [pltpu.VMEM(s, BF16) for s in shapes] + [pltpu.SemaphoreType.DMA((copies,))]


def time_in(T, place, x, edge, vec, weights, after=()):
    N, D = x.shape
    R = N // T
    rs = rows_spec(T, D)
    pieces = weights["key"][0]
    items = [weights[name][1] for name in ("key", "value", "recept")]
    return run(
        k_time_in, T, R // RB,
        [smem(), smem(), rs, edge_spec(D), whole_spec(vec.shape)] + anywhere(len(pieces)),
        [rs] * 8 + [state_spec(D)],
        [shape((N, D), BF16)] * 3 + [shape((N, D), F32)] * 2 + [shape((N, D), BF16)]
        + [shape((N, D), F32)] * 2 + [shape((R, 2, D), F32)],
        (*place, x, edge.reshape(R // RB, RB, D), vec, *pieces),
        6 * N * D * D, 40 * N * D,
        weight_room([(3, D, D)], 24), items, after,
    )


def time_out(T, place, x, kept, state, vec, weights, after=()):
    N, D = x.shape
    R = N // T
    rs = rows_spec(T, D)
    pieces, item = weights["output"]
    return run(
        k_time_out, T, R // RB,
        [smem(), smem()] + [rs] * 6 + [state_spec(D), whole_spec(vec.shape)] + anywhere(len(pieces)),
        [rs] * 2,
        [shape((N, D), BF16), shape((N, D), F32)],
        (*place, x, *kept, state, vec, *pieces),
        2 * N * D * D, 30 * N * D,
        weight_room([(D, D)], 8), [item], after,
    )


def feed_weights(weights):
    blocks = sorted(name for name in weights if name.startswith("feed_key"))
    items = [weights[name][1] for name in ["gate"] + blocks + ["feed_value"]]
    pieces = weights["gate"][0] + weights[blocks[0]][0] + weights["feed_value"][0]
    return items, pieces


def feed(T, place, middle, edge, vec, weights, after=()):
    N, D = middle.shape
    items, pieces = feed_weights(weights)
    B = len(items) - 2
    F = B * D
    whole = whole_spec((N, D))
    wide_spec = pl.BlockSpec((N, D), lambda j: (0, j))
    return run(
        k_feed, T, B,
        [smem(), smem(), whole, whole_spec(edge.shape), whole_spec(vec.shape)] + anywhere(len(pieces)),
        [whole, whole, wide_spec, wide_spec, whole, whole, whole],
        [shape((N, D), BF16)] * 2 + [shape((N, F), BF16)] * 2 + [shape((N, D), BF16)] * 2
        + [shape((N, D), F32)],
        (*place, middle, edge, vec, *pieces),
        4 * N * D * F + 2 * N * D * D, 20 * N * D + 4 * N * F + 4 * D * F,
        [pltpu.VMEM((N, D), F32)]
        + weight_room([(D, D), (B, D, D), (F, D)], 8 * len(items)), items, after,
    )


def feed_back(T, place, grad, gl, vb, sp, middle, edge, vec, weights, after=()):
    N, D = middle.shape
    items, pieces = feed_weights(weights)
    B = len(items) - 2
    F = B * D
    R = N // T
    whole = whole_spec((N, D))
    wide_spec = pl.BlockSpec((N, D), lambda j: (0, j))
    return run(
        k_feed_back, T, B,
        [smem(), smem(), whole, whole, whole, wide_spec, whole, whole_spec(edge.shape),
         whole_spec(vec.shape)] + anywhere(len(pieces)),
        [whole, whole, wide_spec, whole, whole_spec((R, D)), whole_spec((8, D))],
        [shape((N, D), BF16)] * 2 + [shape((N, F), BF16), shape((N, D), F32)]
        + [shape((R, D), F32), shape((8, D), F32)],
        (*place, grad, gl, vb, sp, middle, edge, vec, *pieces),
        4 * N * D * F + 2 * N * D * D, 20 * N * D + 4 * N * F + 4 * D * F,
        [pltpu.VMEM((N, D), F32)]
        + weight_room([(D, D), (B, D, D), (F, D)], 8 * len(items)), items, after,
    )


def mid_back(T, place, gn, edge, middle, grad, vec, weights, kept, state, after=()):
    N, D = middle.shape
    R = N // T
    rs = rows_spec(T, D)
    pieces, item = weights["output"]
    return run(
        k_mid_back, T, R // RB,
        [smem(), smem(), rs, edge_spec(D), rs, rs, whole_spec(vec.shape)]
        + [rs] * 5 + [state_spec(D)] + anywhere(len(pieces)),
        [rs] * 7 + [state_spec(D), whole_spec((8, D))],
        [shape((N, D), F32)] + [shape((N, D), BF16)] * 2 + [shape((N, D), F32)] * 4
        + [shape((R, 2, D), F32), shape((8, D), F32)],
        (*place, gn, edge.reshape(R // RB, RB, D), middle, grad, vec, *kept, state, *pieces),
        2 * N * D * D, 50 * N * D,
        weight_room([(D, D)], 8), [item], after,
    )


def time_back(T, place, x, edge, vec, weights, kept, state, part, later, gr, after=()):
    N, D = x.shape
    R = N // T
    rs = rows_spec(T, D)
    pieces = weights["key"][0]
    items = [weights[name][1] for name in ("key", "value", "recept")]
    return run(
        k_time_back, T, R // RB,
        [smem(), smem(), rs, edge_spec(D), whole_spec(vec.shape)]
        + [rs] * 4 + [state_spec(D)] + [rs] * 4 + [state_spec(D), rs] + anywhere(len(pieces)),
        [rs] * 3 + [edge_spec(D), whole_spec((8, D))],
        [shape((N, D), BF16)] * 2 + [shape((N, D), F32)]
        + [shape((R // RB, RB, D), F32), shape((8, D), F32)],
        (*place, x, edge.reshape(R // RB, RB, D), vec, *kept, state, *part, later, gr, *pieces),
        6 * N * D * D, 50 * N * D,
        weight_room([(3, D, D)], 24), items, after,
    )


def norm_in_back(T, x, gn, edge, gmid, vec, after=()):
    N, D = x.shape
    R = N // T
    rs = rows_spec(T, D)
    return run(
        k_norm_back, T, R // RB,
        [rs, rs, edge_spec(D), rs, whole_spec(vec.shape)],
        [rs, whole_spec((8, D))],
        [shape((N, D), F32), shape((8, D), F32)],
        (x, gn, edge.reshape(R // RB, RB, D), gmid, vec),
        0, 16 * N * D, after=after,
    )


SEQ = ("z", "c")
SWAP = [(0, 1), (1, 0)]


def by_bit(block, bit):
    return lax.ppermute(block, "dp", [(i, i ^ bit) for i in range(lax.axis_size("dp"))])


def after(value, *others):
    return lax.optimization_barrier((value, *others))[0]


def gather_seq(part, *gate):
    return lax.all_gather(after(part, *gate), SEQ, axis=0, tiled=True)


class Exchange:
    def __init__(self, block, names, start, bits):
        self.block, self.names, self.start, self.bits = block, names, start, bits
        self.width = sum(width for _, width in names)
        self.rows = block.shape[0] // 2

    def first(self, *gate):
        block = after(self.block, *gate)
        self.own = lax.dynamic_slice(
            block, (lax.axis_index("c") * self.rows, self.start), (self.rows, self.width)
        )
        self.one = by_bit(self.own, self.bits[0])
        return self.one

    def second(self, *gate):
        one = after(self.one, *gate)
        self.two = by_bit(jnp.stack([self.own, one]), self.bits[1])
        return self.two

    def cores(self, *gate):
        one, two = after((self.one, self.two), *gate)
        self.other_one = lax.ppermute(one, "c", SWAP)
        self.other_two = lax.ppermute(two, "c", SWAP)

    def weights(self):
        pieces = (self.block, self.one, self.two, self.other_one, self.other_two)
        at, found = 0, {}
        for name, width in self.names:
            found[name] = (pieces, (5, self.start + at, at, width, self.rows, self.bits))
            at += width
        return found


class Scatter:
    def __init__(self, grads, bits):
        I, _, C = grads.shape
        self.bits = bits
        self.view = grads.reshape(I, 2, 2, lax.axis_size("z"), 2, -1, C)

    def pick(self, which):
        return lax.dynamic_index_in_dim(self.view, which, 4, keepdims=False)

    def cores(self):
        c, d = lax.axis_index("c"), lax.axis_index("dp")
        self.received = lax.ppermute(self.pick(1 - c), "c", SWAP)
        self.axis, self.me, self.then = (
            (1, d // 2, d % 2) if self.bits[1] == 2 else (2, d % 2, d // 2)
        )
        return self.received

    def part(self, a, axis, which):
        return lax.dynamic_index_in_dim(a, which, axis, keepdims=False).astype(F32)

    def first(self):
        mine = self.pick(lax.axis_index("c"))
        give = 1 - self.me
        send = self.part(mine, self.axis, give) + self.part(self.received, self.axis, give)
        got = by_bit(send.astype(BF16), self.bits[1])
        keep = self.part(mine, self.axis, self.me) + self.part(self.received, self.axis, self.me)
        self.kept = keep + got.astype(F32)
        return got

    def second(self):
        got = by_bit(self.part(self.kept, 1, 1 - self.then).astype(BF16), self.bits[0])
        total = (self.part(self.kept, 1, self.then) + got.astype(F32)).astype(BF16)
        I, C = total.shape[0], total.shape[-1]
        self.total = total.transpose(1, 0, 2, 3).reshape(-1, C)
        self.count = I
        return got

    def last(self):
        if hasattr(self, "out"):
            return self.out
        out = lax.psum_scatter(self.total, "z", scatter_dimension=0, tiled=True)
        self.out = out.reshape(self.count, -1, out.shape[1])
        return self.out


def from_behind(block, distance):
    devices = range(lax.axis_size(SEQ))
    route = [(i - distance, i) for i in devices if i - distance in devices]
    return lax.ppermute(block, SEQ, route)


def chain(mine, starts, rate, T, forward):
    S, i = lax.axis_size(SEQ), lax.axis_index(SEQ)
    all_states = lax.all_gather(mine.astype(BF16), SEQ).astype(F32)
    j = jnp.arange(S, dtype=jnp.int32)

    def document(at):
        return jnp.sum((starts[None] <= at[:, None, None]).astype(jnp.int32), axis=2)

    if forward:
        lag = i - 1 - j
        same = document((j + 1) * T - 1) == document((i * T - 1)[None])
    else:
        lag = j - 1 - i
        same = document(j * T - 1) == document(((i + 1) * T - 1)[None])
    keep = (same & (lag >= 0)[:, None]).astype(F32)
    fade = jnp.exp(-(T * jnp.maximum(lag, 0)).astype(F32)[:, None] * rate[None])
    weight = keep[:, :, None, None] * fade[:, None, None, :]
    return jnp.sum(weight * all_states, axis=0)


def layer_forward(T, place, starts, x, edge, vec, weights, hook):
    N, D = x.shape
    R = N // T
    rate = jnp.exp(vec[5])
    x = hook("start", x)
    mk, mv, mr, key, value, recept, num, den, last = time_in(T, place, x, edge, vec, weights())
    last = hook("time in", last)
    state = chain(last, starts, rate, T, True)
    state = hook("chain", state)
    gated, middle = time_out(T, place, x, (key, value, recept, num, den), state, vec, weights())
    middle = hook("time out", middle)
    edge_two = from_behind(middle.reshape(R, T, D)[:, -1], 1)
    edge_two = hook("edge", edge_two)
    fm, gm, sp, hid, vb, gl, out = feed(T, place, middle, edge_two, vec, weights())
    out = hook("feed", out)
    saved = (x, edge, mk, mv, mr, key, value, recept, num, den, state, gated, middle, edge_two,
             fm, gm, sp, hid, vb, gl)
    return out, saved


def weight_grads(lefts, gradients):
    count, (N, D), C = len(lefts), lefts[0].shape, gradients[0].shape[1]
    return run(
        k_weight_grad, 0, count, anywhere(2 * count),
        [pl.BlockSpec((1, D, C), lambda i: (i, 0, 0))], [shape((count, D, C), BF16)],
        (*lefts, *gradients), 2 * count * N * D * C, 2 * count * (N * (D + C) + D * C),
        [pltpu.VMEM((count, N, D), BF16), pltpu.VMEM((count, N, C), BF16),
         pltpu.SemaphoreType.DMA((2 * count,))], count,
    )[0]


def weight_grad(left, gradient):
    return lax.dot_general(
        left, gradient, (((0,), (0,)), ((), ())), preferred_element_type=F32
    ).astype(BF16)


def layer_backward(T, place, starts, grad, saved, vec, weights, work):
    (x, edge, mk, mv, mr, key, value, recept, num, den, state, gated, middle, edge_two,
     fm, gm, sp, hid, vb, gl) = saved
    rate = jnp.exp(vec[5])
    gb, gg, gin, gn, first, sums_feed = feed_back(
        T, place, grad, gl, vb, sp, middle, edge_two, vec, weights, work("feed")
    )
    behind = from_behind(first, -1)
    work("feed done", hid=hid, gb=gb, fm=fm, gin=gin)
    gmid, gblk, gr, gkp, gvp, gno, gdo, direct, sums_mid = mid_back(
        T, place, gn, behind, middle, grad, vec, weights, (key, value, recept, num, den), state,
        work("mid"),
    )
    after_state = chain(direct, starts, rate, T, False)
    gk, gv, gn_one, first_one, sums_time = time_back(
        T, place, x, edge, vec, weights, (key, value, num, den), state, (gkp, gvp, gno, gdo),
        after_state, gr, work("time"),
    )
    behind_one = from_behind(first_one.reshape(edge.shape), -1)
    work("time done", lefts=(mk, mv, mr, gm, gated), grads=(gk, gv, gr, gg, gblk))
    grad_in, sums_norm = norm_in_back(T, x, gn_one, behind_one, gmid, vec, work("norm"))
    d_vec = jnp.concatenate(
        [sums_norm[0:2], sums_time[0:4], sums_mid[2:3], sums_mid[0:2], sums_feed[0:2]], axis=0
    )
    return grad_in, d_vec


def vector_rates(row_total):
    slot = jnp.arange(row_total)
    return jnp.where((slot == 5) | (slot == 6), rate_time, rate_main)[:, None]


def adam_step(parameter, gradient, first_moment, second_moment, learning_rates, decay_weight):
    new_first = beta_one * first_moment + (1.0 - beta_one) * gradient
    new_second = beta_two * second_moment + (1.0 - beta_two) * gradient * gradient
    step_ratio = (
        new_first
        / (1.0 - beta_one**step_count)
        / (jnp.sqrt(new_second / (1.0 - beta_two**step_count)) + adam_epsilon)
    )
    return (learning_rates * (step_ratio + decay_weight * parameter), new_first, new_second)


AXES = ("dp", "z", "c")
XY, YX = (1, 2), (2, 1)


def body(tokens, cotangent, document_starts, *rest):
    weights, means, powers = rest[:5], rest[5:10], rest[10:15]
    vectors, matrices, time_output, feed_key, feed_value = weights
    R, T, D = tokens.shape
    layers, kinds, n = vectors.shape
    blocks = feed_key.shape[2] // D
    base = jnp.stack(
        [lax.axis_index(SEQ) * T, lax.axis_index("dp"), lax.axis_index("c")]
    ).astype(jnp.int32)
    place = (document_starts, base)

    keys = [(f"feed_key{b}", D) for b in range(blocks)]
    time_names = [("key", D), ("value", D), ("recept", D)]
    rest_names = [("gate", D), ("output", D)]
    values = [("feed_value", D)]
    layout = [[time_names + [("vectors", 128)], rest_names + keys, values]]
    layout += [[time_names + rest_names, keys, values]] * (layers - 1)

    vector_columns = jnp.pad(
        vectors.reshape(layers * kinds, n).T, ((0, 0), (0, 128 - layers * kinds))
    )

    def shard(l, names):
        found = {
            "key": matrices[l, 0], "value": matrices[l, 1], "recept": matrices[l, 2],
            "gate": matrices[l, 3], "output": time_output[l], "feed_value": feed_value[l],
            "vectors": vector_columns,
        }
        for b in range(blocks):
            found[f"feed_key{b}"] = feed_key[l, :, b * D : (b + 1) * D]
        return jnp.concatenate([found[name].astype(BF16) for name, _ in names], axis=1)

    def sets_of(l, k, gate, *split):
        block = gather_seq(shard(l, layout[l][k]), *gate)
        sets, at = [], 0
        for count, bits in split:
            names = layout[l][k][at : at + count]
            sets.append(Exchange(block, names, sum(w for _, w in layout[l][k][:at]), bits))
            at += count
        return sets

    def weights_of(l):
        def found():
            have = {}
            for exchange in here[l]:
                if hasattr(exchange, "other_two"):
                    have.update(exchange.weights())
            return have

        return found

    here = [[] for _ in range(layers)]
    A = sets_of(0, 0, (), (4, XY))[0]
    B = sets_of(0, 1, (), (2 + blocks, XY)) + sets_of(0, 2, (), (1, YX))
    here[0] = [A] + B
    A.first()
    A.second()
    A.cores()
    pieces, item = A.weights()["vectors"]
    d, c = lax.axis_index("dp"), lax.axis_index("c")
    block, one, two, other_one, other_two = (a[..., item[2] : item[2] + 128] for a in pieces)
    bits, half = item[5], item[4]
    mine = lax.dynamic_slice_in_dim(block, c * half, half, axis=0)
    other = lax.dynamic_slice_in_dim(block, (1 - c) * half, half, axis=0)
    by_m = {
        0: (mine, other), bits[0]: (one, other_one), bits[1]: (two[0], other_two[0]),
        bits[0] | bits[1]: (two[1], other_two[1]),
    }
    rel = jnp.stack([jnp.stack(by_m[m]) for m in range(4)])
    rel = jnp.where(c == 0, rel, rel[:, ::-1])
    columns = jnp.stack([lax.dynamic_index_in_dim(rel, d ^ j, 0, keepdims=False) for j in range(4)])
    spread = columns.reshape(D, 128)[:, : layers * kinds].astype(F32).T.reshape(layers, kinds, D)
    vecs = [jnp.pad(spread[l], ((0, 16 - kinds), (0, 0))) for l in range(layers)]

    def hook_of(l):
        more = l + 1 < layers

        def hook(name, value):
            nonlocal B
            if name == "start":
                if l > 0:
                    F = here[l][2:]
                    hook.F = F
                    for e in F:
                        e.first(value)
                    return value
                for e in B:
                    e.first(A.two)
            elif name == "time in":
                if l == 0:
                    value = after(value, *[e.one for e in B])
                    for e in B:
                        e.second(value)
                else:
                    value = after(value, *[e.one for e in hook.F])
                    for e in hook.F:
                        e.second(value)
            elif name == "chain":
                F = B if l == 0 else hook.F
                value = after(value, *[e.two for e in F])
                for e in F:
                    e.cores(value)
                if more:
                    hook.M = here[l + 1][:2]
                    for e in hook.M:
                        e.first(value)
            elif name == "time out" and more:
                value = after(value, *[e.one for e in hook.M])
            elif name == "edge" and more:
                for e in hook.M:
                    e.second(value)
            elif name == "feed" and more:
                value = after(value, *[e.two for e in hook.M])
                for e in hook.M:
                    e.cores(value)
            return value

        return hook

    for l in range(1, layers):
        here[l] = (
            sets_of(l, 0, (A.one,), (3, XY), (2, YX))
            + sets_of(l, 1, (A.two,), (blocks, XY))
            + sets_of(l, 2, (A.two,), (1, YX))
        )
    x = tokens.reshape(R * T, D)
    saved = []
    for l in range(layers):
        edge = from_behind(x.reshape(R, T, D)[:, -1], 1).astype(F32)
        x, kept = layer_forward(
            T, place, document_starts, x, edge, vecs[l], weights_of(l), hook_of(l)
        )
        saved.append(kept)
    block_out = x.astype(BF16).reshape(R, T, D)

    grad = cotangent.reshape(R * T, D)
    scatters = [None] * layers
    vec_grads = [None] * layers
    running = []

    def advance():
        nonlocal running
        waits = []
        for entry in running:
            scatter = entry[0]
            waits.append((scatter.cores, scatter.first, scatter.second, scatter.last)[entry[1]]())
            entry[1] += 1
        running = [entry for entry in running if entry[1] < 4]
        return waits

    def work_of(l):
        def work(place_name, **have):
            nonlocal running
            if place_name == "feed done":
                fv = Scatter(weight_grad(have["hid"], have["gb"])[None], YX)
                fk = Scatter(weight_grad(have["fm"], have["gin"])[None], XY)
                scatters[l] = [fv, fk]
                running += [[fv, 0], [fk, 0]]
                return ()
            if place_name == "time done":
                m = Scatter(weight_grads(have["lefts"], have["grads"]), XY)
                scatters[l].append(m)
                running += [[m, 0]]
                return ()
            if place_name == "norm":
                return ()
            return advance()

        return work

    for l in reversed(range(layers)):
        grad, vec_grads[l] = layer_backward(
            T, place, document_starts, grad, saved[l], vecs[l], weights_of(l)(), work_of(l)
        )
    vec_columns = jnp.concatenate([g.T for g in vec_grads], axis=1).astype(BF16)
    vec_columns = jnp.pad(vec_columns, ((0, 0), (0, 128 - layers * kinds)))
    vec_scatter = Scatter(vec_columns[None], XY)
    running += [[vec_scatter, 0]]
    while running:
        advance()
    g_vec = vec_scatter.last()[0].astype(F32)
    grads = []
    for l in range(layers):
        g_fv, g_fk, g_m = (s.last().astype(F32) for s in scatters[l])
        grads.append((g_vec[:, l * kinds : (l + 1) * kinds].T, g_m[:4], g_m[4], g_fk[0], g_fv[0]))
    shards = tuple(jnp.stack([g[m] for g in grads]) for m in range(5))
    rates = (vector_rates(kinds),) + (rate_main,) * 4
    decays = (0.0,) + (weight_decay,) * 4
    new = [adam_step(*z) for z in zip(weights, shards, means, powers, rates, decays)]
    return (
        block_out,
        grad.reshape(R, T, D),
        *shards,
        *[z[0] for z in new],
        *[z[1] for z in new],
        *[z[2] for z in new],
    )


def solution(mesh):
    dp, seq = mesh.shape["dp"], mesh.shape["seq"]
    mesh = Mesh(mesh.devices.reshape(dp, seq // 2, 2), AXES)
    tokens = P("dp", SEQ, None)
    group = (
        P(None, None, AXES),
        P(None, None, AXES, None),
        P(None, AXES, None),
        P(None, AXES, None),
        P(None, AXES, None),
    )
    in_specs = (tokens, tokens, P("dp", None)) + group * 3
    out_specs = (tokens, tokens) + group * 4
    return jax.shard_map(body, mesh=mesh, in_specs=in_specs, out_specs=out_specs, check_vma=False)
```

```python
import jax
import jax.numpy as jnp
from jax import lax
from jax.experimental import pallas as pl
from jax.experimental.pallas import tpu as pltpu
from jax.sharding import Mesh, PartitionSpec as P

norm_epsilon = 1e-05
beta_one = 0.9
beta_two = 0.99
adam_epsilon = 1e-08
step_count = 10
rate_main = 0.0006
rate_time = 0.0012
weight_decay = 0.1

RB = 2
COST = 20
VMEM = 63 * 1024 * 1024
F32, BF16 = jnp.float32, jnp.bfloat16


def dot_nn(a, b):
    return lax.dot_general(a, b, (((1,), (0,)), ((), ())), preferred_element_type=F32)


def dot_nt(a, b):
    return lax.dot_general(a, b, (((1,), (1,)), ((), ())), preferred_element_type=F32)


def dot_tn(a, b):
    return lax.dot_general(a, b, (((0,), (0,)), ((), ())), preferred_element_type=F32)


def colsum(a):
    return jnp.sum(a, axis=0, keepdims=True)


LANES = 128


def columns(D):
    return [slice(j, j + LANES) for j in range(0, D, LANES)]


def place_of(starts_ref, base_ref, row, T):
    local = lax.broadcasted_iota(jnp.int32, (T, LANES), 0)
    base = base_ref[0]
    begin = jnp.zeros((T, LANES), jnp.int32)
    last_begin = jnp.int32(0)
    for j in range(starts_ref.shape[1]):
        s = starts_ref[row, j]
        begin = jnp.where(local + base >= s, jnp.maximum(begin, s), begin)
        last_begin = jnp.where(base + T - 1 >= s, jnp.maximum(last_begin, s), last_begin)
    dist = local + base - begin
    tail = (local + base >= last_begin).astype(F32)
    return local, dist, tail


def levels(T):
    k = 1
    while k < T:
        yield k
        k *= 2


def keeps_of(local, dist, T):
    return [((dist >= k) & (local >= k)).astype(F32) for k in levels(T)]


def lane_mean(total, D):
    return jnp.broadcast_to(jnp.sum(total, axis=-1, keepdims=True) * (1.0 / D), total.shape)


def norm_stats(x, rows, D):
    mean = lane_mean(sum(x[rows, c].astype(F32) for c in columns(D)), D)
    spread = [x[rows, c].astype(F32) - mean for c in columns(D)]
    rstd = lax.rsqrt(lane_mean(sum(s * s for s in spread), D) + norm_epsilon)
    return mean, rstd


def norm_rows(x, gain, bias):
    centred = x - jnp.mean(x, axis=-1, keepdims=True)
    rstd = lax.rsqrt(jnp.mean(centred * centred, axis=-1, keepdims=True) + norm_epsilon)
    return centred * rstd * gain + bias


def previous_of(normalized, edge, local, joined):
    return jnp.where(local == 0, edge, pltpu.roll(normalized, 1, 0)) * joined


def mixed(x, rows, c, stats, vec, gain_row, edge, local, joined):
    mean, rstd = stats
    normalized = (x[rows, c].astype(F32) - mean) * rstd * vec[gain_row : gain_row + 1, c]
    normalized = normalized + vec[gain_row + 1 : gain_row + 2, c]
    previous = previous_of(normalized, edge, local, joined)
    return previous, normalized - previous


def shift_up(masked, local, T):
    return jnp.where(local == T - 1, 0.0, pltpu.roll(masked, T - 1, 0))


def scan_down(pair, rate, keeps, T):
    for k, keep in zip(levels(T), keeps):
        weight = keep * jnp.exp(-float(k) * rate)
        pair = tuple(a + weight * pltpu.roll(a, k, 0) for a in pair)
    return pair


def scan_up(pair, rate, keeps, T):
    for k, keep in zip(levels(T), keeps):
        weight = keep * jnp.exp(-float(k) * rate)
        pair = tuple(a + pltpu.roll(weight * a, T - k, 0) for a in pair)
    return pair


def piece_copies(base, pieces, item, target, sems, at):
    count, first_in_block, first, width, rows, bits = item
    columns = pl.ds(first, width)
    if count == 1:
        return [(0, pltpu.make_async_copy(pieces[0].at[:, pl.ds(first_in_block, width)], target, sems.at[at]))]
    block, one, two, other_one, other_two = pieces
    d, c = base[1], base[2]
    copies = []
    for half, first_ref, second_ref in ((c, one, two), (1 - c, other_one, other_two)):
        start = pl.multiple_of(half * rows, rows)
        for source, m in (
            (block.at[pl.ds(start, rows), pl.ds(first_in_block, width)], 0),
            (first_ref.at[:, columns], bits[0]),
            (second_ref.at[0, :, columns], bits[1]),
            (second_ref.at[1, :, columns], bits[0] | bits[1]),
        ):
            row = pl.multiple_of(((d ^ m) * 2 + half) * rows, rows)
            copies.append(
                (m, pltpu.make_async_copy(
                    source, target.at[pl.ds(row, rows)], sems.at[at + len(copies)]
                ))
            )
    return copies


def split_refs(items, refs):
    groups, at = [], 0
    for count in items:
        groups.append(refs[at : at + count])
        at += count
    return groups, refs[at:]


def k_time_in(items, T, starts, base, x, edge, vec, *refs):
    (pieces,), (mk, mv, mr, ko, vo, ro, no, do, last, w, sems) = split_refs([items[0][0]], refs)
    D = x.shape[1]
    i = pl.program_id(0)
    copies = [
        copy
        for s, item in enumerate(items)
        for copy in piece_copies(base, pieces, item, w.at[s], sems, 8 * s)
    ]

    @pl.when(i == 0)
    def _():
        for _, copy in copies:
            copy.start()

    edge_norm = norm_rows(edge[0], vec[0:1], vec[1:2])
    places = [place_of(starts, base, i * RB + q, T) for q in range(RB)]
    for q, (local, dist, _) in enumerate(places):
        rows = slice(q * T, q * T + T)
        joined = (dist >= 1).astype(F32)
        stats = norm_stats(x, rows, D)
        for c in columns(D):
            previous, change = mixed(
                x, rows, c, stats, vec, 0, edge_norm[q : q + 1, c], local, joined
            )
            for j, out in ((2, mk), (3, mv), (4, mr)):
                out[rows, c] = (previous + change * vec[j : j + 1, c]).astype(BF16)

    @pl.when(i == 0)
    def _():
        for _, copy in copies:
            copy.wait()

    ko[...] = dot_nn(mk[...], w[0])
    vo[...] = dot_nn(mv[...], w[1]).astype(vo.dtype)
    ro[...] = dot_nn(mr[...], w[2]).astype(ro.dtype)
    for q, (local, dist, _) in enumerate(places):
        rows = slice(q * T, q * T + T)
        keeps = keeps_of(local, dist, T)
        for c in columns(D):
            rate = jnp.exp(vec[5:6, c])
            weight = jnp.exp(ko[rows, c])
            sums = scan_down((weight * vo[rows, c].astype(F32), weight), rate, keeps, T)
            for side, (out, total) in enumerate(zip((no, do), sums)):
                out[rows, c] = (keeps[0] * pltpu.roll(total, 1, 0)).astype(out.dtype)
                last[q, side : side + 1, c] = total[T - 1 : T]


def decay_state(vec, c, key, value, num, den, state, local, dist):
    rate = jnp.exp(vec[5:6, c])
    fade = (dist >= local + 1).astype(F32) * jnp.exp(-local.astype(F32) * rate)
    full_n = num.astype(F32) + fade * state[0:1]
    full_d = den.astype(F32) + fade * state[1:2]
    extra = jnp.exp(vec[6:7, c] + key)
    inverse = 1.0 / (full_d + extra)
    mean = (full_n + extra * value) * inverse
    return full_n, full_d, extra, inverse, mean


def k_time_out(items, T, starts, base, x, key, value, recept, num, den, state, vec, *refs):
    (pieces,), (gated, middle, w, sems) = split_refs([items[0][0]], refs)
    D = x.shape[1]
    i = pl.program_id(0)
    copies = piece_copies(base, pieces, items[0], w, sems, 0)

    @pl.when(i == 0)
    def _():
        for _, copy in copies:
            copy.start()

    for q in range(RB):
        local, dist, _ = place_of(starts, base, i * RB + q, T)
        rows = slice(q * T, q * T + T)
        for c in columns(D):
            mean = decay_state(
                vec, c, key[rows, c], value[rows, c].astype(F32), num[rows, c], den[rows, c], state[q, :, c],
                local, dist,
            )[4]
            gated[rows, c] = (jax.nn.sigmoid(recept[rows, c].astype(F32)) * mean).astype(BF16)

    @pl.when(i == 0)
    def _():
        for _, copy in copies:
            copy.wait()

    middle[...] = x[...].astype(F32) + dot_nn(gated[...], w[...])


def feed_copies(items, base, pieces, wg, wk, wv, sems):
    items = items[1:]

    def copies(index, target, at):
        group, item = items[index]
        return piece_copies(base, pieces[group], item, target, sems, at)

    blocks = (len(items) - 1) // 2
    pairs = [
        copies(1 + b, wk.at[b], 8 + 16 * b) + copies(1 + blocks + b, wv.at[b], 16 + 16 * b)
        for b in range(blocks)
    ]
    return copies(0, wg, 0), pairs


def feed_start(copies):
    gate, pairs = copies
    for _, copy in [z for block in pairs for z in block] + gate:
        copy.start()


def feed_wait(copies, j):
    for b, block in enumerate(copies[1]):

        @pl.when(j == b)
        def _():
            for _, copy in block:
                copy.wait()


def k_feed(items, T, starts, base, middle, edge, vec, *refs):
    pieces, (fm, gm, sp, hid, vb, gl, xo, acc, wg, wk, wv, sems) = split_refs(items[0], refs)
    M, D = middle.shape
    j = pl.program_id(0)
    copies = feed_copies(items, base, pieces, wg, wk, wv, sems)

    @pl.when(j == 0)
    def _():
        feed_start(copies)
        edge_norm = norm_rows(edge[...], vec[7:8], vec[8:9])
        for q in range(M // T):
            local, dist, _ = place_of(starts, base, q, T)
            rows = slice(q * T, q * T + T)
            joined = (dist >= 1).astype(F32)
            stats = norm_stats(middle, rows, D)
            for c in columns(D):
                previous, change = mixed(
                    middle, rows, c, stats, vec, 7, edge_norm[q : q + 1, c], local, joined
                )
                fm[rows, c] = (previous + change * vec[9:10, c]).astype(BF16)
                gm[rows, c] = (previous + change * vec[10:11, c]).astype(BF16)
        acc[...] = jnp.zeros_like(acc)

    feed_wait(copies, j)
    pre = dot_nn(fm[...], wk[j])
    soft = jnp.maximum(pre, 0.0) + jnp.log(1.0 + jnp.exp(-jnp.abs(pre)))
    sp[...] = soft.astype(BF16)
    hidden = (soft * soft).astype(BF16)
    hid[...] = hidden
    acc[...] += dot_nn(hidden, wv[j])

    @pl.when(j == pl.num_programs(0) - 1)
    def _():
        for _, copy in copies[0]:
            copy.wait()
        gate = dot_nn(gm[...], wg[...])
        gl[...] = gate.astype(BF16)
        vb[...] = acc[...].astype(BF16)
        xo[...] = middle[...] + jax.nn.sigmoid(gate) * acc[...]


def k_feed_back(items, T, starts, base, grad, gl, vb, sp, middle, edge, vec, *refs):
    pieces, (gb, gg, gin, gn, first, sums, acc, gc, wg, wk, wv, sems) = split_refs(
        items[0], refs
    )
    M, D = middle.shape
    j = pl.program_id(0)
    copies = feed_copies(items, base, pieces, wg, wk, wv, sems)

    @pl.when(j == 0)
    def _():
        feed_start(copies)
        g = grad[...].astype(F32)
        s = jax.nn.sigmoid(gl[...].astype(F32))
        gb[...] = (g * s).astype(BF16)
        gg[...] = (g * vb[...].astype(F32) * s * (1.0 - s)).astype(BF16)
        acc[...] = jnp.zeros_like(acc)

    feed_wait(copies, j)
    soft = sp[...].astype(F32)
    gh = dot_nt(gb[...], wv[j])
    pre = (gh * (2.0 * soft * (1.0 - jnp.exp(-soft)))).astype(BF16)
    gin[...] = pre
    acc[...] += dot_nt(pre, wk[j])

    @pl.when(j == pl.num_programs(0) - 1)
    def _():
        for _, copy in copies[0]:
            copy.wait()
        gc[...] = dot_nt(gg[...], wg[...])
        edge_norm = norm_rows(edge[...], vec[7:8], vec[8:9])
        sums[...] = jnp.zeros_like(sums)
        for q in range(M // T):
            local, dist, _ = place_of(starts, base, q, T)
            rows = slice(q * T, q * T + T)
            joined = (dist >= 1).astype(F32)
            stats = norm_stats(middle, rows, D)
            for c in columns(D):
                _, change = mixed(
                    middle, rows, c, stats, vec, 7, edge_norm[q : q + 1, c], local, joined
                )
                ga, gb_ = acc[rows, c], gc[rows, c]
                sums[0:1, c] += colsum(ga * change)
                sums[1:2, c] += colsum(gb_ * change)
                direct = ga * vec[9:10, c] + gb_ * vec[10:11, c]
                masked = (ga + gb_ - direct) * joined
                gn[rows, c] = (direct + shift_up(masked, local, T)).astype(gn.dtype)
                first[q : q + 1, c] = masked[0:1]


def norm_back(x, rows, gain_row, vec, total, sums, D, put):
    mean, rstd = norm_stats(x, rows, D)
    one = two = None
    for c in columns(D):
        hat = (x[rows, c].astype(F32) - mean) * rstd
        g = total(c)
        scaled = g * vec[gain_row : gain_row + 1, c]
        sums[0:1, c] += colsum(g * hat)
        sums[1:2, c] += colsum(g)
        one = scaled if one is None else one + scaled
        two = scaled * hat if two is None else two + scaled * hat
    one, two = lane_mean(one, D), lane_mean(two, D)
    for c in columns(D):
        hat = (x[rows, c].astype(F32) - mean) * rstd
        put(c, rstd * (total(c) * vec[gain_row : gain_row + 1, c] - one - hat * two))


def with_edge(gn, rows, edge, local, T):
    return lambda c: gn[rows, c].astype(F32) + jnp.where(local == T - 1, edge[:, c], 0.0)


def k_mid_back(items, T, starts, base, gn, edge, middle, grad, vec,
               key, value, recept, num, den, state, *refs):
    (pieces,), rest = split_refs([items[0][0]], refs)
    gm, gblk, gr, gkp, gvp, gno, gdo, direct, sums, ggated, w, sems = rest
    D = middle.shape[1]
    i = pl.program_id(0)
    copies = piece_copies(base, pieces, items[0], w, sems, 0)

    @pl.when(i == 0)
    def _():
        for _, copy in copies:
            copy.start()
        sums[...] = jnp.zeros_like(sums)

    places = [place_of(starts, base, i * RB + q, T) for q in range(RB)]
    for q, (local, dist, _) in enumerate(places):
        rows = slice(q * T, q * T + T)

        def put(c, gx):
            gmid = grad[rows, c].astype(F32) + gx
            gm[rows, c] = gmid
            gblk[rows, c] = gmid.astype(BF16)

        total = with_edge(gn, rows, edge[0, q : q + 1], local, T)
        norm_back(middle, rows, 7, vec, total, sums, D, put)

    @pl.when(i == 0)
    def _():
        for _, copy in copies:
            copy.wait()

    ggated[...] = dot_nt(gblk[...], w[...])
    for q, (local, dist, _) in enumerate(places):
        rows = slice(q * T, q * T + T)
        joined = (dist >= 1).astype(F32)
        keeps = keeps_of(local, dist, T)
        for c in columns(D):
            v, g = value[rows, c].astype(F32), ggated[rows, c]
            _, _, extra, inverse, mean = decay_state(
                vec, c, key[rows, c], v, num[rows, c], den[rows, c], state[q, :, c], local, dist
            )
            s = jax.nn.sigmoid(recept[rows, c].astype(F32))
            gr[rows, c] = (g * mean * s * (1.0 - s)).astype(BF16)
            r = g * s * inverse
            ge = extra * r * (v - mean)
            gkp[rows, c] = ge.astype(gkp.dtype)
            gvp[rows, c] = (r * extra).astype(gvp.dtype)
            sums[2:3, c] += colsum(ge)
            rate = jnp.exp(vec[5:6, c])
            totals = scan_up((r, -r * mean), rate, keeps, T)
            for side, (out, a) in enumerate(zip((gno, gdo), totals)):
                out[rows, c] = pltpu.roll(keeps[0] * a, T - 1, 0).astype(out.dtype)
                direct[q, side : side + 1, c] = (joined * a)[0:1]


def k_time_back(items, T, starts, base, x, edge, vec, key, value, num, den, state,
                gkp, gvp, gno, gdo, after, gr, *refs):
    (pieces,), (gk, gv, gn, first, sums, mixes, w, sems) = split_refs([items[0][0]], refs)
    D = x.shape[1]
    i = pl.program_id(0)
    copies = [
        copy
        for s, item in enumerate(items)
        for copy in piece_copies(base, pieces, item, w.at[s], sems, 8 * s)
    ]

    @pl.when(i == 0)
    def _():
        for _, copy in copies:
            copy.start()
        sums[...] = jnp.zeros_like(sums)

    places = [place_of(starts, base, i * RB + q, T) for q in range(RB)]
    for q, (local, dist, tail) in enumerate(places):
        rows = slice(q * T, q * T + T)
        inside = (dist >= local + 1).astype(F32)
        for c in columns(D):
            rate = jnp.exp(vec[5:6, c])
            fade = inside * jnp.exp(-local.astype(F32) * rate)
            full_n = num[rows, c].astype(F32) + fade * state[q, 0:1, c]
            full_d = den[rows, c].astype(F32) + fade * state[q, 1:2, c]
            left = tail * jnp.exp(-(T - 1 - local).astype(F32) * rate)
            grad_n = gno[rows, c].astype(F32) + left * after[q, 0:1, c]
            grad_d = gdo[rows, c].astype(F32) + left * after[q, 1:2, c]
            weight = jnp.exp(key[rows, c])
            gk[rows, c] = (
                gkp[rows, c].astype(F32) + weight * (grad_n * value[rows, c].astype(F32) + grad_d)
            ).astype(BF16)
            gv[rows, c] = (gvp[rows, c].astype(F32) + weight * grad_n).astype(BF16)
            turn = colsum(grad_n * full_n + grad_d * full_d)
            sums[3:4, c] += -rate * jnp.exp(-rate) * turn

    @pl.when(i == 0)
    def _():
        for _, copy in copies:
            copy.wait()

    for s, g in enumerate((gk, gv, gr)):
        mixes[s] = dot_nt(g[...], w[s])
    edge_norm = norm_rows(edge[0], vec[0:1], vec[1:2])
    for q, (local, dist, _) in enumerate(places):
        rows = slice(q * T, q * T + T)
        joined = (dist >= 1).astype(F32)
        stats = norm_stats(x, rows, D)
        for c in columns(D):
            _, change = mixed(x, rows, c, stats, vec, 0, edge_norm[q : q + 1, c], local, joined)
            gs = [mixes[s, rows, c] for s in range(3)]
            for s in range(3):
                sums[s : s + 1, c] += colsum(gs[s] * change)
            direct = sum(g * vec[2 + s : 3 + s, c] for s, g in enumerate(gs))
            masked = (gs[0] + gs[1] + gs[2] - direct) * joined
            gn[rows, c] = (direct + shift_up(masked, local, T)).astype(gn.dtype)
            first[0, q : q + 1, c] = masked[0:1]


def k_norm_back(T, x, gn, edge, gmid, vec, go, sums):
    i = pl.program_id(0)
    D = x.shape[1]

    @pl.when(i == 0)
    def _():
        sums[...] = jnp.zeros_like(sums)

    local = lax.broadcasted_iota(jnp.int32, (T, LANES), 0)
    for q in range(RB):
        rows = slice(q * T, q * T + T)

        def put(c, gx):
            go[rows, c] = gmid[rows, c] + gx

        total = with_edge(gn, rows, edge[0, q : q + 1], local, T)
        norm_back(x, rows, 0, vec, total, sums, D, put)


def put_halves(base, product, n, mine, send):
    pairs = product.shape[0] // (2 * n)
    lead, Z = mine.shape[0], mine.shape[1]
    for p in range(pairs):
        for out, half in ((mine, base[2]), (send, 1 - base[2])):
            start = pl.multiple_of((2 * p + half) * n, 8)
            out[p // Z, p % Z, 0] = product[pl.ds(start, n), :].astype(BF16)


def k_halves_apart(n, count, T, starts, base, *refs):
    lefts, grads, rest = refs[:count], refs[count : 2 * count], refs[2 * count :]
    mine, send, left, grad, product, sems = rest
    i = pl.program_id(0)
    pairs = [
        [
            pltpu.make_async_copy(source, target.at[k], sems.at[2 * k + side])
            for side, (source, target) in enumerate(((lefts[k], left), (grads[k], grad)))
        ]
        for k in range(count)
    ]

    @pl.when(i == 0)
    def _():
        for pair in pairs:
            for copy in pair:
                copy.start()

    for k, pair in enumerate(pairs):

        @pl.when(i == k)
        def _():
            for copy in pair:
                copy.wait()

    product[...] = dot_tn(left[i], grad[i])
    put_halves(base, product, n, mine, send)


def k_halves_blocks(n, T, starts, base, left, grad, mine, send, product):
    product[...] = dot_tn(left[...], grad[...])
    put_halves(base, product, n, mine, send)


def k_flat(T, fm, gin, hid, gb, out):
    i = pl.program_id(0)
    half = pl.num_programs(0) // 2

    @pl.when(i < half)
    def _():
        out[...] = dot_tn(fm[...], gin[...]).astype(BF16)

    @pl.when(i >= half)
    def _():
        out[...] = dot_tn(hid[...], gb[...]).astype(BF16)


def smem():
    return pl.BlockSpec(memory_space=pltpu.SMEM)


def rows_spec(T, D):
    return pl.BlockSpec((RB * T, D), lambda i: (i, 0))


def col_spec(rows, width, at):
    return pl.BlockSpec((rows, width), lambda i: (0, at))


def whole_spec(shape):
    zeros = (0,) * len(shape)
    return pl.BlockSpec(shape, lambda i: zeros)


def edge_spec(D):
    return pl.BlockSpec((1, RB, D), lambda i: (i, 0, 0))


def state_spec(D):
    return pl.BlockSpec((RB, 2, D), lambda i: (i, 0, 0))


def shape(dims, kind):
    return jax.ShapeDtypeStruct(dims, kind)


def run(kernel, T, grid, in_specs, out_specs, outs, args, flops, moved, scratch=(), items=(),
        after=()):
    count = len(args)
    in_specs = in_specs + anywhere(len(after))
    args = args + tuple(after)

    def body(*refs):
        kernel(*(items if isinstance(items, tuple) else (items,) if items else ()), T, *refs[:count], *refs[count + len(after) :])

    return pl.pallas_call(
        body,
        grid=(grid,),
        in_specs=in_specs,
        out_specs=out_specs,
        out_shape=outs,
        scratch_shapes=scratch,
        compiler_params=pltpu.CompilerParams(
            dimension_semantics=("arbitrary",), vmem_limit_bytes=VMEM
        ),
        cost_estimate=pl.CostEstimate(
            flops=flops // COST, bytes_accessed=moved // COST, transcendentals=0
        ),
        name=kernel.__name__,
    )(*args)


def anywhere(count):
    return [pl.BlockSpec(memory_space=pl.ANY)] * count


def weight_room(shapes, copies):
    return [pltpu.VMEM(s, BF16) for s in shapes] + [pltpu.SemaphoreType.DMA((copies,))]


def time_in(T, place, x, edge, vec, weights, after=()):
    N, D = x.shape
    R = N // T
    rs = rows_spec(T, D)
    pieces = weights["key"][0]
    items = [weights[name][1] for name in ("key", "value", "recept")]
    return run(
        k_time_in, T, R // RB,
        [smem(), smem(), rs, edge_spec(D), whole_spec(vec.shape)] + anywhere(len(pieces)),
        [rs] * 8 + [state_spec(D)],
        [shape((N, D), BF16)] * 3 + [shape((N, D), F32)] + [shape((N, D), BF16)] * 4
        + [shape((R, 2, D), F32)],
        (*place, x, edge.reshape(R // RB, RB, D), vec, *pieces),
        6 * N * D * D, 40 * N * D,
        weight_room([(3, D, D)], 24), items, after,
    )


def time_out(T, place, x, kept, state, vec, weights, after=()):
    N, D = x.shape
    R = N // T
    rs = rows_spec(T, D)
    pieces, item = weights["output"]
    return run(
        k_time_out, T, R // RB,
        [smem(), smem()] + [rs] * 6 + [state_spec(D), whole_spec(vec.shape)] + anywhere(len(pieces)),
        [rs] * 2,
        [shape((N, D), BF16), shape((N, D), F32)],
        (*place, x, *kept, state, vec, *pieces),
        2 * N * D * D, 30 * N * D,
        weight_room([(D, D)], 8), [item], after,
    )


def feed_weights(weights):
    keys, values = (
        sorted(name for name in weights if name.startswith(kind)) for kind in ("feed_key", "feed_value")
    )
    groups, items = [], []
    for name in ["gate"] + keys + values:
        pieces, item = weights[name]
        found = [k for k, group in enumerate(groups) if group is pieces]
        if not found:
            found = [len(groups)]
            groups.append(pieces)
        items.append((found[0], item))
    pieces = tuple(piece for group in groups for piece in group)
    return [[len(group) for group in groups]] + items, pieces


def feed(T, place, middle, edge, vec, weights, after=()):
    N, D = middle.shape
    items, pieces = feed_weights(weights)
    B = (len(items) - 2) // 2
    F = B * D
    whole = whole_spec((N, D))
    wide_spec = pl.BlockSpec((N, D), lambda j: (0, j))
    return run(
        k_feed, T, B,
        [smem(), smem(), whole, whole_spec(edge.shape), whole_spec(vec.shape)] + anywhere(len(pieces)),
        [whole, whole, wide_spec, wide_spec, whole, whole, whole],
        [shape((N, D), BF16)] * 2 + [shape((N, F), BF16)] * 2 + [shape((N, D), BF16)] * 2
        + [shape((N, D), F32)],
        (*place, middle, edge, vec, *pieces),
        4 * N * D * F + 2 * N * D * D, 20 * N * D + 4 * N * F + 4 * D * F,
        [pltpu.VMEM((N, D), F32)]
        + weight_room([(D, D), (B, D, D), (B, D, D)], 8 * len(items)), items, after,
    )


def feed_back(T, place, grad, gl, vb, sp, middle, edge, vec, weights, after=()):
    N, D = middle.shape
    items, pieces = feed_weights(weights)
    B = (len(items) - 2) // 2
    F = B * D
    R = N // T
    whole = whole_spec((N, D))
    wide_spec = pl.BlockSpec((N, D), lambda j: (0, j))
    return run(
        k_feed_back, T, B,
        [smem(), smem(), whole, whole, whole, wide_spec, whole, whole_spec(edge.shape),
         whole_spec(vec.shape)] + anywhere(len(pieces)),
        [whole, whole, wide_spec, whole, whole_spec((R, D)), whole_spec((8, D))],
        [shape((N, D), BF16)] * 2 + [shape((N, F), BF16), shape((N, D), BF16)]
        + [shape((R, D), F32), shape((8, D), F32)],
        (*place, grad, gl, vb, sp, middle, edge, vec, *pieces),
        4 * N * D * F + 2 * N * D * D, 20 * N * D + 4 * N * F + 4 * D * F,
        [pltpu.VMEM((N, D), F32)] * 2
        + weight_room([(D, D), (B, D, D), (B, D, D)], 8 * len(items)), items, after,
    )


def mid_back(T, place, gn, edge, middle, grad, vec, weights, kept, state, after=()):
    N, D = middle.shape
    R = N // T
    rs = rows_spec(T, D)
    pieces, item = weights["output"]
    return run(
        k_mid_back, T, R // RB,
        [smem(), smem(), rs, edge_spec(D), rs, rs, whole_spec(vec.shape)]
        + [rs] * 5 + [state_spec(D)] + anywhere(len(pieces)),
        [rs] * 7 + [state_spec(D), whole_spec((8, D))],
        [shape((N, D), F32)] + [shape((N, D), BF16)] * 6
        + [shape((R, 2, D), F32), shape((8, D), F32)],
        (*place, gn, edge.reshape(R // RB, RB, D), middle, grad, vec, *kept, state, *pieces),
        2 * N * D * D, 50 * N * D,
        [pltpu.VMEM((RB * T, D), F32)] + weight_room([(D, D)], 8), [item], after,
    )


def time_back(T, place, x, edge, vec, weights, kept, state, part, later, gr, after=()):
    N, D = x.shape
    R = N // T
    rs = rows_spec(T, D)
    pieces = weights["key"][0]
    items = [weights[name][1] for name in ("key", "value", "recept")]
    return run(
        k_time_back, T, R // RB,
        [smem(), smem(), rs, edge_spec(D), whole_spec(vec.shape)]
        + [rs] * 4 + [state_spec(D)] + [rs] * 4 + [state_spec(D), rs] + anywhere(len(pieces)),
        [rs] * 3 + [edge_spec(D), whole_spec((8, D))],
        [shape((N, D), BF16)] * 3
        + [shape((R // RB, RB, D), F32), shape((8, D), F32)],
        (*place, x, edge.reshape(R // RB, RB, D), vec, *kept, state, *part, later, gr, *pieces),
        6 * N * D * D, 50 * N * D,
        [pltpu.VMEM((3, RB * T, D), F32)] + weight_room([(3, D, D)], 24), items, after,
    )


def norm_in_back(T, x, gn, edge, gmid, vec, after=()):
    N, D = x.shape
    R = N // T
    rs = rows_spec(T, D)
    return run(
        k_norm_back, T, R // RB,
        [rs, rs, edge_spec(D), rs, whole_spec(vec.shape)],
        [rs, whole_spec((8, D))],
        [shape((N, D), F32), shape((8, D), F32)],
        (x, gn, edge.reshape(R // RB, RB, D), gmid, vec),
        0, 16 * N * D, after=after,
    )


SEQ = ("z", "c")
AXES = ("dp", "z", "c")
SWAP = [(0, 1), (1, 0)]


def by_bit(block, bit):
    return lax.ppermute(block, "dp", [(i, i ^ bit) for i in range(lax.axis_size("dp"))])


def after(value, *others):
    return lax.optimization_barrier((value, *others))[0]


def gather_seq(part, *gate):
    return lax.all_gather(after(part, *gate), SEQ, axis=0, tiled=True)


class Gathered:
    def __init__(self, part, names, *gate):
        self.block = lax.all_gather(after(part, *gate), AXES, axis=0, tiled=True)
        self.names = names

    def weights(self):
        pieces, at, found = (self.block,), 0, {}
        for name, width in self.names:
            found[name] = (pieces, (1, at, 0, width, 0, (0, 0)))
            at += width
        return found


class Exchange:
    def __init__(self, block, names, start, bits):
        self.block, self.names, self.start, self.bits = block, names, start, bits
        self.width = sum(width for _, width in names)
        self.rows = block.shape[0] // 2

    def first(self, *gate):
        block = after(self.block, *gate)
        self.own = lax.dynamic_slice(
            block, (lax.axis_index("c") * self.rows, self.start), (self.rows, self.width)
        )
        self.one = by_bit(self.own, self.bits[0])
        return self.one

    def second(self, *gate):
        one = after(self.one, *gate)
        self.two = by_bit(jnp.stack([self.own, one]), self.bits[1])
        return self.two

    def cores(self, *gate):
        self.one, self.two = after((self.one, self.two), *gate)
        self.other_one = lax.ppermute(self.one, "c", SWAP)
        self.other_two = lax.ppermute(self.two, "c", SWAP)

    def weights(self):
        if not hasattr(self, "pieces"):
            self.pieces = (self.block, self.one, self.two, self.other_one, self.other_two)
        pieces, at, found = self.pieces, 0, {}
        for name, width in self.names:
            found[name] = (pieces, (5, self.start + at, at, width, self.rows, self.bits))
            at += width
        return found


class Scatter:
    def __init__(self, mine, send, bits):
        self.mine, self.send, self.bits = mine, send, bits

    def part(self, a, y, x):
        if y is not None:
            a = lax.dynamic_index_in_dim(a, y, 0, keepdims=True)
        if x is not None:
            a = lax.dynamic_index_in_dim(a, x, 1, keepdims=True)
        return a.astype(F32)

    def cores(self, *gate):
        self.received = lax.ppermute(after(self.send, *gate), "c", SWAP)
        return self.received

    def first(self, *gate):
        d = lax.axis_index("dp")
        y, x = d // 2, d % 2
        terms = after((self.mine, self.received), *gate)
        place = (1 - y, None) if self.bits[1] == 2 else (None, 1 - x)
        self.got = by_bit(sum(self.part(a, *place) for a in terms).astype(BF16), self.bits[1])
        return self.got

    def second(self, *gate):
        d = lax.axis_index("dp")
        y, x = d // 2, d % 2
        terms = after((self.mine, self.received, self.got), *gate)

        def total(y, x):
            got = self.part(terms[2], *((None, x) if self.bits[1] == 2 else (y, None)))
            return self.part(terms[0], y, x) + self.part(terms[1], y, x) + got

        there = (y, 1 - x) if self.bits[1] == 2 else (1 - y, x)
        self.two = by_bit(total(*there).astype(BF16), self.bits[0])
        self.keep = lambda two: (total(y, x) + two.astype(F32)).astype(BF16)
        return self.two


def finish(scatters, *gate):
    parts, shapes = [], []
    width = max(s.mine.shape[-1] for s in scatters)
    for scatter in scatters:
        total = scatter.keep(after(scatter.two, *gate))[0, 0]
        Z, I, n, C = total.shape
        if C < width:
            total = jnp.pad(total, ((0, 0), (0, 0), (0, 0), (0, width - C)))
        parts.append(total.reshape(Z, I * n, width))
        shapes.append((I, n, C))
    whole = jnp.concatenate(parts, axis=1)
    out = lax.psum_scatter(
        whole.reshape(-1, whole.shape[2]), "z", scatter_dimension=0, tiled=True
    )
    at = 0
    for scatter, (I, n, C) in zip(scatters, shapes):
        scatter.out = out[at : at + I * n, :C].reshape(I, n, C).astype(F32)
        at += I * n
    return out, whole


def from_behind(block, distance):
    devices = range(lax.axis_size(SEQ))
    route = [(i - distance, i) for i in devices if i - distance in devices]
    return lax.ppermute(block, SEQ, route)


def chain(mine, starts, rate, T, forward):
    S, i = lax.axis_size(SEQ), lax.axis_index(SEQ)
    all_states = lax.all_gather(mine.astype(BF16), SEQ).astype(F32)
    j = jnp.arange(S, dtype=jnp.int32)

    def document(at):
        return jnp.sum((starts[None] <= at[:, None, None]).astype(jnp.int32), axis=2)

    if forward:
        lag = i - 1 - j
        same = document((j + 1) * T - 1) == document((i * T - 1)[None])
    else:
        lag = j - 1 - i
        same = document(j * T - 1) == document(((i + 1) * T - 1)[None])
    keep = (same & (lag >= 0)[:, None]).astype(F32)
    fade = jnp.exp(-(T * jnp.maximum(lag, 0)).astype(F32)[:, None] * rate[None])
    weight = keep[:, :, None, None] * fade[:, None, None, :]
    return jnp.sum(weight * all_states, axis=0)


def layer_forward(T, place, starts, x, edge, vec, weights, hook):
    N, D = x.shape
    R = N // T
    rate = jnp.exp(vec[5])
    x = hook("start", x)
    mk, mv, mr, key, value, recept, num, den, last = time_in(T, place, x, edge, vec, weights())
    last = hook("time in", last)
    state = chain(last, starts, rate, T, True)
    state = hook("chain", state)
    gated, middle = time_out(T, place, x, (key, value, recept, num, den), state, vec, weights())
    middle = hook("time out", middle)
    edge_two = from_behind(middle.reshape(R, T, D)[:, -1], 1)
    edge_two = hook("edge", edge_two)
    fm, gm, sp, hid, vb, gl, out = feed(T, place, middle, edge_two, vec, weights())
    out = hook("feed", out)
    saved = (x, edge, mk, mv, mr, key, value, recept, num, den, state, gated, middle, edge_two,
             fm, gm, sp, hid, vb, gl)
    return out, saved


def weight_halves(place, lefts, grads, n, kind):
    N = lefts[0].shape[0]
    D = grads[0].shape[1] if kind == "lefts" else lefts[0].shape[1]
    Z = lax.axis_size("z")
    if kind == "apart":
        count = len(lefts)
    else:
        count = (lefts[0] if kind == "lefts" else grads[0]).shape[1] // D
    if n % 8:
        if kind == "lefts":
            lefts, grads = [lefts[0][:, k * D : (k + 1) * D] for k in range(count)], grads * count
        elif kind == "grads":
            lefts, grads = lefts * count, [grads[0][:, k * D : (k + 1) * D] for k in range(count)]
        products = [
            lax.dot_general(a, b, (((0,), (0,)), ((), ())), preferred_element_type=F32).astype(BF16)
            for a, b in zip(lefts, grads)
        ]
        whole = jnp.stack([p.reshape(2, 2, Z, 2, n, D) for p in products], axis=3)
        c = lax.axis_index("c")
        return tuple(
            lax.dynamic_index_in_dim(whole, which, 4, keepdims=False) for which in (c, 1 - c)
        )
    out = pl.BlockSpec((4, Z, 1, n, D), lambda i: (0, 0, i, 0, 0))
    outs = [shape((4, Z, count, n, D), BF16)] * 2
    cost = (2 * count * N * D * D, 2 * count * (2 * N * D + D * D))
    room = [pltpu.VMEM((D, D), F32)]
    if kind == "apart":
        halves = run(
            k_halves_apart, 0, count, [smem(), smem()] + anywhere(2 * count), [out] * 2, outs,
            (*place, *lefts, *grads), *cost,
            [pltpu.VMEM((count, N, D), BF16)] * 2 + room + [pltpu.SemaphoreType.DMA((2 * count,))],
            (n, count),
        )
    else:
        fixed = pl.BlockSpec((N, D), lambda i: (0, 0))
        moving = pl.BlockSpec((N, D), lambda i: (0, i))
        specs = [moving, fixed] if kind == "lefts" else [fixed, moving]
        halves = run(
            k_halves_blocks, 0, count, [smem(), smem()] + specs, [out] * 2, outs,
            (*place, *lefts, *grads), *cost, room, (n,),
        )
    return tuple(a.reshape(2, 2, *a.shape[1:]) for a in halves)


def flat_grads(fm, gin, hid, gb):
    N, D = fm.shape
    B = gin.shape[1] // D
    fixed = pl.BlockSpec((N, D), lambda i: (0, 0))
    return run(
        k_flat, 0, 2 * B,
        [fixed, pl.BlockSpec((N, D), lambda i: (0, jnp.minimum(i, B - 1))),
         pl.BlockSpec((N, D), lambda i: (0, jnp.maximum(i - B, 0))), fixed],
        [pl.BlockSpec((D, D), lambda i: (0, i))], [shape((D, 2 * B * D), BF16)],
        (fm, gin, hid, gb), 4 * B * N * D * D, 4 * B * (2 * N * D + D * D),
    )[0]


def layer_backward(T, place, starts, grad, saved, vec, weights, hook):
    (x, edge, mk, mv, mr, key, value, recept, num, den, state, gated, middle, edge_two,
     fm, gm, sp, hid, vb, gl) = saved
    rate = jnp.exp(vec[5])
    outs = feed_back(T, place, grad, gl, vb, sp, middle, edge_two, vec, weights)
    gb, gg, gin, gn, first, sums_feed = hook("feed", outs)
    hook("feed grads", (hid, gb, fm, gin))
    behind = from_behind(first, -1)
    behind = hook("edge", behind)
    outs = mid_back(
        T, place, gn, behind, middle, grad, vec, weights, (key, value, recept, num, den), state
    )
    gmid, gblk, gr, gkp, gvp, gno, gdo, direct, sums_mid = hook("mid", outs)
    hook("mid grads", ((gated, gm, mr), (gblk, gg, gr)))
    direct = hook("before chain", direct)
    later = chain(direct, starts, rate, T, False)
    later = hook("chain", later)
    outs = time_back(
        T, place, x, edge, vec, weights, (key, value, num, den), state, (gkp, gvp, gno, gdo),
        later, gr,
    )
    gk, gv, gn_one, first_one, sums_time = hook("time", outs)
    hook("time grads", ((mk, mv), (gk, gv)))
    behind_one = from_behind(first_one.reshape(edge.shape), -1)
    behind_one = hook("edge two", behind_one)
    grad_in, sums_norm = norm_in_back(T, x, gn_one, behind_one, gmid, vec)
    grad_in = hook("norm", grad_in)
    return grad_in, jnp.concatenate([sums_norm, sums_time, sums_mid, sums_feed], axis=0)


VECTOR_ROWS = (0, 1, 8, 9, 10, 11, 18, 16, 17, 24, 25)


class Scattered:
    def __init__(self, product):
        out = lax.psum_scatter(product, AXES, scatter_dimension=0, tiled=True)
        self.out = out.astype(F32)


def vector_rates(row_total):
    slot = jnp.arange(row_total)
    return jnp.where((slot == 5) | (slot == 6), rate_time, rate_main)[:, None]


def adam_step(parameter, gradient, first_moment, second_moment, learning_rates, decay_weight):
    new_first = beta_one * first_moment + (1.0 - beta_one) * gradient
    new_second = beta_two * second_moment + (1.0 - beta_two) * gradient * gradient
    step_ratio = (
        new_first
        / (1.0 - beta_one**step_count)
        / (jnp.sqrt(new_second / (1.0 - beta_two**step_count)) + adam_epsilon)
    )
    return (learning_rates * (step_ratio + decay_weight * parameter), new_first, new_second)


XY, YX = (1, 2), (2, 1)


def body(tokens, cotangent, document_starts, *rest):
    weights, means, powers = rest[:5], rest[5:10], rest[10:15]
    vectors, matrices, time_output, feed_key, feed_value = weights
    R, T, D = tokens.shape
    layers, kinds, n = vectors.shape
    blocks = feed_key.shape[2] // D
    base = jnp.stack(
        [lax.axis_index(SEQ) * T, lax.axis_index("dp"), lax.axis_index("c")]
    ).astype(jnp.int32)
    place = (document_starts, base)

    def by_block(a):
        return a.reshape(n, D // n, blocks, n).transpose(0, 2, 1, 3).reshape(n, blocks * D)

    def by_device(a):
        return a.reshape(n, blocks, D // n, n).transpose(0, 2, 1, 3).reshape(n, blocks * D)

    keys = [(f"feed_key{b}", D) for b in range(blocks)]
    values = [(f"feed_value{b}", D) for b in range(blocks)]
    time_names = [("key", D), ("value", D), ("recept", D)]
    rest_names = [("output", D), ("gate", D)] + keys + values
    layout = [[time_names + [("vectors", 128)], rest_names]]
    layout += [[time_names + rest_names[:1], rest_names[1:]]] * (layers - 1)

    vector_columns = jnp.pad(
        vectors.reshape(layers * kinds, n).T, ((0, 0), (0, 128 - layers * kinds))
    )

    def shard(l, names):
        found = {
            "key": matrices[l, 0], "value": matrices[l, 1], "recept": matrices[l, 2],
            "gate": matrices[l, 3], "output": time_output[l], "vectors": vector_columns,
        }
        if ("feed_key0", D) in names:
            key_blocks = by_block(feed_key[l].astype(BF16))
            for b in range(blocks):
                found[f"feed_key{b}"] = key_blocks[:, b * D : (b + 1) * D]
                found[f"feed_value{b}"] = feed_value[l, b * n : (b + 1) * n]
        return jnp.concatenate([found[name].astype(BF16) for name, _ in names], axis=1)

    def sets_of(l, k, gate, *split):
        part = shard(l, layout[l][k])
        block = gather_seq(part, *gate)
        shards.setdefault(l, []).append(part)
        sets, at = [], 0
        for count, bits in split:
            names = layout[l][k][at : at + count]
            sets.append(Exchange(block, names, sum(w for _, w in layout[l][k][:at]), bits))
            at += count
        return sets

    def weights_of(l):
        def found():
            have = {}
            for exchange in here[l]:
                if hasattr(exchange, "other_two") or isinstance(exchange, Gathered):
                    have.update(exchange.weights())
            return have

        return found

    shards = {}
    here = [[] for _ in range(layers)]
    A = sets_of(0, 0, (), (4, XY))[0]
    O, B, V = sets_of(0, 1, (), (1, YX), (1 + blocks, XY), (blocks, YX))
    here[0] = [A, O, B, V]
    A.first()
    for l in range(1, layers):
        here[l] = sets_of(l, 0, (B.block,), (4, XY))
        here[l] += sets_of(l, 1, (here[l][0].block,), (1 + blocks, XY), (blocks, YX))
    A.second()
    O.first(A.one)
    B.first(A.one)
    A.cores(O.one, B.one, *[p for l in range(1, layers) for p in shards[l]])
    O.second(A.two)
    V.first(A.two)
    B.second(A.two)
    pieces, item = A.weights()["vectors"]
    d, c = lax.axis_index("dp"), lax.axis_index("c")
    block, one, two, other_one, other_two = (a[..., item[2] : item[2] + 128] for a in pieces)
    bits, half = item[5], item[4]
    mine = lax.dynamic_slice_in_dim(block, c * half, half, axis=0)
    other = lax.dynamic_slice_in_dim(block, (1 - c) * half, half, axis=0)
    by_m = {
        0: (mine, other), bits[0]: (one, other_one), bits[1]: (two[0], other_two[0]),
        bits[0] | bits[1]: (two[1], other_two[1]),
    }
    rel = jnp.stack([jnp.stack(by_m[m]) for m in range(4)])
    rel = jnp.where(c == 0, rel, rel[:, ::-1])
    columns = jnp.stack([lax.dynamic_index_in_dim(rel, d ^ j, 0, keepdims=False) for j in range(4)])
    spread = columns.reshape(D, 128)[:, : layers * kinds].astype(F32).T.reshape(layers, kinds, D)
    vecs = [jnp.pad(spread[l], ((0, 16 - kinds), (0, 0))) for l in range(layers)]

    def hook_of(l):
        more = l + 1 < layers

        def hook(name, value):
            if name == "start" and l > 0:
                M, U, S = here[l]
                value = after(value, M.two)
                M.cores(value)
                U.second(value)
            elif name == "time in" and l == 0:
                value = after(value, O.two, V.one)
                O.cores(value)
                V.second(value)
            elif name == "time in":
                M, U, S = here[l]
                value = after(value, S.one)
                S.second(value)
            elif name == "time out" and l == 0:
                value = after(value, V.two)
                V.cores(value)
                if more:
                    here[l + 1][0].first(value)
            elif name == "time out":
                M, U, S = here[l]
                value = after(value, S.two, U.two)
                S.cores(value)
                U.cores(value)
            elif name == "edge" and l == 0:
                value = after(value, B.two)
                B.cores(value)
                if more:
                    value = after(value, here[l + 1][0].one)
                    here[l + 1][0].second(value)
                    here[l + 1][1].first(value)
            elif name == "feed" and more:
                M, U, S = here[l + 1]
                value = after(value, U.one)
                S.first(value)
            return value

        return hook

    x = tokens.reshape(R * T, D)
    saved = []
    for l in range(layers):
        edge = from_behind(x.reshape(R, T, D)[:, -1], 1).astype(F32)
        x, kept = layer_forward(
            T, place, document_starts, x, edge, vecs[l], weights_of(l), hook_of(l)
        )
        saved.append(kept)
    block_out = x.astype(BF16).reshape(R, T, D)

    grad = cotangent.reshape(R * T, D)
    vec_grads = [None] * layers
    sums = [dict() for _ in range(layers)]

    def back_hook_of(l):
        own, last = sums[l], sums[l + 1] if l + 1 < layers else None

        def hook(name, value):
            feed = own.get("feed") if l == 0 else None
            if name == "feed" and last:
                value = after(value, last["mid"].got, last["time"].got)
                last["mid"].second(value[3])
                last["time"].second(value[3])
            elif name == "feed grads":
                hid, gb, fm, gin = value
                if l > 0:
                    own["ready"] = flat_grads(fm, gin, hid, gb)
                    own["feed"] = Scattered(own["ready"])
                else:
                    one = Scatter(*weight_halves(place, [hid], [gb], n, "lefts"), YX)
                    one.cores()
                    halves = weight_halves(place, [fm], [after(gin, one.mine)], n, "grads")
                    if last:
                        halves = after(halves, last["mid"].two, last["time"].two)
                    two = Scatter(*halves, XY)
                    two.cores()
                    own["feed"] = [one, two]
            elif name == "edge" and l > 0:
                value = after(value, own["ready"])
            elif name == "edge":
                value = after(value, *[s.received for s in feed])
                for s in feed:
                    s.first()
            elif name == "mid grads":
                halves = weight_halves(place, *value, n, "apart")
                if l == 0:
                    halves = after(halves, *[s.got for s in feed])
                own["mid"] = Scatter(*halves, YX)
                own["mid"].cores()
                if last:
                    own["gate"] = finish(
                        [last["mid"], last["time"]], last["feed"].out, own["mid"].mine
                    )[0]
                if l == 0:
                    for s in feed:
                        s.second()
            elif name == "before chain" and l == 0:
                value = after(value, own["mid"].received)
                own["mid"].first()
            elif name == "chain" and l > 0:
                value = after(value, own["mid"].received)
                own["mid"].first(value)
            elif name == "time":
                if l == 0:
                    value = after(value, own["mid"].got, *[s.two for s in feed])
                    own["gate"], whole = finish(feed, *[own["gate"]] * (layers > 1))
                    value = after(value, whole)
                    own["mid"].second(value[0])
            elif name == "time grads":
                own["time"] = Scatter(*weight_halves(place, *value, n, "apart"), XY)
                own["time"].cores()
            elif name == "edge two" and l == 0:
                value = after(value, own["time"].received)
                own["time"].first()
            elif name == "norm" and l > 0:
                value = after(value, own["time"].received)
                own["time"].first()
            return value

        return hook

    for l in reversed(range(layers)):
        grad, vec_grads[l] = layer_backward(
            T, place, document_starts, grad, saved[l], vecs[l], weights_of(l)(), back_hook_of(l)
        )
    vec_columns = jnp.concatenate(vec_grads, axis=0).astype(BF16).T
    vec_columns = jnp.pad(vec_columns, ((0, 0), (0, 128 - vec_columns.shape[1])))
    vec_view = vec_columns.reshape(2, 2, lax.axis_size("z"), 1, 2, n, 128)
    vec_sum = Scatter(
        *[lax.dynamic_index_in_dim(vec_view, w, 4, keepdims=False) for w in (c, 1 - c)], XY
    )
    tail = sums[0]
    vec_sum.cores(tail["time"].got)
    vec_sum.first()
    tail["time"].second(tail["gate"])
    vec_sum.second()
    _, whole = finish([tail["mid"], tail["time"], vec_sum])
    for l in range(1, layers):
        for e in (sums[l]["feed"], sums[l]["mid"], sums[l]["time"]):
            e.out = after(e.out, whole)
    for e in tail["feed"]:
        e.out = after(e.out, whole)
    g_vec = vec_sum.out[0]
    grads = []
    for l in range(layers):
        if l > 0:
            feed = sums[l]["feed"].out
            g_fk, g_fv = feed[:, : blocks * D], feed[:, blocks * D :]
            g_fv = jnp.concatenate([g_fv[:, b * D : (b + 1) * D] for b in range(blocks)], axis=0)
        else:
            g_fv, g_fk = (s.out for s in sums[l]["feed"])
            g_fv, g_fk = g_fv.reshape(-1, D), jnp.concatenate(list(g_fk), axis=1)
        g_out, g_gate, g_recept = sums[l]["mid"].out
        g_key, g_value = sums[l]["time"].out
        grads.append(
            (
                g_vec[:, [32 * l + k for k in VECTOR_ROWS]].T,
                jnp.stack([g_key, g_value, g_recept, g_gate]),
                g_out,
                by_device(g_fk),
                g_fv,
            )
        )
    totals = tuple(jnp.stack([g[m] for g in grads]) for m in range(5))
    rates = (vector_rates(kinds),) + (rate_main,) * 4
    decays = (0.0,) + (weight_decay,) * 4
    new = [adam_step(*z) for z in zip(weights, totals, means, powers, rates, decays)]
    return (
        block_out,
        grad.reshape(R, T, D),
        *totals,
        *[z[0] for z in new],
        *[z[1] for z in new],
        *[z[2] for z in new],
    )


def solution(mesh):
    dp, seq = mesh.shape["dp"], mesh.shape["seq"]
    mesh = Mesh(mesh.devices.reshape(dp, seq // 2, 2), AXES)
    tokens = P("dp", SEQ, None)
    group = (
        P(None, None, AXES),
        P(None, None, AXES, None),
        P(None, AXES, None),
        P(None, AXES, None),
        P(None, AXES, None),
    )
    in_specs = (tokens, tokens, P("dp", None)) + group * 3
    out_specs = (tokens, tokens) + group * 4
    return jax.shard_map(body, mesh=mesh, in_specs=in_specs, out_specs=out_specs, check_vma=False)
```

```python
import jax
import jax.numpy as jnp
from jax import lax
from jax.experimental import pallas as pl
from jax.experimental.pallas import tpu as pltpu
from jax.sharding import Mesh, PartitionSpec as P

norm_epsilon = 1e-05
beta_one = 0.9
beta_two = 0.99
adam_epsilon = 1e-08
step_count = 10
rate_main = 0.0006
rate_time = 0.0012
weight_decay = 0.1

RB = 2
COST = 20
VMEM = 63 * 1024 * 1024
F32, BF16 = jnp.float32, jnp.bfloat16


def dot_nn(a, b):
    return lax.dot_general(a, b, (((1,), (0,)), ((), ())), preferred_element_type=F32)


def dot_nt(a, b):
    return lax.dot_general(a, b, (((1,), (1,)), ((), ())), preferred_element_type=F32)


def dot_tn(a, b):
    return lax.dot_general(a, b, (((0,), (0,)), ((), ())), preferred_element_type=F32)


def colsum(a):
    return jnp.sum(a, axis=0, keepdims=True)


LANES = 128


def columns(D):
    return [slice(j, j + LANES) for j in range(0, D, LANES)]


def place_of(starts_ref, base_ref, row, T):
    local = lax.broadcasted_iota(jnp.int32, (T, LANES), 0)
    base = base_ref[0]
    begin = jnp.zeros((T, LANES), jnp.int32)
    last_begin = jnp.int32(0)
    for j in range(starts_ref.shape[1]):
        s = starts_ref[row, j]
        begin = jnp.where(local + base >= s, jnp.maximum(begin, s), begin)
        last_begin = jnp.where(base + T - 1 >= s, jnp.maximum(last_begin, s), last_begin)
    dist = local + base - begin
    tail = (local + base >= last_begin).astype(F32)
    return local, dist, tail


def levels(T):
    k = 1
    while k < T:
        yield k
        k *= 2


def keeps_of(local, dist, T):
    return [((dist >= k) & (local >= k)).astype(F32) for k in levels(T)]


def lane_mean(total, D):
    return jnp.broadcast_to(jnp.sum(total, axis=-1, keepdims=True) * (1.0 / D), total.shape)


def norm_stats(x, rows, D):
    mean = lane_mean(sum(x[rows, c].astype(F32) for c in columns(D)), D)
    spread = [x[rows, c].astype(F32) - mean for c in columns(D)]
    rstd = lax.rsqrt(lane_mean(sum(s * s for s in spread), D) + norm_epsilon)
    return mean, rstd


def norm_rows(x, gain, bias):
    centred = x - jnp.mean(x, axis=-1, keepdims=True)
    rstd = lax.rsqrt(jnp.mean(centred * centred, axis=-1, keepdims=True) + norm_epsilon)
    return centred * rstd * gain + bias


def previous_of(normalized, edge, local, joined):
    return jnp.where(local == 0, edge, pltpu.roll(normalized, 1, 0)) * joined


def mixed(x, rows, c, stats, vec, gain_row, edge, local, joined):
    mean, rstd = stats
    normalized = (x[rows, c].astype(F32) - mean) * rstd * vec[gain_row : gain_row + 1, c]
    normalized = normalized + vec[gain_row + 1 : gain_row + 2, c]
    previous = previous_of(normalized, edge, local, joined)
    return previous, normalized - previous


def shift_up(masked, local, T):
    return jnp.where(local == T - 1, 0.0, pltpu.roll(masked, T - 1, 0))


def scan_down(pair, rate, keeps, T):
    for k, keep in zip(levels(T), keeps):
        weight = keep * jnp.exp(-float(k) * rate)
        pair = tuple(a + weight * pltpu.roll(a, k, 0) for a in pair)
    return pair


def scan_up(pair, rate, keeps, T):
    for k, keep in zip(levels(T), keeps):
        weight = keep * jnp.exp(-float(k) * rate)
        pair = tuple(a + pltpu.roll(weight * a, T - k, 0) for a in pair)
    return pair


def piece_copies(base, pieces, item, target, sems, at):
    count, first_in_block, first, width, rows, bits = item
    columns = pl.ds(first, width)
    if count == 1:
        return [(0, pltpu.make_async_copy(pieces[0].at[:, pl.ds(first_in_block, width)], target, sems.at[at]))]
    block, one, two, other_one, other_two = pieces
    d, c = base[1], base[2]
    copies = []
    for half, first_ref, second_ref in ((c, one, two), (1 - c, other_one, other_two)):
        start = pl.multiple_of(half * rows, rows)
        for source, m in (
            (block.at[pl.ds(start, rows), pl.ds(first_in_block, width)], 0),
            (first_ref.at[:, columns], bits[0]),
            (second_ref.at[0, :, columns], bits[1]),
            (second_ref.at[1, :, columns], bits[0] | bits[1]),
        ):
            row = pl.multiple_of(((d ^ m) * 2 + half) * rows, rows)
            copies.append(
                (m, pltpu.make_async_copy(
                    source, target.at[pl.ds(row, rows)], sems.at[at + len(copies)]
                ))
            )
    return copies


def split_refs(items, refs):
    groups, at = [], 0
    for count in items:
        groups.append(refs[at : at + count])
        at += count
    return groups, refs[at:]


def k_time_in(items, T, starts, base, x, edge, vec, *refs):
    (pieces,), (mk, mv, mr, ko, vo, no, do, last, w, sems) = split_refs([items[0][0]], refs)
    D = x.shape[1]
    i = pl.program_id(0)
    copies = [
        copy
        for s, item in enumerate(items)
        for copy in piece_copies(base, pieces, item, w.at[s], sems, 8 * s)
    ]

    @pl.when(i == 0)
    def _():
        for _, copy in copies:
            copy.start()

    edge_norm = norm_rows(edge[0], vec[0:1], vec[1:2])
    places = [place_of(starts, base, i * RB + q, T) for q in range(RB)]
    for q, (local, dist, _) in enumerate(places):
        rows = slice(q * T, q * T + T)
        joined = (dist >= 1).astype(F32)
        stats = norm_stats(x, rows, D)
        for c in columns(D):
            previous, change = mixed(
                x, rows, c, stats, vec, 0, edge_norm[q : q + 1, c], local, joined
            )
            for j, out in ((2, mk), (3, mv), (4, mr)):
                out[rows, c] = (previous + change * vec[j : j + 1, c]).astype(BF16)

    @pl.when(i == 0)
    def _():
        for _, copy in copies:
            copy.wait()

    ko[...] = dot_nn(mk[...], w[0])
    vo[...] = dot_nn(mv[...], w[1]).astype(vo.dtype)
    for q, (local, dist, _) in enumerate(places):
        rows = slice(q * T, q * T + T)
        keeps = keeps_of(local, dist, T)
        for c in columns(D):
            rate = jnp.exp(vec[5:6, c])
            weight = jnp.exp(ko[rows, c])
            sums = scan_down((weight * vo[rows, c].astype(F32), weight), rate, keeps, T)
            for side, (out, total) in enumerate(zip((no, do), sums)):
                out[rows, c] = (keeps[0] * pltpu.roll(total, 1, 0)).astype(out.dtype)
                last[q, side : side + 1, c] = total[T - 1 : T]


def decay_state(vec, c, key, value, num, den, state, local, dist):
    rate = jnp.exp(vec[5:6, c])
    fade = (dist >= local + 1).astype(F32) * jnp.exp(-local.astype(F32) * rate)
    full_n = num.astype(F32) + fade * state[0:1]
    full_d = den.astype(F32) + fade * state[1:2]
    extra = jnp.exp(vec[6:7, c] + key)
    inverse = 1.0 / (full_d + extra)
    mean = (full_n + extra * value) * inverse
    return full_n, full_d, extra, inverse, mean


def k_time_out(items, T, starts, base, x, key, value, mr, num, den, state, vec, *refs):
    (pieces,), (gated, middle, recept, w, sems) = split_refs([items[0][0]], refs)
    D = x.shape[1]
    i = pl.program_id(0)
    copies = [
        copy
        for s, item in enumerate(items)
        for copy in piece_copies(base, pieces, item, w.at[s], sems, 8 * s)
    ]

    @pl.when(i == 0)
    def _():
        for _, copy in copies:
            copy.start()

    @pl.when(i == 0)
    def _():
        for _, copy in copies:
            copy.wait()

    recept[...] = dot_nn(mr[...], w[0]).astype(BF16)
    for q in range(RB):
        local, dist, _ = place_of(starts, base, i * RB + q, T)
        rows = slice(q * T, q * T + T)
        for c in columns(D):
            mean = decay_state(
                vec, c, key[rows, c], value[rows, c].astype(F32), num[rows, c], den[rows, c], state[q, :, c],
                local, dist,
            )[4]
            gated[rows, c] = (jax.nn.sigmoid(recept[rows, c].astype(F32)) * mean).astype(BF16)

    middle[...] = x[...].astype(F32) + dot_nn(gated[...], w[1])


def feed_copies(items, base, pieces, wg, wk, wv, sems):
    items = items[1:]

    def copies(index, target, at):
        group, item = items[index]
        return piece_copies(base, pieces[group], item, target, sems, at)

    blocks = (len(items) - 1) // 2
    pairs = [
        copies(1 + b, wk.at[b], 8 + 16 * b) + copies(1 + blocks + b, wv.at[b], 16 + 16 * b)
        for b in range(blocks)
    ]
    return copies(0, wg, 0), pairs


def feed_start(copies):
    gate, pairs = copies
    for _, copy in [z for block in pairs for z in block] + gate:
        copy.start()


def feed_wait(copies, j):
    for b, block in enumerate(copies[1]):

        @pl.when(j == b)
        def _():
            for _, copy in block:
                copy.wait()


def k_feed(items, T, starts, base, middle, edge, vec, *refs):
    pieces, (fm, gm, sp, hid, vb, gl, xo, acc, wg, wk, wv, sems) = split_refs(items[0], refs)
    M, D = middle.shape
    j = pl.program_id(0)
    copies = feed_copies(items, base, pieces, wg, wk, wv, sems)

    @pl.when(j == 0)
    def _():
        feed_start(copies)
        edge_norm = norm_rows(edge[...], vec[7:8], vec[8:9])
        for q in range(M // T):
            local, dist, _ = place_of(starts, base, q, T)
            rows = slice(q * T, q * T + T)
            joined = (dist >= 1).astype(F32)
            stats = norm_stats(middle, rows, D)
            for c in columns(D):
                previous, change = mixed(
                    middle, rows, c, stats, vec, 7, edge_norm[q : q + 1, c], local, joined
                )
                fm[rows, c] = (previous + change * vec[9:10, c]).astype(BF16)
                gm[rows, c] = (previous + change * vec[10:11, c]).astype(BF16)
        acc[...] = jnp.zeros_like(acc)

    feed_wait(copies, j)
    pre = dot_nn(fm[...], wk[j])
    soft = jnp.maximum(pre, 0.0) + jnp.log(1.0 + jnp.exp(-jnp.abs(pre)))
    sp[...] = soft.astype(BF16)
    hidden = (soft * soft).astype(BF16)
    hid[...] = hidden
    acc[...] += dot_nn(hidden, wv[j])

    @pl.when(j == pl.num_programs(0) - 1)
    def _():
        for _, copy in copies[0]:
            copy.wait()
        gate = dot_nn(gm[...], wg[...])
        gl[...] = gate.astype(BF16)
        vb[...] = acc[...].astype(BF16)
        xo[...] = middle[...] + jax.nn.sigmoid(gate) * acc[...]


def k_feed_back(items, T, starts, base, grad, gl, vb, sp, middle, edge, vec, *refs):
    pieces, (gb, gg, gin, gn, first, sums, acc, gc, wg, wk, wv, sems) = split_refs(
        items[0], refs
    )
    M, D = middle.shape
    j = pl.program_id(0)
    copies = feed_copies(items, base, pieces, wg, wk, wv, sems)

    @pl.when(j == 0)
    def _():
        feed_start(copies)
        g = grad[...].astype(F32)
        s = jax.nn.sigmoid(gl[...].astype(F32))
        gb[...] = (g * s).astype(BF16)
        gg[...] = (g * vb[...].astype(F32) * s * (1.0 - s)).astype(BF16)
        acc[...] = jnp.zeros_like(acc)

    feed_wait(copies, j)
    soft = sp[...].astype(F32)
    gh = dot_nt(gb[...], wv[j])
    pre = (gh * (2.0 * soft * (1.0 - jnp.exp(-soft)))).astype(BF16)
    gin[...] = pre
    acc[...] += dot_nt(pre, wk[j])

    @pl.when(j == pl.num_programs(0) - 1)
    def _():
        for _, copy in copies[0]:
            copy.wait()
        gc[...] = dot_nt(gg[...], wg[...])
        edge_norm = norm_rows(edge[...], vec[7:8], vec[8:9])
        sums[...] = jnp.zeros_like(sums)
        for q in range(M // T):
            local, dist, _ = place_of(starts, base, q, T)
            rows = slice(q * T, q * T + T)
            joined = (dist >= 1).astype(F32)
            stats = norm_stats(middle, rows, D)
            for c in columns(D):
                _, change = mixed(
                    middle, rows, c, stats, vec, 7, edge_norm[q : q + 1, c], local, joined
                )
                ga, gb_ = acc[rows, c], gc[rows, c]
                sums[0:1, c] += colsum(ga * change)
                sums[1:2, c] += colsum(gb_ * change)
                direct = ga * vec[9:10, c] + gb_ * vec[10:11, c]
                masked = (ga + gb_ - direct) * joined
                gn[rows, c] = (direct + shift_up(masked, local, T)).astype(gn.dtype)
                first[q : q + 1, c] = masked[0:1]


def norm_back(x, rows, gain_row, vec, total, sums, D, put):
    mean, rstd = norm_stats(x, rows, D)
    one = two = None
    for c in columns(D):
        hat = (x[rows, c].astype(F32) - mean) * rstd
        g = total(c)
        scaled = g * vec[gain_row : gain_row + 1, c]
        sums[0:1, c] += colsum(g * hat)
        sums[1:2, c] += colsum(g)
        one = scaled if one is None else one + scaled
        two = scaled * hat if two is None else two + scaled * hat
    one, two = lane_mean(one, D), lane_mean(two, D)
    for c in columns(D):
        hat = (x[rows, c].astype(F32) - mean) * rstd
        put(c, rstd * (total(c) * vec[gain_row : gain_row + 1, c] - one - hat * two))


def with_edge(gn, rows, edge, local, T):
    return lambda c: gn[rows, c].astype(F32) + jnp.where(local == T - 1, edge[:, c], 0.0)


def k_mid_back(items, T, starts, base, gn, edge, middle, grad, vec,
               key, value, recept, num, den, state, *refs):
    (pieces,), rest = split_refs([items[0][0]], refs)
    gm, gblk, gr, gkp, gvp, gno, gdo, direct, sums, ggated, w, sems = rest
    D = middle.shape[1]
    i = pl.program_id(0)
    copies = piece_copies(base, pieces, items[0], w, sems, 0)

    @pl.when(i == 0)
    def _():
        for _, copy in copies:
            copy.start()
        sums[...] = jnp.zeros_like(sums)

    places = [place_of(starts, base, i * RB + q, T) for q in range(RB)]
    for q, (local, dist, _) in enumerate(places):
        rows = slice(q * T, q * T + T)

        def put(c, gx):
            gmid = grad[rows, c].astype(F32) + gx
            gm[rows, c] = gmid
            gblk[rows, c] = gmid.astype(BF16)

        total = with_edge(gn, rows, edge[0, q : q + 1], local, T)
        norm_back(middle, rows, 7, vec, total, sums, D, put)

    @pl.when(i == 0)
    def _():
        for _, copy in copies:
            copy.wait()

    ggated[...] = dot_nt(gblk[...], w[...])
    for q, (local, dist, _) in enumerate(places):
        rows = slice(q * T, q * T + T)
        joined = (dist >= 1).astype(F32)
        keeps = keeps_of(local, dist, T)
        for c in columns(D):
            v, g = value[rows, c].astype(F32), ggated[rows, c]
            _, _, extra, inverse, mean = decay_state(
                vec, c, key[rows, c], v, num[rows, c], den[rows, c], state[q, :, c], local, dist
            )
            s = jax.nn.sigmoid(recept[rows, c].astype(F32))
            gr[rows, c] = (g * mean * s * (1.0 - s)).astype(BF16)
            r = g * s * inverse
            ge = extra * r * (v - mean)
            gkp[rows, c] = ge.astype(gkp.dtype)
            gvp[rows, c] = (r * extra).astype(gvp.dtype)
            sums[2:3, c] += colsum(ge)
            rate = jnp.exp(vec[5:6, c])
            totals = scan_up((r, -r * mean), rate, keeps, T)
            for side, (out, a) in enumerate(zip((gno, gdo), totals)):
                out[rows, c] = pltpu.roll(keeps[0] * a, T - 1, 0).astype(out.dtype)
                direct[q, side : side + 1, c] = (joined * a)[0:1]


def k_time_back(items, T, starts, base, x, edge, vec, key, value, num, den, state,
                gkp, gvp, gno, gdo, after, gr, *refs):
    pieces, (gk, gv, gn, first, sums, mixes, w, sems) = split_refs(items[0], refs)
    D = x.shape[1]
    i = pl.program_id(0)
    copies = [
        copy
        for s, (group, item) in enumerate(items[1:])
        for copy in piece_copies(base, pieces[group], item, w.at[s], sems, 8 * s)
    ]

    @pl.when(i == 0)
    def _():
        for _, copy in copies:
            copy.start()
        sums[...] = jnp.zeros_like(sums)

    places = [place_of(starts, base, i * RB + q, T) for q in range(RB)]
    for q, (local, dist, tail) in enumerate(places):
        rows = slice(q * T, q * T + T)
        inside = (dist >= local + 1).astype(F32)
        for c in columns(D):
            rate = jnp.exp(vec[5:6, c])
            fade = inside * jnp.exp(-local.astype(F32) * rate)
            full_n = num[rows, c].astype(F32) + fade * state[q, 0:1, c]
            full_d = den[rows, c].astype(F32) + fade * state[q, 1:2, c]
            left = tail * jnp.exp(-(T - 1 - local).astype(F32) * rate)
            grad_n = gno[rows, c].astype(F32) + left * after[q, 0:1, c]
            grad_d = gdo[rows, c].astype(F32) + left * after[q, 1:2, c]
            weight = jnp.exp(key[rows, c])
            gk[rows, c] = (
                gkp[rows, c].astype(F32) + weight * (grad_n * value[rows, c].astype(F32) + grad_d)
            ).astype(BF16)
            gv[rows, c] = (gvp[rows, c].astype(F32) + weight * grad_n).astype(BF16)
            turn = colsum(grad_n * full_n + grad_d * full_d)
            sums[3:4, c] += -rate * jnp.exp(-rate) * turn

    @pl.when(i == 0)
    def _():
        for _, copy in copies:
            copy.wait()

    for s, g in enumerate((gk, gv, gr)):
        mixes[s] = dot_nt(g[...], w[s])
    edge_norm = norm_rows(edge[0], vec[0:1], vec[1:2])
    for q, (local, dist, _) in enumerate(places):
        rows = slice(q * T, q * T + T)
        joined = (dist >= 1).astype(F32)
        stats = norm_stats(x, rows, D)
        for c in columns(D):
            _, change = mixed(x, rows, c, stats, vec, 0, edge_norm[q : q + 1, c], local, joined)
            gs = [mixes[s, rows, c] for s in range(3)]
            for s in range(3):
                sums[s : s + 1, c] += colsum(gs[s] * change)
            direct = sum(g * vec[2 + s : 3 + s, c] for s, g in enumerate(gs))
            masked = (gs[0] + gs[1] + gs[2] - direct) * joined
            gn[rows, c] = (direct + shift_up(masked, local, T)).astype(gn.dtype)
            first[0, q : q + 1, c] = masked[0:1]


def k_norm_back(T, x, gn, edge, gmid, vec, go, sums):
    i = pl.program_id(0)
    D = x.shape[1]

    @pl.when(i == 0)
    def _():
        sums[...] = jnp.zeros_like(sums)

    local = lax.broadcasted_iota(jnp.int32, (T, LANES), 0)
    for q in range(RB):
        rows = slice(q * T, q * T + T)

        def put(c, gx):
            go[rows, c] = gmid[rows, c] + gx

        total = with_edge(gn, rows, edge[0, q : q + 1], local, T)
        norm_back(x, rows, 0, vec, total, sums, D, put)


def put_halves(base, product, n, mine, send):
    pairs = product.shape[0] // (2 * n)
    lead, Z = mine.shape[0], mine.shape[1]
    for p in range(pairs):
        for out, half in ((mine, base[2]), (send, 1 - base[2])):
            start = pl.multiple_of((2 * p + half) * n, 8)
            out[p // Z, p % Z, 0] = product[pl.ds(start, n), :].astype(BF16)


def k_halves_apart(n, count, T, starts, base, *refs):
    lefts, grads, rest = refs[:count], refs[count : 2 * count], refs[2 * count :]
    mine, send, left, grad, product, sems = rest
    i = pl.program_id(0)
    pairs = [
        [
            pltpu.make_async_copy(source, target.at[k], sems.at[2 * k + side])
            for side, (source, target) in enumerate(((lefts[k], left), (grads[k], grad)))
        ]
        for k in range(count)
    ]

    @pl.when(i == 0)
    def _():
        for pair in pairs:
            for copy in pair:
                copy.start()

    for k, pair in enumerate(pairs):

        @pl.when(i == k)
        def _():
            for copy in pair:
                copy.wait()

    product[...] = dot_tn(left[i], grad[i])
    put_halves(base, product, n, mine, send)


def k_halves_blocks(n, T, starts, base, left, grad, mine, send, product):
    product[...] = dot_tn(left[...], grad[...])
    put_halves(base, product, n, mine, send)


def k_flat(T, fm, gin, hid, gb, out):
    i = pl.program_id(0)
    half = pl.num_programs(0) // 2

    @pl.when(i < half)
    def _():
        out[...] = dot_tn(fm[...], gin[...]).astype(BF16)

    @pl.when(i >= half)
    def _():
        out[...] = dot_tn(hid[...], gb[...]).astype(BF16)


def smem():
    return pl.BlockSpec(memory_space=pltpu.SMEM)


def rows_spec(T, D):
    return pl.BlockSpec((RB * T, D), lambda i: (i, 0))


def col_spec(rows, width, at):
    return pl.BlockSpec((rows, width), lambda i: (0, at))


def whole_spec(shape):
    zeros = (0,) * len(shape)
    return pl.BlockSpec(shape, lambda i: zeros)


def edge_spec(D):
    return pl.BlockSpec((1, RB, D), lambda i: (i, 0, 0))


def state_spec(D):
    return pl.BlockSpec((RB, 2, D), lambda i: (i, 0, 0))


def shape(dims, kind):
    return jax.ShapeDtypeStruct(dims, kind)


def run(kernel, T, grid, in_specs, out_specs, outs, args, flops, moved, scratch=(), items=(),
        after=()):
    count = len(args)
    in_specs = in_specs + anywhere(len(after))
    args = args + tuple(after)

    def body(*refs):
        kernel(*(items if isinstance(items, tuple) else (items,) if items else ()), T, *refs[:count], *refs[count + len(after) :])

    return pl.pallas_call(
        body,
        grid=(grid,),
        in_specs=in_specs,
        out_specs=out_specs,
        out_shape=outs,
        scratch_shapes=scratch,
        compiler_params=pltpu.CompilerParams(
            dimension_semantics=("arbitrary",), vmem_limit_bytes=VMEM
        ),
        cost_estimate=pl.CostEstimate(
            flops=flops // COST, bytes_accessed=moved // COST, transcendentals=0
        ),
        name=kernel.__name__,
    )(*args)


def anywhere(count):
    return [pl.BlockSpec(memory_space=pl.ANY)] * count


def weight_room(shapes, copies):
    return [pltpu.VMEM(s, BF16) for s in shapes] + [pltpu.SemaphoreType.DMA((copies,))]


def time_in(T, place, x, edge, vec, weights, after=()):
    N, D = x.shape
    R = N // T
    rs = rows_spec(T, D)
    pieces = weights["key"][0]
    items = [weights[name][1] for name in ("key", "value")]
    return run(
        k_time_in, T, R // RB,
        [smem(), smem(), rs, edge_spec(D), whole_spec(vec.shape)] + anywhere(len(pieces)),
        [rs] * 7 + [state_spec(D)],
        [shape((N, D), BF16)] * 3 + [shape((N, D), F32)] + [shape((N, D), BF16)] * 3
        + [shape((R, 2, D), F32)],
        (*place, x, edge.reshape(R // RB, RB, D), vec, *pieces),
        4 * N * D * D, 40 * N * D,
        weight_room([(2, D, D)], 16), items, after,
    )


def time_out(T, place, x, kept, state, vec, weights, after=()):
    N, D = x.shape
    R = N // T
    rs = rows_spec(T, D)
    pieces = weights["output"][0]
    items = [weights[name][1] for name in ("recept", "output")]
    return run(
        k_time_out, T, R // RB,
        [smem(), smem()] + [rs] * 6 + [state_spec(D), whole_spec(vec.shape)] + anywhere(len(pieces)),
        [rs] * 3,
        [shape((N, D), BF16), shape((N, D), F32), shape((N, D), BF16)],
        (*place, x, *kept, state, vec, *pieces),
        4 * N * D * D, 30 * N * D,
        weight_room([(2, D, D)], 16), items, after,
    )


def grouped(weights, names):
    groups, items = [], []
    for name in names:
        pieces, item = weights[name]
        found = [k for k, group in enumerate(groups) if group is pieces]
        if not found:
            found = [len(groups)]
            groups.append(pieces)
        items.append((found[0], item))
    pieces = tuple(piece for group in groups for piece in group)
    return [[len(group) for group in groups]] + items, pieces


def feed_weights(weights):
    keys, values = (
        sorted(name for name in weights if name.startswith(kind)) for kind in ("feed_key", "feed_value")
    )
    return grouped(weights, ["gate"] + keys + values)


def feed(T, place, middle, edge, vec, weights, after=()):
    N, D = middle.shape
    items, pieces = feed_weights(weights)
    B = (len(items) - 2) // 2
    F = B * D
    whole = whole_spec((N, D))
    wide_spec = pl.BlockSpec((N, D), lambda j: (0, j))
    return run(
        k_feed, T, B,
        [smem(), smem(), whole, whole_spec(edge.shape), whole_spec(vec.shape)] + anywhere(len(pieces)),
        [whole, whole, wide_spec, wide_spec, whole, whole, whole],
        [shape((N, D), BF16)] * 2 + [shape((N, F), BF16)] * 2 + [shape((N, D), BF16)] * 2
        + [shape((N, D), F32)],
        (*place, middle, edge, vec, *pieces),
        4 * N * D * F + 2 * N * D * D, 20 * N * D + 4 * N * F + 4 * D * F,
        [pltpu.VMEM((N, D), F32)]
        + weight_room([(D, D), (B, D, D), (B, D, D)], 8 * len(items)), items, after,
    )


def feed_back(T, place, grad, gl, vb, sp, middle, edge, vec, weights, after=()):
    N, D = middle.shape
    items, pieces = feed_weights(weights)
    B = (len(items) - 2) // 2
    F = B * D
    R = N // T
    whole = whole_spec((N, D))
    wide_spec = pl.BlockSpec((N, D), lambda j: (0, j))
    return run(
        k_feed_back, T, B,
        [smem(), smem(), whole, whole, whole, wide_spec, whole, whole_spec(edge.shape),
         whole_spec(vec.shape)] + anywhere(len(pieces)),
        [whole, whole, wide_spec, whole, whole_spec((R, D)), whole_spec((8, D))],
        [shape((N, D), BF16)] * 2 + [shape((N, F), BF16), shape((N, D), BF16)]
        + [shape((R, D), F32), shape((8, D), F32)],
        (*place, grad, gl, vb, sp, middle, edge, vec, *pieces),
        4 * N * D * F + 2 * N * D * D, 20 * N * D + 4 * N * F + 4 * D * F,
        [pltpu.VMEM((N, D), F32)] * 2
        + weight_room([(D, D), (B, D, D), (B, D, D)], 8 * len(items)), items, after,
    )


def mid_back(T, place, gn, edge, middle, grad, vec, weights, kept, state, after=()):
    N, D = middle.shape
    R = N // T
    rs = rows_spec(T, D)
    pieces, item = weights["output"]
    return run(
        k_mid_back, T, R // RB,
        [smem(), smem(), rs, edge_spec(D), rs, rs, whole_spec(vec.shape)]
        + [rs] * 5 + [state_spec(D)] + anywhere(len(pieces)),
        [rs] * 7 + [state_spec(D), whole_spec((8, D))],
        [shape((N, D), F32)] + [shape((N, D), BF16)] * 6
        + [shape((R, 2, D), F32), shape((8, D), F32)],
        (*place, gn, edge.reshape(R // RB, RB, D), middle, grad, vec, *kept, state, *pieces),
        2 * N * D * D, 50 * N * D,
        [pltpu.VMEM((RB * T, D), F32)] + weight_room([(D, D)], 8), [item], after,
    )


def time_back(T, place, x, edge, vec, weights, kept, state, part, later, gr, after=()):
    N, D = x.shape
    R = N // T
    rs = rows_spec(T, D)
    items, pieces = grouped(weights, ("key", "value", "recept"))
    return run(
        k_time_back, T, R // RB,
        [smem(), smem(), rs, edge_spec(D), whole_spec(vec.shape)]
        + [rs] * 4 + [state_spec(D)] + [rs] * 4 + [state_spec(D), rs] + anywhere(len(pieces)),
        [rs] * 3 + [edge_spec(D), whole_spec((8, D))],
        [shape((N, D), BF16)] * 3
        + [shape((R // RB, RB, D), F32), shape((8, D), F32)],
        (*place, x, edge.reshape(R // RB, RB, D), vec, *kept, state, *part, later, gr, *pieces),
        6 * N * D * D, 50 * N * D,
        [pltpu.VMEM((3, RB * T, D), F32)] + weight_room([(3, D, D)], 24), items, after,
    )


def norm_in_back(T, x, gn, edge, gmid, vec, after=()):
    N, D = x.shape
    R = N // T
    rs = rows_spec(T, D)
    return run(
        k_norm_back, T, R // RB,
        [rs, rs, edge_spec(D), rs, whole_spec(vec.shape)],
        [rs, whole_spec((8, D))],
        [shape((N, D), F32), shape((8, D), F32)],
        (x, gn, edge.reshape(R // RB, RB, D), gmid, vec),
        0, 16 * N * D, after=after,
    )


SEQ = ("z", "c")
AXES = ("dp", "z", "c")
SWAP = [(0, 1), (1, 0)]


def by_bit(block, bit):
    return lax.ppermute(block, "dp", [(i, i ^ bit) for i in range(lax.axis_size("dp"))])


def after(value, *others):
    return lax.optimization_barrier((value, *others))[0]


def gather_seq(part, *gate):
    return lax.all_gather(after(part, *gate), SEQ, axis=0, tiled=True)


class Gathered:
    def __init__(self, part, names, *gate):
        self.block = lax.all_gather(after(part, *gate), AXES, axis=0, tiled=True)
        self.names = names

    def weights(self):
        pieces, at, found = (self.block,), 0, {}
        for name, width in self.names:
            found[name] = (pieces, (1, at, 0, width, 0, (0, 0)))
            at += width
        return found


class Exchange:
    def __init__(self, block, names, start, bits):
        self.block, self.names, self.start, self.bits = block, names, start, bits
        self.width = sum(width for _, width in names)
        self.rows = block.shape[0] // 2

    def prepare(self, *gate):
        block = after(self.block, *gate)
        self.own = lax.dynamic_slice(
            block, (lax.axis_index("c") * self.rows, self.start), (self.rows, self.width)
        )
        return self.own

    def first(self, *gate):
        own = self.prepare(*gate) if gate else self.own
        self.one = by_bit(own, self.bits[0])
        return self.one

    def second(self, *gate):
        one = after(self.one, *gate)
        self.two = by_bit(jnp.stack([self.own, one]), self.bits[1])
        return self.two

    def cores(self, *gate):
        self.one, self.two = after((self.one, self.two), *gate)
        self.other_one = lax.ppermute(self.one, "c", SWAP)
        self.other_two = lax.ppermute(self.two, "c", SWAP)

    def weights(self):
        if not hasattr(self, "pieces"):
            self.pieces = (self.block, self.one, self.two, self.other_one, self.other_two)
        pieces, at, found = self.pieces, 0, {}
        for name, width in self.names:
            found[name] = (pieces, (5, self.start + at, at, width, self.rows, self.bits))
            at += width
        return found


class Scatter:
    def __init__(self, mine, send, bits):
        self.mine, self.send, self.bits = mine, send, bits

    def part(self, a, y, x):
        if y is not None:
            a = lax.dynamic_index_in_dim(a, y, 0, keepdims=True)
        if x is not None:
            a = lax.dynamic_index_in_dim(a, x, 1, keepdims=True)
        return a.astype(F32)

    def cores(self, *gate):
        self.received = lax.ppermute(after(self.send, *gate), "c", SWAP)
        return self.received

    def first(self, *gate):
        d = lax.axis_index("dp")
        y, x = d // 2, d % 2
        terms = after((self.mine, self.received), *gate)
        place = (1 - y, None) if self.bits[1] == 2 else (None, 1 - x)
        self.sent = sum(self.part(a, *place) for a in terms).astype(BF16)
        self.got = by_bit(self.sent, self.bits[1])
        return self.got

    def second(self, *gate):
        d = lax.axis_index("dp")
        y, x = d // 2, d % 2
        terms = after((self.mine, self.received, self.got), *gate)

        def total(y, x):
            got = self.part(terms[2], *((None, x) if self.bits[1] == 2 else (y, None)))
            return self.part(terms[0], y, x) + self.part(terms[1], y, x) + got

        there = (y, 1 - x) if self.bits[1] == 2 else (1 - y, x)
        self.two = by_bit(total(*there).astype(BF16), self.bits[0])
        self.keep = lambda two: (total(y, x) + two.astype(F32)).astype(BF16)
        return self.two


def finish(scatters, *gate):
    parts, shapes = [], []
    width = max(s.mine.shape[-1] for s in scatters)
    for scatter in scatters:
        total = scatter.keep(after(scatter.two, *gate))[0, 0]
        Z, I, n, C = total.shape
        if C < width:
            total = jnp.pad(total, ((0, 0), (0, 0), (0, 0), (0, width - C)))
        parts.append(total.reshape(Z, I * n, width))
        shapes.append((I, n, C))
    whole = jnp.concatenate(parts, axis=1)
    out = lax.psum_scatter(
        whole.reshape(-1, whole.shape[2]), "z", scatter_dimension=0, tiled=True
    )
    at = 0
    for scatter, (I, n, C) in zip(scatters, shapes):
        scatter.out = out[at : at + I * n, :C].reshape(I, n, C).astype(F32)
        at += I * n
    return out, whole


def from_behind(block, distance):
    devices = range(lax.axis_size(SEQ))
    route = [(i - distance, i) for i in devices if i - distance in devices]
    return lax.ppermute(block, SEQ, route)


def chain(mine, starts, rate, T, forward):
    S, i = lax.axis_size(SEQ), lax.axis_index(SEQ)
    all_states = lax.all_gather(mine.astype(BF16), SEQ).astype(F32)
    j = jnp.arange(S, dtype=jnp.int32)

    def document(at):
        return jnp.sum((starts[None] <= at[:, None, None]).astype(jnp.int32), axis=2)

    if forward:
        lag = i - 1 - j
        same = document((j + 1) * T - 1) == document((i * T - 1)[None])
    else:
        lag = j - 1 - i
        same = document(j * T - 1) == document(((i + 1) * T - 1)[None])
    keep = (same & (lag >= 0)[:, None]).astype(F32)
    fade = jnp.exp(-(T * jnp.maximum(lag, 0)).astype(F32)[:, None] * rate[None])
    weight = keep[:, :, None, None] * fade[:, None, None, :]
    return jnp.sum(weight * all_states, axis=0)


def layer_forward(T, place, starts, x, edge, vec, weights, hook):
    N, D = x.shape
    R = N // T
    rate = jnp.exp(vec[5])
    x = hook("start", x)
    mk, mv, mr, key, value, num, den, last = time_in(T, place, x, edge, vec, weights())
    last = hook("time in", last)
    state = chain(last, starts, rate, T, True)
    state = hook("chain", state)
    gated, middle, recept = time_out(
        T, place, x, (key, value, mr, num, den), state, vec, weights()
    )
    middle = hook("time out", middle)
    edge_two = from_behind(middle.reshape(R, T, D)[:, -1], 1)
    edge_two = hook("edge", edge_two)
    fm, gm, sp, hid, vb, gl, out = feed(T, place, middle, edge_two, vec, weights())
    out = hook("feed", out)
    saved = (x, edge, mk, mv, mr, key, value, recept, num, den, state, gated, middle, edge_two,
             fm, gm, sp, hid, vb, gl)
    return out, saved


def weight_halves(place, lefts, grads, n, kind):
    N = lefts[0].shape[0]
    D = grads[0].shape[1] if kind == "lefts" else lefts[0].shape[1]
    Z = lax.axis_size("z")
    if kind == "apart":
        count = len(lefts)
    else:
        count = (lefts[0] if kind == "lefts" else grads[0]).shape[1] // D
    if n % 8:
        if kind == "lefts":
            lefts, grads = [lefts[0][:, k * D : (k + 1) * D] for k in range(count)], grads * count
        elif kind == "grads":
            lefts, grads = lefts * count, [grads[0][:, k * D : (k + 1) * D] for k in range(count)]
        products = [
            lax.dot_general(a, b, (((0,), (0,)), ((), ())), preferred_element_type=F32).astype(BF16)
            for a, b in zip(lefts, grads)
        ]
        whole = jnp.stack([p.reshape(2, 2, Z, 2, n, D) for p in products], axis=3)
        c = lax.axis_index("c")
        return tuple(
            lax.dynamic_index_in_dim(whole, which, 4, keepdims=False) for which in (c, 1 - c)
        )
    out = pl.BlockSpec((4, Z, 1, n, D), lambda i: (0, 0, i, 0, 0))
    outs = [shape((4, Z, count, n, D), BF16)] * 2
    cost = (2 * count * N * D * D, 2 * count * (2 * N * D + D * D))
    room = [pltpu.VMEM((D, D), F32)]
    if kind == "apart":
        halves = run(
            k_halves_apart, 0, count, [smem(), smem()] + anywhere(2 * count), [out] * 2, outs,
            (*place, *lefts, *grads), *cost,
            [pltpu.VMEM((count, N, D), BF16)] * 2 + room + [pltpu.SemaphoreType.DMA((2 * count,))],
            (n, count),
        )
    else:
        fixed = pl.BlockSpec((N, D), lambda i: (0, 0))
        moving = pl.BlockSpec((N, D), lambda i: (0, i))
        specs = [moving, fixed] if kind == "lefts" else [fixed, moving]
        halves = run(
            k_halves_blocks, 0, count, [smem(), smem()] + specs, [out] * 2, outs,
            (*place, *lefts, *grads), *cost, room, (n,),
        )
    return tuple(a.reshape(2, 2, *a.shape[1:]) for a in halves)


def flat_grads(fm, gin, hid, gb):
    N, D = fm.shape
    B = gin.shape[1] // D
    fixed = pl.BlockSpec((N, D), lambda i: (0, 0))
    return run(
        k_flat, 0, 2 * B,
        [fixed, pl.BlockSpec((N, D), lambda i: (0, jnp.minimum(i, B - 1))),
         pl.BlockSpec((N, D), lambda i: (0, jnp.maximum(i - B, 0))), fixed],
        [pl.BlockSpec((D, D), lambda i: (0, i))], [shape((D, 2 * B * D), BF16)],
        (fm, gin, hid, gb), 4 * B * N * D * D, 4 * B * (2 * N * D + D * D),
    )[0]


def layer_backward(T, place, starts, grad, saved, vec, weights, hook):
    (x, edge, mk, mv, mr, key, value, recept, num, den, state, gated, middle, edge_two,
     fm, gm, sp, hid, vb, gl) = saved
    rate = jnp.exp(vec[5])
    outs = feed_back(T, place, grad, gl, vb, sp, middle, edge_two, vec, weights)
    gb, gg, gin, gn, first, sums_feed = hook("feed", outs)
    hook("feed grads", (hid, gb, fm, gin))
    behind = from_behind(first, -1)
    behind = hook("edge", behind)
    outs = mid_back(
        T, place, gn, behind, middle, grad, vec, weights, (key, value, recept, num, den), state
    )
    gmid, gblk, gr, gkp, gvp, gno, gdo, direct, sums_mid = hook("mid", outs)
    hook("mid grads", ((gated, gm, mr), (gblk, gg, gr)))
    direct = hook("before chain", direct)
    later = chain(direct, starts, rate, T, False)
    later = hook("chain", later)
    outs = time_back(
        T, place, x, edge, vec, weights, (key, value, num, den), state, (gkp, gvp, gno, gdo),
        later, gr,
    )
    gk, gv, gn_one, first_one, sums_time = hook("time", outs)
    hook("time grads", ((mk, mv), (gk, gv)))
    behind_one = from_behind(first_one.reshape(edge.shape), -1)
    behind_one = hook("edge two", behind_one)
    grad_in, sums_norm = norm_in_back(T, x, gn_one, behind_one, gmid, vec)
    grad_in = hook("norm", grad_in)
    return grad_in, jnp.concatenate([sums_norm, sums_time, sums_mid, sums_feed], axis=0)


VECTOR_ROWS = (0, 1, 8, 9, 10, 11, 18, 16, 17, 24, 25)


class Scattered:
    def __init__(self, product):
        out = lax.psum_scatter(product, AXES, scatter_dimension=0, tiled=True)
        self.out = out.astype(F32)


def vector_rates(row_total):
    slot = jnp.arange(row_total)
    return jnp.where((slot == 5) | (slot == 6), rate_time, rate_main)[:, None]


def adam_step(parameter, gradient, first_moment, second_moment, learning_rates, decay_weight):
    new_first = beta_one * first_moment + (1.0 - beta_one) * gradient
    new_second = beta_two * second_moment + (1.0 - beta_two) * gradient * gradient
    step_ratio = (
        new_first
        / (1.0 - beta_one**step_count)
        / (jnp.sqrt(new_second / (1.0 - beta_two**step_count)) + adam_epsilon)
    )
    return (learning_rates * (step_ratio + decay_weight * parameter), new_first, new_second)


XY, YX = (1, 2), (2, 1)


def body(tokens, cotangent, document_starts, *rest):
    weights, means, powers = rest[:5], rest[5:10], rest[10:15]
    vectors, matrices, time_output, feed_key, feed_value = weights
    R, T, D = tokens.shape
    layers, kinds, n = vectors.shape
    blocks = feed_key.shape[2] // D
    base = jnp.stack(
        [lax.axis_index(SEQ) * T, lax.axis_index("dp"), lax.axis_index("c")]
    ).astype(jnp.int32)
    place = (document_starts, base)

    def by_block(a):
        return a.reshape(n, D // n, blocks, n).transpose(0, 2, 1, 3).reshape(n, blocks * D)

    def by_device(a):
        return a.reshape(n, blocks, D // n, n).transpose(0, 2, 1, 3).reshape(n, blocks * D)

    keys = [(f"feed_key{b}", D) for b in range(blocks)]
    values = [(f"feed_value{b}", D) for b in range(blocks)]
    time_names = [("key", D), ("value", D)]
    out_names = [("recept", D), ("output", D)]
    key_names = [("gate", D)] + keys
    layout = [[time_names + [("vectors", 128)], out_names + key_names, values]]
    layout += [[time_names + out_names, key_names + values]] * (layers - 1)

    vector_columns = jnp.pad(
        vectors.reshape(layers * kinds, n).T, ((0, 0), (0, 128 - layers * kinds))
    )

    arguments = {0: (matrices, time_output, feed_key, feed_value)}

    def shard(l, names):
        matrices, time_output, feed_key, feed_value = arguments[l]
        found = {
            "key": matrices[l, 0], "value": matrices[l, 1], "recept": matrices[l, 2],
            "gate": matrices[l, 3], "output": time_output[l], "vectors": vector_columns,
        }
        for b in range(blocks):
            found[f"feed_value{b}"] = feed_value[l, b * n : (b + 1) * n]
        if ("feed_key0", D) in names:
            key_blocks = by_block(feed_key[l].astype(BF16))
            for b in range(blocks):
                found[f"feed_key{b}"] = key_blocks[:, b * D : (b + 1) * D]
        return jnp.concatenate([found[name].astype(BF16) for name, _ in names], axis=1)

    def sets_of(l, k, gate, *split):
        part = shard(l, layout[l][k])
        block = gather_seq(part, *gate)
        shards.setdefault(l, []).append(part)
        sets, at = [], 0
        for count, bits in split:
            names = layout[l][k][at : at + count]
            sets.append(Exchange(block, names, sum(w for _, w in layout[l][k][:at]), bits))
            at += count
        return sets

    def weights_of(l):
        def found():
            have = {}
            for exchange in here[l]:
                if hasattr(exchange, "other_two") or isinstance(exchange, Gathered):
                    have.update(exchange.weights())
            return have

        return found

    shards = {}
    here = [[] for _ in range(layers)]
    A = sets_of(0, 0, (), (3, XY))[0]
    O, B = sets_of(0, 1, (), (2, YX), (1 + blocks, XY))
    V = sets_of(0, 2, (A.block,), (blocks, YX))[0]
    here[0] = [A, O, B, V]
    A.prepare()
    A.first()
    for l in range(1, layers):
        arguments[l] = after(arguments[0], A.block)
        here[l] = sets_of(l, 0, (A.one,), (4, XY))
    for l in range(1, layers):
        here[l] += sets_of(l, 1, (B.block,), (1 + blocks, XY), (blocks, YX))
    A.second(O.prepare(A.block), B.prepare(A.block), *[p for l in range(1, layers) for p in shards[l]])
    O.first()
    B.first()
    A.cores(O.one, B.one)
    O.second(A.two)
    V.first(A.two)
    B.second(A.two)
    pieces, item = A.weights()["vectors"]
    d, c = lax.axis_index("dp"), lax.axis_index("c")
    block, one, two, other_one, other_two = (a[..., item[2] : item[2] + 128] for a in pieces)
    bits, half = item[5], item[4]
    mine = lax.dynamic_slice_in_dim(block, c * half, half, axis=0)
    other = lax.dynamic_slice_in_dim(block, (1 - c) * half, half, axis=0)
    by_m = {
        0: (mine, other), bits[0]: (one, other_one), bits[1]: (two[0], other_two[0]),
        bits[0] | bits[1]: (two[1], other_two[1]),
    }
    rel = jnp.stack([jnp.stack(by_m[m]) for m in range(4)])
    rel = jnp.where(c == 0, rel, rel[:, ::-1])
    columns = jnp.stack([lax.dynamic_index_in_dim(rel, d ^ j, 0, keepdims=False) for j in range(4)])
    spread = columns.reshape(D, 128)[:, : layers * kinds].astype(F32).T.reshape(layers, kinds, D)
    vecs = [jnp.pad(spread[l], ((0, 16 - kinds), (0, 0))) for l in range(layers)]

    def hook_of(l):
        more = l + 1 < layers

        def hook(name, value):
            if name == "start" and l > 0:
                M, U, S = here[l]
                value = after(value, M.two)
                M.cores(value)
                U.second(value)
            elif name == "time in" and l == 0:
                value = after(value, O.two, V.one)
                O.cores(value)
                V.second(value)
            elif name == "time in":
                M, U, S = here[l]
                value = after(value, S.one)
                S.second(value)
            elif name == "time out" and l == 0:
                value = after(value, V.two)
                V.cores(value)
                if more:
                    here[l + 1][0].first(value)
            elif name == "time out":
                M, U, S = here[l]
                value = after(value, S.two, U.two)
                S.cores(value)
                U.cores(value)
            elif name == "edge" and l == 0:
                value = after(value, B.two)
                B.cores(value)
                if more:
                    value = after(value, here[l + 1][0].one)
                    here[l + 1][0].second(value)
                    here[l + 1][1].first(value)
            elif name == "feed" and more:
                M, U, S = here[l + 1]
                value = after(value, U.one)
                S.first(value)
            return value

        return hook

    x = tokens.reshape(R * T, D)
    saved = []
    for l in range(layers):
        edge = from_behind(x.reshape(R, T, D)[:, -1], 1).astype(F32)
        x, kept = layer_forward(
            T, place, document_starts, x, edge, vecs[l], weights_of(l), hook_of(l)
        )
        saved.append(kept)
    block_out = x.astype(BF16).reshape(R, T, D)

    grad = cotangent.reshape(R * T, D)
    vec_grads = [None] * layers
    sums = [dict() for _ in range(layers)]

    def back_hook_of(l):
        own, last = sums[l], sums[l + 1] if l + 1 < layers else None

        def hook(name, value):
            feed = own.get("feed") if l == 0 else None
            if name == "feed" and last:
                value = after(value, last["mid"].got, last["time"].got)
                last["mid"].second(value[3])
                last["time"].second(value[3])
            elif name == "feed grads":
                hid, gb, fm, gin = value
                if l > 0:
                    own["ready"] = flat_grads(fm, gin, hid, gb)
                    own["feed"] = Scattered(own["ready"])
                else:
                    one = Scatter(*weight_halves(place, [hid], [gb], n, "lefts"), YX)
                    one.cores()
                    halves = weight_halves(place, [fm], [after(gin, one.mine)], n, "grads")
                    if last:
                        halves = after(halves, last["mid"].two, last["time"].two)
                    two = Scatter(*halves, XY)
                    two.cores()
                    own["feed"] = [one, two]
            elif name == "edge" and l > 0:
                value = after(value, own["ready"])
            elif name == "edge":
                value = after(value, *[s.received for s in feed])
                for s in feed:
                    s.first()
            elif name == "mid grads":
                halves = weight_halves(place, *value, n, "apart")
                if l == 0:
                    halves = after(halves, *[s.got for s in feed])
                own["mid"] = Scatter(*halves, YX)
                own["mid"].cores()
                if last:
                    own["gate"] = finish(
                        [last["mid"], last["time"]], last["feed"].out, own["mid"].mine
                    )[0]
                if l == 0:
                    for s in feed:
                        s.second()
            elif name == "before chain" and l == 0:
                value = after(value, own["mid"].received)
                own["mid"].first()
            elif name == "chain" and l > 0:
                value = after(value, own["mid"].received)
                own["mid"].first(value)
            elif name == "time":
                if l == 0:
                    value = after(value, own["mid"].got, *[s.two for s in feed])
                    own["gate"], whole = finish(feed, *[own["gate"]] * (layers > 1))
                    value = after(value, whole)
            elif name == "time grads":
                own["time"] = Scatter(*weight_halves(place, *value, n, "apart"), XY if l else YX)
                own["time"].cores()
            elif name == "edge two" and l == 0:
                own["time"].first()
                own["mid"].second(own["time"].sent)
                value = after(value, own["time"].sent)
            elif name == "norm" and l > 0:
                value = after(value, own["time"].received)
                own["time"].first()
            return value

        return hook

    for l in reversed(range(layers)):
        grad, vec_grads[l] = layer_backward(
            T, place, document_starts, grad, saved[l], vecs[l], weights_of(l)(), back_hook_of(l)
        )
    vec_columns = jnp.concatenate(vec_grads, axis=0).astype(BF16).T
    vec_columns = jnp.pad(vec_columns, ((0, 0), (0, 128 - vec_columns.shape[1])))
    vec_view = vec_columns.reshape(2, 2, lax.axis_size("z"), 1, 2, n, 128)
    vec_sum = Scatter(
        *[lax.dynamic_index_in_dim(vec_view, w, 4, keepdims=False) for w in (c, 1 - c)], XY
    )
    tail = sums[0]
    vec_sum.cores()
    vec_sum.first(tail["time"].got)
    tail["time"].second()
    vec_sum.second(tail["gate"])
    _, whole = finish([tail["mid"], tail["time"], vec_sum])
    for l in range(1, layers):
        for e in (sums[l]["feed"], sums[l]["mid"], sums[l]["time"]):
            e.out = after(e.out, whole)
    for e in tail["feed"]:
        e.out = after(e.out, whole)
    g_vec = vec_sum.out[0]
    grads = []
    for l in range(layers):
        if l > 0:
            feed = sums[l]["feed"].out
            g_fk, g_fv = feed[:, : blocks * D], feed[:, blocks * D :]
            g_fv = jnp.concatenate([g_fv[:, b * D : (b + 1) * D] for b in range(blocks)], axis=0)
        else:
            g_fv, g_fk = (s.out for s in sums[l]["feed"])
            g_fv, g_fk = g_fv.reshape(-1, D), jnp.concatenate(list(g_fk), axis=1)
        g_out, g_gate, g_recept = sums[l]["mid"].out
        g_key, g_value = sums[l]["time"].out
        grads.append(
            (
                g_vec[:, [32 * l + k for k in VECTOR_ROWS]].T,
                jnp.stack([g_key, g_value, g_recept, g_gate]),
                g_out,
                by_device(g_fk),
                g_fv,
            )
        )
    totals = tuple(jnp.stack([g[m] for g in grads]) for m in range(5))
    rates = (vector_rates(kinds),) + (rate_main,) * 4
    decays = (0.0,) + (weight_decay,) * 4
    new = [adam_step(*z) for z in zip(weights, totals, means, powers, rates, decays)]
    return (
        block_out,
        grad.reshape(R, T, D),
        *totals,
        *[z[0] for z in new],
        *[z[1] for z in new],
        *[z[2] for z in new],
    )


def solution(mesh):
    dp, seq = mesh.shape["dp"], mesh.shape["seq"]
    mesh = Mesh(mesh.devices.reshape(dp, seq // 2, 2), AXES)
    tokens = P("dp", SEQ, None)
    group = (
        P(None, None, AXES),
        P(None, None, AXES, None),
        P(None, AXES, None),
        P(None, AXES, None),
        P(None, AXES, None),
    )
    in_specs = (tokens, tokens, P("dp", None)) + group * 3
    out_specs = (tokens, tokens) + group * 4
    return jax.shard_map(body, mesh=mesh, in_specs=in_specs, out_specs=out_specs, check_vma=False)
```

```python
import jax
import jax.numpy as jnp
from jax import lax
from jax.experimental import pallas as pl
from jax.experimental.pallas import tpu as pltpu
from jax.sharding import Mesh, PartitionSpec as P

norm_epsilon = 1e-05
beta_one = 0.9
beta_two = 0.99
adam_epsilon = 1e-08
step_count = 10
rate_main = 0.0006
rate_time = 0.0012
weight_decay = 0.1

RB = 2
COST = 20
VMEM = 54 * 1024 * 1024
F32, BF16 = jnp.float32, jnp.bfloat16


def dot_nn(a, b):
    return lax.dot_general(a, b, (((1,), (0,)), ((), ())), preferred_element_type=F32)


def dot_nt(a, b):
    return lax.dot_general(a, b, (((1,), (1,)), ((), ())), preferred_element_type=F32)


def dot_tn(a, b):
    return lax.dot_general(a, b, (((0,), (0,)), ((), ())), preferred_element_type=F32)


def colsum(a):
    return jnp.sum(a, axis=0, keepdims=True)


LANES = 128


def columns(D):
    return [slice(j, j + LANES) for j in range(0, D, LANES)]


def place_of(starts_ref, base_ref, row, T):
    local = lax.broadcasted_iota(jnp.int32, (T, LANES), 0)
    base = base_ref[0]
    begin = jnp.zeros((T, LANES), jnp.int32)
    last_begin = jnp.int32(0)
    for j in range(starts_ref.shape[1]):
        s = starts_ref[row, j]
        begin = jnp.where(local + base >= s, jnp.maximum(begin, s), begin)
        last_begin = jnp.where(base + T - 1 >= s, jnp.maximum(last_begin, s), last_begin)
    dist = local + base - begin
    tail = (local + base >= last_begin).astype(F32)
    return local, dist, tail


def levels(T):
    k = 1
    while k < T:
        yield k
        k *= 2


def keeps_of(local, dist, T):
    return [((dist >= k) & (local >= k)).astype(F32) for k in levels(T)]


def lane_mean(total, D):
    return jnp.broadcast_to(jnp.sum(total, axis=-1, keepdims=True) * (1.0 / D), total.shape)


def norm_stats(x, rows, D):
    mean = lane_mean(sum(x[rows, c].astype(F32) for c in columns(D)), D)
    spread = [x[rows, c].astype(F32) - mean for c in columns(D)]
    rstd = lax.rsqrt(lane_mean(sum(s * s for s in spread), D) + norm_epsilon)
    return mean, rstd


def norm_rows(x, gain, bias):
    centred = x - jnp.mean(x, axis=-1, keepdims=True)
    rstd = lax.rsqrt(jnp.mean(centred * centred, axis=-1, keepdims=True) + norm_epsilon)
    return centred * rstd * gain + bias


def previous_of(normalized, edge, local, joined):
    return jnp.where(local == 0, edge, pltpu.roll(normalized, 1, 0)) * joined


def mixed(x, rows, c, stats, vec, gain_row, edge, local, joined):
    mean, rstd = stats
    normalized = (x[rows, c].astype(F32) - mean) * rstd * vec[gain_row : gain_row + 1, c]
    normalized = normalized + vec[gain_row + 1 : gain_row + 2, c]
    previous = previous_of(normalized, edge, local, joined)
    return previous, normalized - previous


def shift_up(masked, local, T):
    return jnp.where(local == T - 1, 0.0, pltpu.roll(masked, T - 1, 0))


def scan_down(pair, rate, keeps, T):
    for k, keep in zip(levels(T), keeps):
        weight = keep * jnp.exp(-float(k) * rate)
        pair = tuple(a + weight * pltpu.roll(a, k, 0) for a in pair)
    return pair


def scan_up(pair, rate, keeps, T):
    for k, keep in zip(levels(T), keeps):
        weight = keep * jnp.exp(-float(k) * rate)
        pair = tuple(a + pltpu.roll(weight * a, T - k, 0) for a in pair)
    return pair


def piece_copies(base, pieces, item, target, sems, at):
    count, first_in_block, first, width, rows, bits = item
    columns = pl.ds(first, width)
    if count == 1:
        return [(0, pltpu.make_async_copy(pieces[0].at[:, pl.ds(first_in_block, width)], target, sems.at[at]))]
    block, one, two, other_one, other_two = pieces
    d, c = base[1], base[2]
    copies = []
    for half, first_ref, second_ref in ((c, one, two), (1 - c, other_one, other_two)):
        start = pl.multiple_of(half * rows, rows)
        for source, m in (
            (block.at[pl.ds(start, rows), pl.ds(first_in_block, width)], 0),
            (first_ref.at[:, columns], bits[0]),
            (second_ref.at[0, :, columns], bits[1]),
            (second_ref.at[1, :, columns], bits[0] | bits[1]),
        ):
            row = pl.multiple_of(((d ^ m) * 2 + half) * rows, rows)
            copies.append(
                (m, pltpu.make_async_copy(
                    source, target.at[pl.ds(row, rows)], sems.at[at + len(copies)]
                ))
            )
    return copies


def split_refs(items, refs):
    groups, at = [], 0
    for count in items:
        groups.append(refs[at : at + count])
        at += count
    return groups, refs[at:]


def k_time_in(items, T, starts, base, x, edge, vec, *refs):
    (pieces,), (mk, mv, mr, ko, vo, no, do, last, w, sems) = split_refs([items[0][0]], refs)
    D = x.shape[1]
    i = pl.program_id(0)
    copies = [
        copy
        for s, item in enumerate(items)
        for copy in piece_copies(base, pieces, item, w.at[s], sems, 8 * s)
    ]

    @pl.when(i == 0)
    def _():
        for _, copy in copies:
            copy.start()

    edge_norm = norm_rows(edge[0], vec[0:1], vec[1:2])
    places = [place_of(starts, base, i * RB + q, T) for q in range(RB)]
    for q, (local, dist, _) in enumerate(places):
        rows = slice(q * T, q * T + T)
        joined = (dist >= 1).astype(F32)
        stats = norm_stats(x, rows, D)
        for c in columns(D):
            previous, change = mixed(
                x, rows, c, stats, vec, 0, edge_norm[q : q + 1, c], local, joined
            )
            for j, out in ((2, mk), (3, mv), (4, mr)):
                out[rows, c] = (previous + change * vec[j : j + 1, c]).astype(BF16)

    @pl.when(i == 0)
    def _():
        for _, copy in copies:
            copy.wait()

    ko[...] = dot_nn(mk[...], w[0])
    vo[...] = dot_nn(mv[...], w[1]).astype(vo.dtype)
    for q, (local, dist, _) in enumerate(places):
        rows = slice(q * T, q * T + T)
        keeps = keeps_of(local, dist, T)
        for c in columns(D):
            rate = jnp.exp(vec[5:6, c])
            weight = jnp.exp(ko[rows, c])
            sums = scan_down((weight * vo[rows, c].astype(F32), weight), rate, keeps, T)
            for side, (out, total) in enumerate(zip((no, do), sums)):
                out[rows, c] = (keeps[0] * pltpu.roll(total, 1, 0)).astype(out.dtype)
                last[q, side : side + 1, c] = total[T - 1 : T]


def decay_state(vec, c, key, value, num, den, state, local, dist):
    rate = jnp.exp(vec[5:6, c])
    fade = (dist >= local + 1).astype(F32) * jnp.exp(-local.astype(F32) * rate)
    full_n = num.astype(F32) + fade * state[0:1]
    full_d = den.astype(F32) + fade * state[1:2]
    extra = jnp.exp(vec[6:7, c] + key)
    inverse = 1.0 / (full_d + extra)
    mean = (full_n + extra * value) * inverse
    return full_n, full_d, extra, inverse, mean


def k_time_out(items, T, starts, base, x, key, value, mr, num, den, state, vec, *refs):
    (pieces,), (gated, middle, recept, w, sems) = split_refs([items[0][0]], refs)
    D = x.shape[1]
    i = pl.program_id(0)
    copies = [
        copy
        for s, item in enumerate(items)
        for copy in piece_copies(base, pieces, item, w.at[s], sems, 8 * s)
    ]

    @pl.when(i == 0)
    def _():
        for _, copy in copies:
            copy.start()

    @pl.when(i == 0)
    def _():
        for _, copy in copies:
            copy.wait()

    recept[...] = dot_nn(mr[...], w[0]).astype(BF16)
    for q in range(RB):
        local, dist, _ = place_of(starts, base, i * RB + q, T)
        rows = slice(q * T, q * T + T)
        for c in columns(D):
            mean = decay_state(
                vec, c, key[rows, c], value[rows, c].astype(F32), num[rows, c], den[rows, c], state[q, :, c],
                local, dist,
            )[4]
            gated[rows, c] = (jax.nn.sigmoid(recept[rows, c].astype(F32)) * mean).astype(BF16)

    middle[...] = x[...].astype(F32) + dot_nn(gated[...], w[1])


def feed_copies(items, base, pieces, wg, wk, wv, sems):
    items = items[1:]

    def copies(index, target, at):
        group, item = items[index]
        return piece_copies(base, pieces[group], item, target, sems, at)

    blocks = (len(items) - 1) // 2
    pairs = [
        copies(1 + b, wk.at[b], 8 + 16 * b) + copies(1 + blocks + b, wv.at[b], 16 + 16 * b)
        for b in range(blocks)
    ]
    return copies(0, wg, 0), pairs


def feed_start(copies):
    gate, pairs = copies
    for _, copy in [z for block in pairs for z in block] + gate:
        copy.start()


def feed_wait(copies, j):
    for b, block in enumerate(copies[1]):

        @pl.when(j == b)
        def _():
            for _, copy in block:
                copy.wait()


def k_feed(items, T, starts, base, middle, edge, vec, *refs):
    pieces, (fm, gm, sp, hid, vb, gl, xo, acc, wg, wk, wv, sems) = split_refs(items[0], refs)
    M, D = middle.shape
    j = pl.program_id(0)
    copies = feed_copies(items, base, pieces, wg, wk, wv, sems)

    @pl.when(j == 0)
    def _():
        feed_start(copies)
        edge_norm = norm_rows(edge[...], vec[7:8], vec[8:9])
        for q in range(M // T):
            local, dist, _ = place_of(starts, base, q, T)
            rows = slice(q * T, q * T + T)
            joined = (dist >= 1).astype(F32)
            stats = norm_stats(middle, rows, D)
            for c in columns(D):
                previous, change = mixed(
                    middle, rows, c, stats, vec, 7, edge_norm[q : q + 1, c], local, joined
                )
                fm[rows, c] = (previous + change * vec[9:10, c]).astype(BF16)
                gm[rows, c] = (previous + change * vec[10:11, c]).astype(BF16)
        acc[...] = jnp.zeros_like(acc)

    feed_wait(copies, j)
    pre = dot_nn(fm[...], wk[j])
    soft = jnp.maximum(pre, 0.0) + jnp.log(1.0 + jnp.exp(-jnp.abs(pre)))
    sp[...] = soft.astype(BF16)
    hidden = (soft * soft).astype(BF16)
    hid[...] = hidden
    acc[...] += dot_nn(hidden, wv[j])

    @pl.when(j == pl.num_programs(0) - 1)
    def _():
        for _, copy in copies[0]:
            copy.wait()
        gate = dot_nn(gm[...], wg[...])
        gl[...] = gate.astype(BF16)
        vb[...] = acc[...].astype(BF16)
        xo[...] = middle[...] + jax.nn.sigmoid(gate) * acc[...]


def k_feed_back(items, T, starts, base, grad, gl, vb, sp, middle, edge, vec, *refs):
    pieces, (gb, gg, gin, gn, first, sums, acc, gc, wg, wk, wv, sems) = split_refs(
        items[0], refs
    )
    M, D = middle.shape
    j = pl.program_id(0)
    copies = feed_copies(items, base, pieces, wg, wk, wv, sems)

    @pl.when(j == 0)
    def _():
        feed_start(copies)
        g = grad[...].astype(F32)
        s = jax.nn.sigmoid(gl[...].astype(F32))
        gb[...] = (g * s).astype(BF16)
        gg[...] = (g * vb[...].astype(F32) * s * (1.0 - s)).astype(BF16)
        acc[...] = jnp.zeros_like(acc)

    feed_wait(copies, j)
    soft = sp[...].astype(F32)
    gh = dot_nt(gb[...], wv[j])
    pre = (gh * (2.0 * soft * (1.0 - jnp.exp(-soft)))).astype(BF16)
    gin[...] = pre
    acc[...] += dot_nt(pre, wk[j])

    @pl.when(j == pl.num_programs(0) - 1)
    def _():
        for _, copy in copies[0]:
            copy.wait()
        gc[...] = dot_nt(gg[...], wg[...])
        edge_norm = norm_rows(edge[...], vec[7:8], vec[8:9])
        sums[...] = jnp.zeros_like(sums)
        for q in range(M // T):
            local, dist, _ = place_of(starts, base, q, T)
            rows = slice(q * T, q * T + T)
            joined = (dist >= 1).astype(F32)
            stats = norm_stats(middle, rows, D)
            for c in columns(D):
                _, change = mixed(
                    middle, rows, c, stats, vec, 7, edge_norm[q : q + 1, c], local, joined
                )
                ga, gb_ = acc[rows, c], gc[rows, c]
                sums[0:1, c] += colsum(ga * change)
                sums[1:2, c] += colsum(gb_ * change)
                direct = ga * vec[9:10, c] + gb_ * vec[10:11, c]
                masked = (ga + gb_ - direct) * joined
                gn[rows, c] = (direct + shift_up(masked, local, T)).astype(gn.dtype)
                first[q : q + 1, c] = masked[0:1]


def norm_back(x, rows, gain_row, vec, total, sums, D, put):
    mean, rstd = norm_stats(x, rows, D)
    one = two = None
    for c in columns(D):
        hat = (x[rows, c].astype(F32) - mean) * rstd
        g = total(c)
        scaled = g * vec[gain_row : gain_row + 1, c]
        sums[0:1, c] += colsum(g * hat)
        sums[1:2, c] += colsum(g)
        one = scaled if one is None else one + scaled
        two = scaled * hat if two is None else two + scaled * hat
    one, two = lane_mean(one, D), lane_mean(two, D)
    for c in columns(D):
        hat = (x[rows, c].astype(F32) - mean) * rstd
        put(c, rstd * (total(c) * vec[gain_row : gain_row + 1, c] - one - hat * two))


def with_edge(gn, rows, edge, local, T):
    return lambda c: gn[rows, c].astype(F32) + jnp.where(local == T - 1, edge[:, c], 0.0)


def k_mid_back(items, T, starts, base, gn, edge, middle, grad, vec,
               key, value, recept, num, den, state, *refs):
    (pieces,), rest = split_refs([items[0][0]], refs)
    gm, gblk, gr, gkp, gvp, gno, gdo, direct, sums, ggated, w, sems = rest
    D = middle.shape[1]
    i = pl.program_id(0)
    copies = piece_copies(base, pieces, items[0], w, sems, 0)

    @pl.when(i == 0)
    def _():
        for _, copy in copies:
            copy.start()
        sums[...] = jnp.zeros_like(sums)

    places = [place_of(starts, base, i * RB + q, T) for q in range(RB)]
    for q, (local, dist, _) in enumerate(places):
        rows = slice(q * T, q * T + T)

        def put(c, gx):
            gmid = grad[rows, c].astype(F32) + gx
            gm[rows, c] = gmid
            gblk[rows, c] = gmid.astype(BF16)

        total = with_edge(gn, rows, edge[0, q : q + 1], local, T)
        norm_back(middle, rows, 7, vec, total, sums, D, put)

    @pl.when(i == 0)
    def _():
        for _, copy in copies:
            copy.wait()

    ggated[...] = dot_nt(gblk[...], w[...])
    for q, (local, dist, _) in enumerate(places):
        rows = slice(q * T, q * T + T)
        joined = (dist >= 1).astype(F32)
        keeps = keeps_of(local, dist, T)
        for c in columns(D):
            v, g = value[rows, c].astype(F32), ggated[rows, c]
            _, _, extra, inverse, mean = decay_state(
                vec, c, key[rows, c], v, num[rows, c], den[rows, c], state[q, :, c], local, dist
            )
            s = jax.nn.sigmoid(recept[rows, c].astype(F32))
            gr[rows, c] = (g * mean * s * (1.0 - s)).astype(BF16)
            r = g * s * inverse
            ge = extra * r * (v - mean)
            gkp[rows, c] = ge.astype(gkp.dtype)
            gvp[rows, c] = (r * extra).astype(gvp.dtype)
            sums[2:3, c] += colsum(ge)
            rate = jnp.exp(vec[5:6, c])
            totals = scan_up((r, -r * mean), rate, keeps, T)
            for side, (out, a) in enumerate(zip((gno, gdo), totals)):
                out[rows, c] = pltpu.roll(keeps[0] * a, T - 1, 0).astype(out.dtype)
                direct[q, side : side + 1, c] = (joined * a)[0:1]


def k_time_back(items, T, starts, base, x, edge, vec, key, value, num, den, state,
                gkp, gvp, gno, gdo, after, gr, *refs):
    pieces, (gk, gv, gn, first, sums, mixes, w, sems) = split_refs(items[0], refs)
    D = x.shape[1]
    i = pl.program_id(0)
    copies = [
        copy
        for s, (group, item) in enumerate(items[1:])
        for copy in piece_copies(base, pieces[group], item, w.at[s], sems, 8 * s)
    ]

    @pl.when(i == 0)
    def _():
        for _, copy in copies:
            copy.start()
        sums[...] = jnp.zeros_like(sums)

    places = [place_of(starts, base, i * RB + q, T) for q in range(RB)]
    for q, (local, dist, tail) in enumerate(places):
        rows = slice(q * T, q * T + T)
        inside = (dist >= local + 1).astype(F32)
        for c in columns(D):
            rate = jnp.exp(vec[5:6, c])
            fade = inside * jnp.exp(-local.astype(F32) * rate)
            full_n = num[rows, c].astype(F32) + fade * state[q, 0:1, c]
            full_d = den[rows, c].astype(F32) + fade * state[q, 1:2, c]
            left = tail * jnp.exp(-(T - 1 - local).astype(F32) * rate)
            grad_n = gno[rows, c].astype(F32) + left * after[q, 0:1, c]
            grad_d = gdo[rows, c].astype(F32) + left * after[q, 1:2, c]
            weight = jnp.exp(key[rows, c])
            gk[rows, c] = (
                gkp[rows, c].astype(F32) + weight * (grad_n * value[rows, c].astype(F32) + grad_d)
            ).astype(BF16)
            gv[rows, c] = (gvp[rows, c].astype(F32) + weight * grad_n).astype(BF16)
            turn = colsum(grad_n * full_n + grad_d * full_d)
            sums[3:4, c] += -rate * jnp.exp(-rate) * turn

    @pl.when(i == 0)
    def _():
        for _, copy in copies:
            copy.wait()

    for s, g in enumerate((gk, gv, gr)):
        mixes[s] = dot_nt(g[...], w[s])
    edge_norm = norm_rows(edge[0], vec[0:1], vec[1:2])
    for q, (local, dist, _) in enumerate(places):
        rows = slice(q * T, q * T + T)
        joined = (dist >= 1).astype(F32)
        stats = norm_stats(x, rows, D)
        for c in columns(D):
            _, change = mixed(x, rows, c, stats, vec, 0, edge_norm[q : q + 1, c], local, joined)
            gs = [mixes[s, rows, c] for s in range(3)]
            for s in range(3):
                sums[s : s + 1, c] += colsum(gs[s] * change)
            direct = sum(g * vec[2 + s : 3 + s, c] for s, g in enumerate(gs))
            masked = (gs[0] + gs[1] + gs[2] - direct) * joined
            gn[rows, c] = (direct + shift_up(masked, local, T)).astype(gn.dtype)
            first[0, q : q + 1, c] = masked[0:1]


def k_norm_back(T, x, gn, edge, gmid, vec, go, sums):
    i = pl.program_id(0)
    D = x.shape[1]

    @pl.when(i == 0)
    def _():
        sums[...] = jnp.zeros_like(sums)

    local = lax.broadcasted_iota(jnp.int32, (T, LANES), 0)
    for q in range(RB):
        rows = slice(q * T, q * T + T)

        def put(c, gx):
            go[rows, c] = gmid[rows, c] + gx

        total = with_edge(gn, rows, edge[0, q : q + 1], local, T)
        norm_back(x, rows, 0, vec, total, sums, D, put)


def put_halves(base, product, n, mine, send):
    pairs = product.shape[0] // (2 * n)
    lead, Z = mine.shape[0], mine.shape[1]
    for p in range(pairs):
        for out, half in ((mine, base[2]), (send, 1 - base[2])):
            start = pl.multiple_of((2 * p + half) * n, 8)
            out[p // Z, p % Z, 0] = product[pl.ds(start, n), :].astype(BF16)


def k_halves_apart(n, count, T, starts, base, *refs):
    lefts, grads, rest = refs[:count], refs[count : 2 * count], refs[2 * count :]
    mine, send, left, grad, product, sems = rest
    i = pl.program_id(0)
    pairs = [
        [
            pltpu.make_async_copy(source, target.at[k], sems.at[2 * k + side])
            for side, (source, target) in enumerate(((lefts[k], left), (grads[k], grad)))
        ]
        for k in range(count)
    ]

    @pl.when(i == 0)
    def _():
        for pair in pairs:
            for copy in pair:
                copy.start()

    for k, pair in enumerate(pairs):

        @pl.when(i == k)
        def _():
            for copy in pair:
                copy.wait()

    product[...] = dot_tn(left[i], grad[i])
    put_halves(base, product, n, mine, send)


def k_halves_blocks(n, T, starts, base, left, grad, mine, send, product):
    product[...] = dot_tn(left[...], grad[...])
    put_halves(base, product, n, mine, send)


def k_flat(T, fm, gin, hid, gb, out):
    i = pl.program_id(0)
    half = pl.num_programs(0) // 2

    @pl.when(i < half)
    def _():
        out[...] = dot_tn(fm[...], gin[...]).astype(BF16)

    @pl.when(i >= half)
    def _():
        out[...] = dot_tn(hid[...], gb[...]).astype(BF16)


def smem():
    return pl.BlockSpec(memory_space=pltpu.SMEM)


def rows_spec(T, D):
    return pl.BlockSpec((RB * T, D), lambda i: (i, 0))


def col_spec(rows, width, at):
    return pl.BlockSpec((rows, width), lambda i: (0, at))


def whole_spec(shape):
    zeros = (0,) * len(shape)
    return pl.BlockSpec(shape, lambda i: zeros)


def edge_spec(D):
    return pl.BlockSpec((1, RB, D), lambda i: (i, 0, 0))


def state_spec(D):
    return pl.BlockSpec((RB, 2, D), lambda i: (i, 0, 0))


def shape(dims, kind):
    return jax.ShapeDtypeStruct(dims, kind)


def run(kernel, T, grid, in_specs, out_specs, outs, args, flops, moved, scratch=(), items=(),
        after=()):
    count = len(args)
    in_specs = in_specs + anywhere(len(after))
    args = args + tuple(after)

    def body(*refs):
        kernel(*(items if isinstance(items, tuple) else (items,) if items else ()), T, *refs[:count], *refs[count + len(after) :])

    return pl.pallas_call(
        body,
        grid=(grid,),
        in_specs=in_specs,
        out_specs=out_specs,
        out_shape=outs,
        scratch_shapes=scratch,
        compiler_params=pltpu.CompilerParams(
            dimension_semantics=("arbitrary",), vmem_limit_bytes=VMEM
        ),
        cost_estimate=pl.CostEstimate(
            flops=flops // COST, bytes_accessed=moved // COST, transcendentals=0
        ),
        name=kernel.__name__,
    )(*args)


def anywhere(count):
    return [pl.BlockSpec(memory_space=pl.ANY)] * count


def weight_room(shapes, copies):
    return [pltpu.VMEM(s, BF16) for s in shapes] + [pltpu.SemaphoreType.DMA((copies,))]


def time_in(T, place, x, edge, vec, weights, after=()):
    N, D = x.shape
    R = N // T
    rs = rows_spec(T, D)
    pieces = weights["key"][0]
    items = [weights[name][1] for name in ("key", "value")]
    return run(
        k_time_in, T, R // RB,
        [smem(), smem(), rs, edge_spec(D), whole_spec(vec.shape)] + anywhere(len(pieces)),
        [rs] * 7 + [state_spec(D)],
        [shape((N, D), BF16)] * 3 + [shape((N, D), F32)] + [shape((N, D), BF16)] * 3
        + [shape((R, 2, D), F32)],
        (*place, x, edge.reshape(R // RB, RB, D), vec, *pieces),
        4 * N * D * D, 40 * N * D,
        weight_room([(2, D, D)], 16), items, after,
    )


def time_out(T, place, x, kept, state, vec, weights, after=()):
    N, D = x.shape
    R = N // T
    rs = rows_spec(T, D)
    pieces = weights["output"][0]
    items = [weights[name][1] for name in ("recept", "output")]
    return run(
        k_time_out, T, R // RB,
        [smem(), smem()] + [rs] * 6 + [state_spec(D), whole_spec(vec.shape)] + anywhere(len(pieces)),
        [rs] * 3,
        [shape((N, D), BF16), shape((N, D), F32), shape((N, D), BF16)],
        (*place, x, *kept, state, vec, *pieces),
        4 * N * D * D, 30 * N * D,
        weight_room([(2, D, D)], 16), items, after,
    )


def grouped(weights, names):
    groups, items = [], []
    for name in names:
        pieces, item = weights[name]
        found = [k for k, group in enumerate(groups) if group is pieces]
        if not found:
            found = [len(groups)]
            groups.append(pieces)
        items.append((found[0], item))
    pieces = tuple(piece for group in groups for piece in group)
    return [[len(group) for group in groups]] + items, pieces


def feed_weights(weights):
    keys, values = (
        sorted(name for name in weights if name.startswith(kind)) for kind in ("feed_key", "feed_value")
    )
    return grouped(weights, ["gate"] + keys + values)


def feed(T, place, middle, edge, vec, weights, after=()):
    N, D = middle.shape
    items, pieces = feed_weights(weights)
    B = (len(items) - 2) // 2
    F = B * D
    whole = whole_spec((N, D))
    wide_spec = pl.BlockSpec((N, D), lambda j: (0, j))
    return run(
        k_feed, T, B,
        [smem(), smem(), whole, whole_spec(edge.shape), whole_spec(vec.shape)] + anywhere(len(pieces)),
        [whole, whole, wide_spec, wide_spec, whole, whole, whole],
        [shape((N, D), BF16)] * 2 + [shape((N, F), BF16)] * 2 + [shape((N, D), BF16)] * 2
        + [shape((N, D), F32)],
        (*place, middle, edge, vec, *pieces),
        4 * N * D * F + 2 * N * D * D, 20 * N * D + 4 * N * F + 4 * D * F,
        [pltpu.VMEM((N, D), F32)]
        + weight_room([(D, D), (B, D, D), (B, D, D)], 8 * len(items)), items, after,
    )


def feed_back(T, place, grad, gl, vb, sp, middle, edge, vec, weights, after=()):
    N, D = middle.shape
    items, pieces = feed_weights(weights)
    B = (len(items) - 2) // 2
    F = B * D
    R = N // T
    whole = whole_spec((N, D))
    wide_spec = pl.BlockSpec((N, D), lambda j: (0, j))
    return run(
        k_feed_back, T, B,
        [smem(), smem(), whole, whole, whole, wide_spec, whole, whole_spec(edge.shape),
         whole_spec(vec.shape)] + anywhere(len(pieces)),
        [whole, whole, wide_spec, whole, whole_spec((R, D)), whole_spec((8, D))],
        [shape((N, D), BF16)] * 2 + [shape((N, F), BF16), shape((N, D), BF16)]
        + [shape((R, D), F32), shape((8, D), F32)],
        (*place, grad, gl, vb, sp, middle, edge, vec, *pieces),
        4 * N * D * F + 2 * N * D * D, 20 * N * D + 4 * N * F + 4 * D * F,
        [pltpu.VMEM((N, D), F32)] * 2
        + weight_room([(D, D), (B, D, D), (B, D, D)], 8 * len(items)), items, after,
    )


def mid_back(T, place, gn, edge, middle, grad, vec, weights, kept, state, after=()):
    N, D = middle.shape
    R = N // T
    rs = rows_spec(T, D)
    pieces, item = weights["output"]
    return run(
        k_mid_back, T, R // RB,
        [smem(), smem(), rs, edge_spec(D), rs, rs, whole_spec(vec.shape)]
        + [rs] * 5 + [state_spec(D)] + anywhere(len(pieces)),
        [rs] * 7 + [state_spec(D), whole_spec((8, D))],
        [shape((N, D), F32)] + [shape((N, D), BF16)] * 6
        + [shape((R, 2, D), F32), shape((8, D), F32)],
        (*place, gn, edge.reshape(R // RB, RB, D), middle, grad, vec, *kept, state, *pieces),
        2 * N * D * D, 50 * N * D,
        [pltpu.VMEM((RB * T, D), F32)] + weight_room([(D, D)], 8), [item], after,
    )


def time_back(T, place, x, edge, vec, weights, kept, state, part, later, gr, after=()):
    N, D = x.shape
    R = N // T
    rs = rows_spec(T, D)
    items, pieces = grouped(weights, ("key", "value", "recept"))
    return run(
        k_time_back, T, R // RB,
        [smem(), smem(), rs, edge_spec(D), whole_spec(vec.shape)]
        + [rs] * 4 + [state_spec(D)] + [rs] * 4 + [state_spec(D), rs] + anywhere(len(pieces)),
        [rs] * 3 + [edge_spec(D), whole_spec((8, D))],
        [shape((N, D), BF16)] * 3
        + [shape((R // RB, RB, D), F32), shape((8, D), F32)],
        (*place, x, edge.reshape(R // RB, RB, D), vec, *kept, state, *part, later, gr, *pieces),
        6 * N * D * D, 50 * N * D,
        [pltpu.VMEM((3, RB * T, D), F32)] + weight_room([(3, D, D)], 24), items, after,
    )


def norm_in_back(T, x, gn, edge, gmid, vec, after=()):
    N, D = x.shape
    R = N // T
    rs = rows_spec(T, D)
    return run(
        k_norm_back, T, R // RB,
        [rs, rs, edge_spec(D), rs, whole_spec(vec.shape)],
        [rs, whole_spec((8, D))],
        [shape((N, D), F32), shape((8, D), F32)],
        (x, gn, edge.reshape(R // RB, RB, D), gmid, vec),
        0, 16 * N * D, after=after,
    )


SEQ = ("z", "c")
AXES = ("dp", "z", "c")
SWAP = [(0, 1), (1, 0)]


def by_bit(block, bit):
    return lax.ppermute(block, "dp", [(i, i ^ bit) for i in range(lax.axis_size("dp"))])


def after(value, *others):
    return lax.optimization_barrier((value, *others))[0]


def gather_seq(part, *gate):
    return lax.all_gather(after(part, *gate), SEQ, axis=0, tiled=True)


class Gathered:
    def __init__(self, part, names, *gate):
        self.block = lax.all_gather(after(part, *gate), AXES, axis=0, tiled=True)
        self.names = names

    def weights(self):
        pieces, at, found = (self.block,), 0, {}
        for name, width in self.names:
            found[name] = (pieces, (1, at, 0, width, 0, (0, 0)))
            at += width
        return found


class Exchange:
    def __init__(self, block, names, start, bits):
        self.block, self.names, self.start, self.bits = block, names, start, bits
        self.width = sum(width for _, width in names)
        self.rows = block.shape[0] // 2

    def prepare(self, *gate):
        block = after(self.block, *gate)
        self.own = lax.dynamic_slice(
            block, (lax.axis_index("c") * self.rows, self.start), (self.rows, self.width)
        )
        return self.own

    def first(self, *gate):
        own = self.prepare(*gate) if gate else self.own
        self.one = by_bit(own, self.bits[0])
        return self.one

    def second(self, *gate):
        one = after(self.one, *gate)
        self.two = by_bit(jnp.stack([self.own, one]), self.bits[1])
        return self.two

    def cores(self, *gate):
        self.one, self.two = after((self.one, self.two), *gate)
        self.other_one = lax.ppermute(self.one, "c", SWAP)
        self.other_two = lax.ppermute(self.two, "c", SWAP)

    def weights(self):
        if not hasattr(self, "pieces"):
            self.pieces = (self.block, self.one, self.two, self.other_one, self.other_two)
        pieces, at, found = self.pieces, 0, {}
        for name, width in self.names:
            found[name] = (pieces, (5, self.start + at, at, width, self.rows, self.bits))
            at += width
        return found


class Scatter:
    def __init__(self, mine, send, bits):
        self.mine, self.send, self.bits = mine, send, bits

    def part(self, a, y, x):
        if y is not None:
            a = lax.dynamic_index_in_dim(a, y, 0, keepdims=True)
        if x is not None:
            a = lax.dynamic_index_in_dim(a, x, 1, keepdims=True)
        return a.astype(F32)

    def cores(self, *gate):
        self.received = lax.ppermute(after(self.send, *gate), "c", SWAP)
        return self.received

    def first(self, *gate):
        d = lax.axis_index("dp")
        y, x = d // 2, d % 2
        terms = after((self.mine, self.received), *gate)
        place = (1 - y, None) if self.bits[1] == 2 else (None, 1 - x)
        self.sent = sum(self.part(a, *place) for a in terms).astype(BF16)
        self.got = by_bit(self.sent, self.bits[1])
        return self.got

    def second(self, *gate):
        d = lax.axis_index("dp")
        y, x = d // 2, d % 2
        terms = after((self.mine, self.received, self.got), *gate)

        def total(y, x):
            got = self.part(terms[2], *((None, x) if self.bits[1] == 2 else (y, None)))
            return self.part(terms[0], y, x) + self.part(terms[1], y, x) + got

        there = (y, 1 - x) if self.bits[1] == 2 else (1 - y, x)
        self.two = by_bit(total(*there).astype(BF16), self.bits[0])
        self.keep = lambda two: (total(y, x) + two.astype(F32)).astype(BF16)
        return self.two


def finish(scatters, *gate):
    parts, shapes = [], []
    width = max(s.mine.shape[-1] for s in scatters)
    for scatter in scatters:
        total = scatter.keep(after(scatter.two, *gate))[0, 0]
        Z, I, n, C = total.shape
        if C < width:
            total = jnp.pad(total, ((0, 0), (0, 0), (0, 0), (0, width - C)))
        parts.append(total.reshape(Z, I * n, width))
        shapes.append((I, n, C))
    whole = jnp.concatenate(parts, axis=1)
    out = lax.psum_scatter(
        whole.reshape(-1, whole.shape[2]), "z", scatter_dimension=0, tiled=True
    )
    at = 0
    for scatter, (I, n, C) in zip(scatters, shapes):
        scatter.out = out[at : at + I * n, :C].reshape(I, n, C).astype(F32)
        at += I * n
    return out, whole


def from_behind(block, distance):
    devices = range(lax.axis_size(SEQ))
    route = [(i - distance, i) for i in devices if i - distance in devices]
    return lax.ppermute(block, SEQ, route)


def chain(mine, starts, rate, T, forward):
    S, i = lax.axis_size(SEQ), lax.axis_index(SEQ)
    all_states = lax.all_gather(mine.astype(BF16), SEQ).astype(F32)
    j = jnp.arange(S, dtype=jnp.int32)

    def document(at):
        return jnp.sum((starts[None] <= at[:, None, None]).astype(jnp.int32), axis=2)

    if forward:
        lag = i - 1 - j
        same = document((j + 1) * T - 1) == document((i * T - 1)[None])
    else:
        lag = j - 1 - i
        same = document(j * T - 1) == document(((i + 1) * T - 1)[None])
    keep = (same & (lag >= 0)[:, None]).astype(F32)
    fade = jnp.exp(-(T * jnp.maximum(lag, 0)).astype(F32)[:, None] * rate[None])
    weight = keep[:, :, None, None] * fade[:, None, None, :]
    return jnp.sum(weight * all_states, axis=0)


def layer_forward(T, place, starts, x, edge, vec, weights, hook):
    N, D = x.shape
    R = N // T
    rate = jnp.exp(vec[5])
    x = hook("start", x)
    mk, mv, mr, key, value, num, den, last = time_in(T, place, x, edge, vec, weights())
    last = hook("time in", last)
    state = chain(last, starts, rate, T, True)
    state = hook("chain", state)
    gated, middle, recept = time_out(
        T, place, x, (key, value, mr, num, den), state, vec, weights()
    )
    middle = hook("time out", middle)
    edge_two = from_behind(middle.reshape(R, T, D)[:, -1], 1)
    edge_two = hook("edge", edge_two)
    fm, gm, sp, hid, vb, gl, out = feed(T, place, middle, edge_two, vec, weights())
    out = hook("feed", out)
    saved = (x, edge, mk, mv, mr, key, value, recept, num, den, state, gated, middle, edge_two,
             fm, gm, sp, hid, vb, gl)
    return out, saved


def weight_halves(place, lefts, grads, n, kind):
    N = lefts[0].shape[0]
    D = grads[0].shape[1] if kind == "lefts" else lefts[0].shape[1]
    Z = lax.axis_size("z")
    if kind == "apart":
        count = len(lefts)
    else:
        count = (lefts[0] if kind == "lefts" else grads[0]).shape[1] // D
    if n % 8:
        if kind == "lefts":
            lefts, grads = [lefts[0][:, k * D : (k + 1) * D] for k in range(count)], grads * count
        elif kind == "grads":
            lefts, grads = lefts * count, [grads[0][:, k * D : (k + 1) * D] for k in range(count)]
        products = [
            lax.dot_general(a, b, (((0,), (0,)), ((), ())), preferred_element_type=F32).astype(BF16)
            for a, b in zip(lefts, grads)
        ]
        whole = jnp.stack([p.reshape(2, 2, Z, 2, n, D) for p in products], axis=3)
        c = lax.axis_index("c")
        return tuple(
            lax.dynamic_index_in_dim(whole, which, 4, keepdims=False) for which in (c, 1 - c)
        )
    out = pl.BlockSpec((4, Z, 1, n, D), lambda i: (0, 0, i, 0, 0))
    outs = [shape((4, Z, count, n, D), BF16)] * 2
    cost = (2 * count * N * D * D, 2 * count * (2 * N * D + D * D))
    room = [pltpu.VMEM((D, D), F32)]
    if kind == "apart":
        halves = run(
            k_halves_apart, 0, count, [smem(), smem()] + anywhere(2 * count), [out] * 2, outs,
            (*place, *lefts, *grads), *cost,
            [pltpu.VMEM((count, N, D), BF16)] * 2 + room + [pltpu.SemaphoreType.DMA((2 * count,))],
            (n, count),
        )
    else:
        fixed = pl.BlockSpec((N, D), lambda i: (0, 0))
        moving = pl.BlockSpec((N, D), lambda i: (0, i))
        specs = [moving, fixed] if kind == "lefts" else [fixed, moving]
        halves = run(
            k_halves_blocks, 0, count, [smem(), smem()] + specs, [out] * 2, outs,
            (*place, *lefts, *grads), *cost, room, (n,),
        )
    return tuple(a.reshape(2, 2, *a.shape[1:]) for a in halves)


def flat_grads(fm, gin, hid, gb):
    N, D = fm.shape
    B = gin.shape[1] // D
    fixed = pl.BlockSpec((N, D), lambda i: (0, 0))
    return run(
        k_flat, 0, 2 * B,
        [fixed, pl.BlockSpec((N, D), lambda i: (0, jnp.minimum(i, B - 1))),
         pl.BlockSpec((N, D), lambda i: (0, jnp.maximum(i - B, 0))), fixed],
        [pl.BlockSpec((D, D), lambda i: (0, i))], [shape((D, 2 * B * D), BF16)],
        (fm, gin, hid, gb), 4 * B * N * D * D, 4 * B * (2 * N * D + D * D),
    )[0]


def layer_backward(T, place, starts, grad, saved, vec, weights, hook):
    (x, edge, mk, mv, mr, key, value, recept, num, den, state, gated, middle, edge_two,
     fm, gm, sp, hid, vb, gl) = saved
    rate = jnp.exp(vec[5])
    outs = feed_back(T, place, grad, gl, vb, sp, middle, edge_two, vec, weights)
    gb, gg, gin, gn, first, sums_feed = hook("feed", outs)
    hook("feed grads", (hid, gb, fm, gin))
    behind = from_behind(first, -1)
    behind = hook("edge", behind)
    outs = mid_back(
        T, place, gn, behind, middle, grad, vec, weights, (key, value, recept, num, den), state
    )
    gmid, gblk, gr, gkp, gvp, gno, gdo, direct, sums_mid = hook("mid", outs)
    hook("mid grads", ((gated, gm, mr), (gblk, gg, gr)))
    direct = hook("before chain", direct)
    later = chain(direct, starts, rate, T, False)
    later = hook("chain", later)
    outs = time_back(
        T, place, x, edge, vec, weights, (key, value, num, den), state, (gkp, gvp, gno, gdo),
        later, gr,
    )
    gk, gv, gn_one, first_one, sums_time = hook("time", outs)
    hook("time grads", ((mk, mv), (gk, gv)))
    behind_one = from_behind(first_one.reshape(edge.shape), -1)
    behind_one = hook("edge two", behind_one)
    grad_in, sums_norm = norm_in_back(T, x, gn_one, behind_one, gmid, vec)
    grad_in = hook("norm", grad_in)
    return grad_in, jnp.concatenate([sums_norm, sums_time, sums_mid, sums_feed], axis=0)


VECTOR_ROWS = (0, 1, 8, 9, 10, 11, 18, 16, 17, 24, 25)


class Scattered:
    def __init__(self, product):
        out = lax.psum_scatter(product, AXES, scatter_dimension=0, tiled=True)
        self.out = out.astype(F32)


def vector_rates(row_total):
    slot = jnp.arange(row_total)
    return jnp.where((slot == 5) | (slot == 6), rate_time, rate_main)[:, None]


def adam_step(parameter, gradient, first_moment, second_moment, learning_rates, decay_weight):
    new_first = beta_one * first_moment + (1.0 - beta_one) * gradient
    new_second = beta_two * second_moment + (1.0 - beta_two) * gradient * gradient
    step_ratio = (
        new_first
        / (1.0 - beta_one**step_count)
        / (jnp.sqrt(new_second / (1.0 - beta_two**step_count)) + adam_epsilon)
    )
    return (learning_rates * (step_ratio + decay_weight * parameter), new_first, new_second)


XY, YX = (1, 2), (2, 1)


def body(tokens, cotangent, document_starts, *rest):
    weights, means, powers = rest[:5], rest[5:10], rest[10:15]
    vectors, matrices, time_output, feed_key, feed_value = weights
    R, T, D = tokens.shape
    layers, kinds, n = vectors.shape
    blocks = feed_key.shape[2] // D
    base = jnp.stack(
        [lax.axis_index(SEQ) * T, lax.axis_index("dp"), lax.axis_index("c")]
    ).astype(jnp.int32)
    place = (document_starts, base)

    def by_block(a):
        return a.reshape(n, D // n, blocks, n).transpose(0, 2, 1, 3).reshape(n, blocks * D)

    def by_device(a):
        return a.reshape(n, blocks, D // n, n).transpose(0, 2, 1, 3).reshape(n, blocks * D)

    keys = [(f"feed_key{b}", D) for b in range(blocks)]
    values = [(f"feed_value{b}", D) for b in range(blocks)]
    time_names = [("key", D), ("value", D)]
    out_names = [("recept", D), ("output", D)]
    key_names = [("gate", D)] + keys
    layout = [[time_names + [("vectors", 128)], out_names + key_names, values]]
    layout += [[time_names + out_names, key_names + values]] * (layers - 1)

    vector_columns = jnp.pad(
        vectors.reshape(layers * kinds, n).T, ((0, 0), (0, 128 - layers * kinds))
    )

    arguments = {0: (matrices, time_output, feed_key, feed_value)}

    def shard(l, names):
        matrices, time_output, feed_key, feed_value = arguments[l]
        found = {
            "key": matrices[l, 0], "value": matrices[l, 1], "recept": matrices[l, 2],
            "gate": matrices[l, 3], "output": time_output[l], "vectors": vector_columns,
        }
        for b in range(blocks):
            found[f"feed_value{b}"] = feed_value[l, b * n : (b + 1) * n]
        if ("feed_key0", D) in names:
            key_blocks = by_block(feed_key[l].astype(BF16))
            for b in range(blocks):
                found[f"feed_key{b}"] = key_blocks[:, b * D : (b + 1) * D]
        return jnp.concatenate([found[name].astype(BF16) for name, _ in names], axis=1)

    def sets_of(l, k, gate, *split):
        part = shard(l, layout[l][k])
        block = gather_seq(part, *gate)
        shards.setdefault(l, []).append(part)
        sets, at = [], 0
        for count, bits in split:
            names = layout[l][k][at : at + count]
            sets.append(Exchange(block, names, sum(w for _, w in layout[l][k][:at]), bits))
            at += count
        return sets

    def weights_of(l):
        def found():
            have = {}
            for exchange in here[l]:
                if hasattr(exchange, "other_two") or isinstance(exchange, Gathered):
                    have.update(exchange.weights())
            return have

        return found

    shards = {}
    here = [[] for _ in range(layers)]
    A = sets_of(0, 0, (), (3, XY))[0]
    O, B = sets_of(0, 1, (), (2, YX), (1 + blocks, XY))
    V = sets_of(0, 2, (A.block,), (blocks, YX))[0]
    here[0] = [A, O, B, V]
    A.prepare()
    A.first()
    for l in range(1, layers):
        arguments[l] = after(arguments[0], A.block)
        here[l] = sets_of(l, 0, (A.one,), (4, XY))
    for l in range(1, layers):
        here[l] += sets_of(l, 1, (B.block,), (1 + blocks, XY), (blocks, YX))
    A.second(O.prepare(A.block), B.prepare(A.block), *[p for l in range(1, layers) for p in shards[l]])
    O.first()
    B.first()
    A.cores(O.one, B.one)
    O.second(A.two)
    V.first(A.two)
    B.second(A.two)
    pieces, item = A.weights()["vectors"]
    d, c = lax.axis_index("dp"), lax.axis_index("c")
    block, one, two, other_one, other_two = (a[..., item[2] : item[2] + 128] for a in pieces)
    bits, half = item[5], item[4]
    mine = lax.dynamic_slice_in_dim(block, c * half, half, axis=0)
    other = lax.dynamic_slice_in_dim(block, (1 - c) * half, half, axis=0)
    by_m = {
        0: (mine, other), bits[0]: (one, other_one), bits[1]: (two[0], other_two[0]),
        bits[0] | bits[1]: (two[1], other_two[1]),
    }
    rel = jnp.stack([jnp.stack(by_m[m]) for m in range(4)])
    rel = jnp.where(c == 0, rel, rel[:, ::-1])
    columns = jnp.stack([lax.dynamic_index_in_dim(rel, d ^ j, 0, keepdims=False) for j in range(4)])
    spread = columns.reshape(D, 128)[:, : layers * kinds].astype(F32).T.reshape(layers, kinds, D)
    vecs = [jnp.pad(spread[l], ((0, 16 - kinds), (0, 0))) for l in range(layers)]

    def hook_of(l):
        more = l + 1 < layers

        def hook(name, value):
            if name == "start" and l > 0:
                M, U, S = here[l]
                value = after(value, M.two)
                M.cores(value)
                U.second(value)
            elif name == "time in" and l == 0:
                value = after(value, O.two, V.one)
                O.cores(value)
                V.second(value)
            elif name == "time in":
                M, U, S = here[l]
                value = after(value, S.one)
                S.second(value)
            elif name == "time out" and l == 0:
                value = after(value, V.two)
                V.cores(value)
                if more:
                    here[l + 1][0].first(value)
            elif name == "time out":
                M, U, S = here[l]
                value = after(value, S.two, U.two)
                S.cores(value)
                U.cores(value)
            elif name == "edge" and l == 0:
                value = after(value, B.two)
                B.cores(value)
                if more:
                    value = after(value, here[l + 1][0].one)
                    here[l + 1][0].second(value)
                    here[l + 1][1].first(value)
            elif name == "feed" and more:
                M, U, S = here[l + 1]
                value = after(value, U.one)
                S.first(value)
            return value

        return hook

    x = tokens.reshape(R * T, D)
    saved = []
    for l in range(layers):
        edge = from_behind(x.reshape(R, T, D)[:, -1], 1).astype(F32)
        x, kept = layer_forward(
            T, place, document_starts, x, edge, vecs[l], weights_of(l), hook_of(l)
        )
        saved.append(kept)
    block_out = x.astype(BF16).reshape(R, T, D)

    grad = cotangent.reshape(R * T, D)
    vec_grads = [None] * layers
    sums = [dict() for _ in range(layers)]

    def back_hook_of(l):
        own, last = sums[l], sums[l + 1] if l + 1 < layers else None

        def hook(name, value):
            feed = own.get("feed") if l == 0 else None
            if name == "feed" and last:
                value = after(value, last["mid"].got, last["time"].got)
                last["mid"].second(value[3])
                last["time"].second(value[3])
            elif name == "feed grads":
                hid, gb, fm, gin = value
                if l > 0:
                    own["ready"] = flat_grads(fm, gin, hid, gb)
                    own["feed"] = Scattered(own["ready"])
                else:
                    one = Scatter(*weight_halves(place, [hid], [gb], n, "lefts"), YX)
                    one.cores()
                    halves = weight_halves(place, [fm], [after(gin, one.mine)], n, "grads")
                    if last:
                        halves = after(halves, last["mid"].two, last["time"].two)
                    two = Scatter(*halves, XY)
                    two.cores()
                    own["feed"] = [one, two]
            elif name == "edge" and l > 0:
                value = after(value, own["ready"])
            elif name == "edge":
                value = after(value, *[s.received for s in feed])
                for s in feed:
                    s.first()
            elif name == "mid grads":
                halves = weight_halves(place, *value, n, "apart")
                if l == 0:
                    halves = after(halves, *[s.got for s in feed])
                own["mid"] = Scatter(*halves, YX)
                own["mid"].cores()
                if last:
                    own["gate"] = finish(
                        [last["mid"], last["time"]], last["feed"].out, own["mid"].mine
                    )[0]
                if l == 0:
                    for s in feed:
                        s.second()
            elif name == "before chain" and l == 0:
                value = after(value, own["mid"].received)
                own["mid"].first()
            elif name == "chain" and l > 0:
                value = after(value, own["mid"].received)
                own["mid"].first(value)
            elif name == "time":
                if l == 0:
                    value = after(value, own["mid"].got, *[s.two for s in feed])
                    own["gate"], whole = finish(feed, *[own["gate"]] * (layers > 1))
                    value = after(value, whole)
            elif name == "time grads":
                own["time"] = Scatter(*weight_halves(place, *value, n, "apart"), XY if l else YX)
                own["time"].cores()
            elif name == "edge two" and l == 0:
                own["time"].first()
                own["mid"].second(own["time"].sent)
                value = after(value, own["time"].sent)
            elif name == "norm" and l > 0:
                value = after(value, own["time"].received)
                own["time"].first()
            return value

        return hook

    for l in reversed(range(layers)):
        grad, vec_grads[l] = layer_backward(
            T, place, document_starts, grad, saved[l], vecs[l], weights_of(l)(), back_hook_of(l)
        )
    vec_columns = jnp.concatenate(vec_grads, axis=0).astype(BF16).T
    vec_columns = jnp.pad(vec_columns, ((0, 0), (0, 128 - vec_columns.shape[1])))
    vec_view = vec_columns.reshape(2, 2, lax.axis_size("z"), 1, 2, n, 128)
    vec_sum = Scatter(
        *[lax.dynamic_index_in_dim(vec_view, w, 4, keepdims=False) for w in (c, 1 - c)], XY
    )
    tail = sums[0]
    vec_sum.cores()
    vec_sum.first(tail["time"].got)
    tail["time"].second()
    vec_sum.second(tail["gate"])
    _, whole = finish([tail["mid"], tail["time"], vec_sum])
    for l in range(1, layers):
        for e in (sums[l]["feed"], sums[l]["mid"], sums[l]["time"]):
            e.out = after(e.out, whole)
    for e in tail["feed"]:
        e.out = after(e.out, whole)
    g_vec = vec_sum.out[0]
    grads = []
    for l in range(layers):
        if l > 0:
            feed = sums[l]["feed"].out
            g_fk, g_fv = feed[:, : blocks * D], feed[:, blocks * D :]
            g_fv = jnp.concatenate([g_fv[:, b * D : (b + 1) * D] for b in range(blocks)], axis=0)
        else:
            g_fv, g_fk = (s.out for s in sums[l]["feed"])
            g_fv, g_fk = g_fv.reshape(-1, D), jnp.concatenate(list(g_fk), axis=1)
        g_out, g_gate, g_recept = sums[l]["mid"].out
        g_key, g_value = sums[l]["time"].out
        grads.append(
            (
                g_vec[:, [32 * l + k for k in VECTOR_ROWS]].T,
                jnp.stack([g_key, g_value, g_recept, g_gate]),
                g_out,
                by_device(g_fk),
                g_fv,
            )
        )
    totals = tuple(jnp.stack([g[m] for g in grads]) for m in range(5))
    rates = (vector_rates(kinds),) + (rate_main,) * 4
    decays = (0.0,) + (weight_decay,) * 4
    new = [adam_step(*z) for z in zip(weights, totals, means, powers, rates, decays)]
    return (
        block_out,
        grad.reshape(R, T, D),
        *totals,
        *[z[0] for z in new],
        *[z[1] for z in new],
        *[z[2] for z in new],
    )


def solution(mesh):
    dp, seq = mesh.shape["dp"], mesh.shape["seq"]
    mesh = Mesh(mesh.devices.reshape(dp, seq // 2, 2), AXES)
    tokens = P("dp", SEQ, None)
    group = (
        P(None, None, AXES),
        P(None, None, AXES, None),
        P(None, AXES, None),
        P(None, AXES, None),
        P(None, AXES, None),
    )
    in_specs = (tokens, tokens, P("dp", None)) + group * 3
    out_specs = (tokens, tokens) + group * 4
    return jax.shard_map(body, mesh=mesh, in_specs=in_specs, out_specs=out_specs, check_vma=False)
```
